32 devices in a mesh: dp: 8 (over z, y), tensor: 4 (over x, core).
Axes of the slice: x: 2, y: 2, z: 4, core: 2. Of those that a mesh axis runs over, the one named last changes fastest.
Arguments:
- inputs: bfloat16 [16384, 768], P(('dp', 'tensor')), may hold values from -6 to 6
- segments: int32 [16384], P('dp'), may hold values from 0 to 39, as said below
- w_query: bfloat16 [768, 768], P('dp', 'tensor'), may hold values from -0.21875 to 0.21875
- w_key: bfloat16 [768, 768], P('dp', 'tensor'), may hold values from -0.21875 to 0.21875
- w_value: bfloat16 [768, 768], P('dp', 'tensor'), may hold values from -0.21875 to 0.21875
- w_output: bfloat16 [768, 768], P('tensor', 'dp'), may hold values from -3.5 to 3.5
- w_hidden: bfloat16 [768, 3072], P('dp', 'tensor'), may hold values from -0.21875 to 0.21875
- w_back: bfloat16 [3072, 768], P('tensor', 'dp'), may hold values from -0.15625 to 0.15625
- gain_one: bfloat16 [768], P('dp'), may hold values from 0.5 to 1.5
- gain_two: bfloat16 [768], P('dp'), may hold values from 0.5 to 1.5
- cotangent: bfloat16 [16384, 768], P(('dp', 'tensor')), may hold values from -6 to 6
Outputs:
- result: bfloat16 [16384, 768], P(('dp', 'tensor'))
- grad_inputs: bfloat16 [16384, 768], P(('dp', 'tensor'))
- grad_query: float32 [768, 768], P('dp', 'tensor')
- grad_key: float32 [768, 768], P('dp', 'tensor')
- grad_value: float32 [768, 768], P('dp', 'tensor')
- grad_output: float32 [768, 768], P('tensor', 'dp')
- grad_hidden: float32 [768, 3072], P('dp', 'tensor')
- grad_back: float32 [3072, 768], P('tensor', 'dp')
- grad_gain_one: float32 [768], P(('dp', 'tensor'))
- grad_gain_two: float32 [768], P(('dp', 'tensor'))
The draws below stay inside these ranges and needn't reach their ends.
Inputs may be any that keep to these rules, and one draw needn't show every extreme that they name: `segments`: segment numbers start at 0, never fall, and rise by one at each document start; every sequence of 2048 positions holds exactly five documents, the first beginning at its first position, and one of them, longer than 1536 positions, runs from before position 256 to position 1536 or past it.
All inputs are finite; a program needn't handle non-finite values.
Results may differ from the reference program's by a relative error of at most 0.018.
Values may be sent and summed in bfloat16 or wider, within the bound.
A program may use at most 128 MiB of HBM per device.

```python
import jax
import jax.numpy as jnp
from jax import lax

D = 768
H = 12
E = 64
FF = 3072
SEQ_LEN = 2048
WINDOW = 1536
TOKENS = 16384


def draw_segments(key, part):
    count = TOKENS // SEQ_LEN
    unit = min(SEQ_LEN - WINDOW, SEQ_LEN // 2) // 8
    keys = jax.random.split(jax.random.fold_in(key, 17), 4)
    first_cut = jax.random.randint(keys[0], (count, 1), 1, unit)
    long_start = jax.random.randint(keys[1], (count, 1), unit, 2 * unit)
    long_end = SEQ_LEN - 4 * unit + jax.random.randint(keys[2], (count, 1), 1, unit + 1)
    last_cut = long_end + jax.random.randint(keys[3], (count, 1), 1, unit)
    positions = jnp.arange(SEQ_LEN, dtype=jnp.int32)[None, :]
    flags = (positions == 0) | (positions == first_cut) | (positions == long_start) | (positions == long_end) | (positions == last_cut)
    numbers = jnp.cumsum(flags.reshape(-1).astype(jnp.int32)) - 1
    return numbers.astype(jnp.int32)


def spiked(entries, stream_key, source, target, blocks, factor):
    owner, partner = [(jnp.arange(entries.shape[axis_at]) // (entries.shape[axis_at] // blocks)).reshape([-1 if axis == axis_at else 1 for axis in range(entries.ndim)]) for axis_at in (source, target)]
    chosen = jax.random.permutation(stream_key, blocks)[partner]
    strong = (owner == chosen) | (owner == (partner + blocks // 2) % blocks)
    return jnp.where(strong, factor * entries, entries)


def level_of(own_key, shape, shards, least, largest):
    loudness = 1.0
    for position, parts in shards:
        heights = jax.random.uniform(jax.random.fold_in(jax.random.fold_in(own_key, 6), position), (parts,), jnp.float32, least / len(shards), largest / len(shards))
        loudness = loudness * jnp.repeat(jnp.exp(heights), shape[position] // parts).reshape((-1,) + (1,) * (len(shape) - 1 - position))
    return loudness


def bell_draw(key, shape, scale, limit, cuts=(), kind=jnp.bfloat16):
    result = jax.random.normal(key, shape, jnp.float32) * scale
    if len(cuts) > 0:
        result = level_of(key, shape, cuts, -0.22, 0.18) * result
    return jnp.clip(result, min=-limit, max=limit).astype(kind)


def bell_draw_with(key, extent, scale, limit, cuts, heavy, kind=jnp.bfloat16):
    drawn = scale * jax.random.normal(key, extent, jnp.float32)
    if cuts:
        drawn = drawn * level_of(key, extent, cuts, -0.22, 0.18)
    return jnp.clip(spiked(drawn, jax.random.fold_in(key, 3), *heavy), -limit, limit).astype(kind)


def setup_inputs(seed: int = 0) -> dict:
    seeds = jax.random.split(jax.random.key(seed), 12)
    inputs = bell_draw(seeds[0], (TOKENS, D), 1.0, 6.0, ((0, 32),))
    segments = draw_segments(jax.random.fold_in(seeds[11], 71), 0)
    w_query = bell_draw(seeds[2], (D, D), D ** -0.5, 0.21875, ((0, 8), (1, 4)))
    w_key = bell_draw(seeds[3], (D, D), D ** -0.5, 0.21875, ((0, 8), (1, 4)))
    w_value = bell_draw(seeds[4], (D, D), D ** -0.5, 0.21875, ((0, 8), (1, 4)))
    w_output = bell_draw(seeds[5], (D, D), (D // 256) ** -0.5, 3.5, ((0, 4), (1, 8)))
    w_hidden = bell_draw(seeds[6], (D, FF), D ** -0.5, 0.21875, ((0, 8), (1, 4)))
    w_back = bell_draw(seeds[7], (FF, D), (FF // 2) ** -0.5, 0.15625, ((0, 4), (1, 8)))
    gain_one = jnp.clip(1.0 + 0.1 * jax.random.normal(seeds[8], (D,), jnp.float32), 0.5, 1.5).astype(jnp.bfloat16)
    gain_two = jnp.clip(1.0 + 0.1 * jax.random.normal(seeds[9], (D,), jnp.float32), 0.5, 1.5).astype(jnp.bfloat16)
    cotangent = bell_draw_with(seeds[10], (TOKENS, D), 1.0, 6.0, ((0, 32),), (0, 1, 32, 2.75))
    return {"inputs": inputs, "segments": segments, "w_query": w_query, "w_key": w_key, "w_value": w_value, "w_output": w_output, "w_hidden": w_hidden, "w_back": w_back, "gain_one": gain_one, "gain_two": gain_two, "cotangent": cotangent}


@jax.custom_vjp
def low(v):
    return lax.optimization_barrier(v.astype(jnp.bfloat16)).astype(jnp.float32)

@jax.custom_vjp
def low_back(v):
    return v

def low_keep(v):
    return (low(v), None)

def low_pass(kept, grad):
    return (grad,)

def back_keep(v):
    return (v, None)

def back_low(kept, grad):
    return (low(grad),)
low.defvjp(low_keep, low_pass)
low_back.defvjp(back_keep, back_low)

def matmul(left, right):
    return jnp.dot(left, right, precision=lax.Precision.HIGHEST, preferred_element_type=jnp.float32)

def rounded(value):
    return low(low_back(value))

def normed(value, gain):
    return value * lax.rsqrt(lax.optimization_barrier(jnp.mean(value * value, axis=-1, keepdims=True)) + 1e-05) * gain

def attend(query_rows, key_rows, value_rows, segment_ids):
    block_rows = min(512, SEQ_LEN)
    blocks = SEQ_LEN // block_rows
    positions = jnp.arange(SEQ_LEN, dtype=jnp.int32)

    def block_out(packed):
        query_block, block_start = packed
        query_pos = block_start + jnp.arange(block_rows, dtype=jnp.int32)
        query_seg = lax.dynamic_slice_in_dim(segment_ids, block_start, block_rows)
        scores = jnp.einsum('qhe,khe->hqk', query_block, key_rows, precision=lax.Precision.HIGHEST) * E ** (-0.5)
        scores = low_back(scores)
        distance = query_pos[:, None] - positions[None, :]
        allowed = (query_seg[:, None] == segment_ids[None, :]) & (distance >= 0) & (distance < WINDOW)
        scores = jnp.where(allowed[None], scores, -1e+30)
        row_top = lax.optimization_barrier(jnp.max(scores, axis=-1, keepdims=True))
        weights_exp = jnp.exp(scores - row_top)
        probability = weights_exp / lax.optimization_barrier(jnp.sum(weights_exp, axis=-1, keepdims=True))
        return jnp.einsum('hqk,khe->qhe', low(probability), value_rows, precision=lax.Precision.HIGHEST)
    starts = jnp.arange(blocks, dtype=jnp.int32) * block_rows
    attended = lax.map(jax.checkpoint(block_out), (query_rows.reshape(blocks, block_rows, H, E), starts))
    return attended.reshape(SEQ_LEN, H * E)

def layer(sequence, segment_ids, weights):
    w_query, w_key, w_value, w_output, w_hidden, w_back, gain_one, gain_two = weights
    normed_one = low(normed(sequence, gain_one))
    query_rows = rounded(matmul(normed_one, w_query)).reshape(SEQ_LEN, H, E)
    key_rows = rounded(matmul(normed_one, w_key)).reshape(SEQ_LEN, H, E)
    value_rows = rounded(matmul(normed_one, w_value)).reshape(SEQ_LEN, H, E)
    attended = rounded(attend(query_rows, key_rows, value_rows, segment_ids))
    middle = sequence + low_back(matmul(attended, w_output))
    normed_two = low(normed(middle, gain_two))
    hidden = low_back(matmul(normed_two, w_hidden))
    active = low(jax.nn.gelu(hidden, approximate=True))
    return middle + low_back(matmul(active, w_back))

def forward(inputs_f, segments, weights):
    count = TOKENS // SEQ_LEN
    stacked = inputs_f.reshape(count, SEQ_LEN, D)
    seg_stack = segments.reshape(count, SEQ_LEN)

    def one_sequence(packed):
        return layer(packed[0], packed[1], weights)
    outcome = lax.map(jax.checkpoint(one_sequence), (stacked, seg_stack))
    return outcome.reshape(TOKENS, D)

def reference(inputs, segments, w_query, w_key, w_value, w_output, w_hidden, w_back, gain_one, gain_two, cotangent):
    floats = tuple((item.astype(jnp.float32) for item in (inputs, w_query, w_key, w_value, w_output, w_hidden, w_back, gain_one, gain_two)))

    def wrapped(inputs_f, *weights):
        return forward(inputs_f, segments, weights)
    output, pull = jax.vjp(wrapped, *floats)
    grads = pull(cotangent.astype(jnp.float32))
    return (output.astype(jnp.bfloat16), grads[0].astype(jnp.bfloat16), grads[1], grads[2], grads[3], grads[4], grads[5], grads[6], grads[7], grads[8])
```

```python
import functools

import jax
import jax.numpy as jnp
from jax import lax
from jax.experimental import pallas as pl
from jax.experimental.pallas import tpu as pltpu
from jax.sharding import PartitionSpec as P

MESH = pl.DeviceIdType.MESH
f32, bf = jnp.float32, jnp.bfloat16
E = 64
WINDOW = 1536
B = 256
LOG2E = 1.4426950408889634
SCALE = E**-0.5
FILL = -1e30
CUT = 1280
NZ = 4


def nn(a, b):
    return lax.dot_general(a, b, (((1,), (0,)), ((), ())), preferred_element_type=f32)


def nt(a, b):
    return lax.dot_general(a, b, (((1,), (1,)), ((), ())), preferred_element_type=f32)


def tn(a, b):
    return lax.dot_general(a, b, (((0,), (0,)), ((), ())), preferred_element_type=f32)


class Place:
    def __init__(self):
        self.dp = lax.axis_index("dp")
        self.t = lax.axis_index("tensor")
        self.z, self.y = lax.div(self.dp, 2), lax.rem(self.dp, 2)
        self.x, self.c = lax.div(self.t, 2), lax.rem(self.t, 2)

    def at(self, z=None, y=None, x=None, c=None):
        z = self.z if z is None else z
        y = self.y if y is None else y
        x = self.x if x is None else x
        c = self.c if c is None else c
        return (z * 2 + y, x * 2 + c)

    def greet(self, far_z):
        barrier = pltpu.get_barrier_semaphore()
        x, y, z, c = self.x, self.y, self.z, self.c
        near = [self.at(y=1 - y), self.at(x=1 - x), self.at(c=1 - c), self.at(x=1 - x, c=1 - c)]
        for there in near:
            pl.semaphore_signal(barrier, inc=1, device_id=there, device_id_type=MESH)
        for step in range(1, NZ):
            pl.semaphore_signal(
                barrier, inc=1, device_id=self.at(z=lax.rem(z + step, NZ)), device_id_type=MESH
            )
        pl.semaphore_wait(barrier, len(near) + NZ - 1)


class Lanes:
    def __init__(self, send, recv):
        self.send, self.recv, self.n, self.base, self.late = send, recv, 0, {}, []

    def block(self, name, count):
        self.base[name] = self.n
        self.n += count

    def copy(self, name, k, src, dst, there):
        i = self.base[name] + k
        return pltpu.make_async_remote_copy(
            src_ref=src,
            dst_ref=dst,
            send_sem=self.send.at[i],
            recv_sem=self.recv.at[i],
            device_id=there,
            device_id_type=MESH,
        )

    def start(self, name, k, ends, there, when=None):
        at = k if callable(k) else lambda: k
        self.copy(name, at(), *ends(), there).start()

        def finish():
            self.copy(name, at(), *ends(), there).wait_send()

        self.late.append((finish, when))

    def arrived(self, name, k, dst, there):
        self.copy(name, k, dst, dst, there).wait_recv()

    def finish(self):
        for act, when in self.late:
            if when is None:
                act()
            else:
                pl.when(when())(act)


def sides(me, rnd):
    z = me.z
    if rnd == 0:
        return [(z, None, None)]
    return [(z - rnd, True, lambda: z >= rnd), (z + rnd, False, lambda: z + rnd < NZ)]


def line_round(me, lanes, name, rnd, ref_of, arrive):
    z = me.z
    left, right = me.at(z=z - 1), me.at(z=z + 1)

    def go(zi, to_right, when):
        def side():
            return z < NZ - 1 if to_right else z > 0

        def whole():
            return side() if when is None else jnp.logical_and(when(), side())

        lane, there = name + ("R" if to_right else "L"), right if to_right else left

        def copy():
            return lanes.copy(lane, zi, ref_of(zi), ref_of(zi), there)

        pl.when(side())(lambda: copy().start())
        lanes.late.append((lambda: copy().wait_send(), whole))

    for zi, from_left, ok in sides(me, rnd):
        if rnd == 0:
            go(zi, True, None)
            go(zi, False, None)
            arrive(zi, None)
            continue

        @pl.when(ok())
        def _(zi=zi, from_left=from_left, ok=ok):
            lanes.arrived(name + ("R" if from_left else "L"), zi, ref_of(zi), left if from_left else right)
            go(zi, from_left, ok)
            arrive(zi, ok)


def masked(i, j, blocks):
    return j == i or j == 0 or i >= blocks - 2 or i - j >= WINDOW // B


def keep(i, j, low, value, fill):
    key_pos = lax.broadcasted_iota(jnp.int32, value.shape, 0) + j * B
    ok = key_pos >= low
    if i == j:
        ok = ok & (key_pos <= lax.broadcasted_iota(jnp.int32, value.shape, 1) + i * B)
    return jnp.where(ok, value, fill)


def spans(i):
    first = max(0, i - WINDOW // B)
    return first, list(range(first, i + 1))


def score_pass(i, h, slot, blocks, kn, qh, low_ref, S):
    j0, js = spans(i)
    cols = slice(i * B, (i + 1) * B)
    qT = qh[h, 0:E, cols]
    low = low_ref[0:1, cols]
    top = jnp.full((1, B), FILL, f32)
    for j in js:
        s = nn(kn[h, j * B : (j + 1) * B, :], qT)
        if masked(i, j, blocks):
            s = keep(i, j, low, s, FILL)
        S[slot, (j - j0) * B : (j - j0 + 1) * B, :] = s
        top = jnp.maximum(top, jnp.max(s, axis=0, keepdims=True))
    return top * (SCALE * LOG2E)


def value_pass(i, h, slot, top, qh, S, o_ref, L_ref):
    j0, js = spans(i)
    total = jnp.zeros((1, B), f32)
    out = jnp.zeros((E, B), f32)
    for j in js:
        p = jnp.exp2(S[slot, (j - j0) * B : (j - j0 + 1) * B, :] * (SCALE * LOG2E) - top)
        total = total + jnp.sum(p, axis=0, keepdims=True)
        out = out + nn(qh[h, 2 * E : 3 * E, j * B : (j + 1) * B], p.astype(bf))
    half = i % 2
    o_ref[i // 2, pl.ds(pl.multiple_of(h * E, E), E), half * B : (half + 1) * B] = (out / total).astype(bf)
    L_ref[h, :, i * B : (i + 1) * B] = jnp.broadcast_to(top + jnp.log2(total), (8, B))


def lows(seg, total):
    pos = lax.broadcasted_iota(jnp.int32, (1, total), 1)
    low = jnp.maximum(pos - (WINDOW - 1), 0)
    first = seg[0:1, 0:1]
    for d in range(1, 5):
        begin = jnp.sum((seg < first + d).astype(f32), axis=1, keepdims=True).astype(jnp.int32)
        low = jnp.where(seg >= first + d, jnp.maximum(low, begin), low)
    return low


def fwd_kernel(xo, w1, w2, cot, seg, n1, qh, o_ref, oin, L_ref, low_ref, W1T, W2g, cot2, wox, X4, W1, kn, S, send, recv):
    me = Place()
    dp, t, x, y, z, c = me.dp, me.t, me.x, me.y, me.z, me.c
    total = n1.shape[0]
    rows = xo.shape[0]
    blocks = total // B
    heads = kn.shape[0]
    X_, Y_, C_, XC_ = me.at(x=1 - x), me.at(y=1 - y), me.at(c=1 - c), me.at(x=1 - x, c=1 - c)
    lanes = Lanes(send, recv)
    for name, count in (
        ("aR", 4), ("aL", 4), ("ay", 4), ("x", 2), ("cx", 2), ("co", 1), ("cc", 1),
        ("bR", 4), ("bL", 4), ("bx", 4), ("by", 4), ("bxy", 4), ("byx", 4), ("o", 4), ("w", 1),
    ):
        lanes.block(name, count)

    me.greet(True)
    W1[dp] = w1[...]
    half = rows // 2

    def a_ref(zi):
        return W1.at[zi * 2 + y]

    def a_arrive(zi, when):
        lanes.start("ay", zi, lambda: (a_ref(zi), a_ref(zi)), Y_, when)

    line_round(me, lanes, "a", 0, a_ref, a_arrive)
    for k in range(2):
        lanes.start("x", k, lambda k=k: (xo.at[pl.ds(k * half, half)], X4.at[t, pl.ds(k * half, half)]), X_)
    lanes.start("co", 0, lambda: (xo, X4.at[t]), C_)
    W2g[x, dp] = w2[...]
    low_ref[...] = jnp.broadcast_to(lows(seg[...], total), low_ref.shape)
    X4[t] = xo[...]
    line_round(me, lanes, "a", 1, a_ref, a_arrive)
    line_round(me, lanes, "a", 2, a_ref, a_arrive)
    line_round(me, lanes, "a", 3, a_ref, a_arrive)

    def b_ref(zi):
        return W2g.at[x, zi * 2 + y]

    def b_arrive(zi, when):
        lanes.start("bx", zi, lambda: (b_ref(zi), b_ref(zi)), X_, when)
        lanes.start("by", zi, lambda: (b_ref(zi), b_ref(zi)), Y_, when)

    def b_corner(rnd):
        def one(zi, ok):
            def from_x():
                return W2g.at[1 - x, zi * 2 + y]

            def from_y():
                return W2g.at[x, zi * 2 + 1 - y]

            lanes.arrived("bx", zi, from_x(), X_)
            lanes.start("bxy", zi, lambda: (from_x().at[:, 0:CUT],) * 2, Y_, ok)
            lanes.arrived("by", zi, from_y(), Y_)
            lanes.start("byx", zi, lambda: (from_y().at[:, CUT:],) * 2, X_, ok)

        for zi, _, ok in sides(me, rnd):
            if ok is None:
                one(zi, None)
            else:
                pl.when(ok())(functools.partial(one, zi, ok))

    def b_round(rnd):
        line_round(me, lanes, "b", rnd, b_ref, b_arrive)

    b_round(0)
    for zi in range(NZ):
        lanes.arrived("ay", zi, W1.at[zi * 2 + 1 - y], Y_)
    W1T[...] = W1[...].reshape(W1.shape[0] * W1.shape[1], W1.shape[2]).T
    lanes.start("cc", 0, lambda: (cot, cot2), C_)

    def project(blk):
        base = pl.multiple_of(blk * rows, rows)
        gain = W1T[heads * 3 * E : heads * 3 * E + 16, :].astype(f32)[0:1]
        value = X4[blk].astype(f32)
        inv = lax.rsqrt(jnp.mean(value * value, axis=-1, keepdims=True) + 1e-05)
        normed = (value * inv * gain).astype(bf)
        n1[pl.ds(base, rows), :] = normed
        out = nt(W1T[0 : heads * 3 * E, :], normed).astype(bf)
        for h in range(heads):
            qh[h, :, pl.ds(base, rows)] = out[h * 3 * E : (h + 1) * 3 * E]
            kn[h, pl.ds(base, rows), :] = out[h * 3 * E + E : h * 3 * E + 2 * E].T

    project(t)
    lanes.arrived("co", 0, X4.at[x * 2 + 1 - c], C_)
    project(x * 2 + 1 - c)
    for k in range(2):
        got = X4.at[(1 - x) * 2 + c, pl.ds(k * half, half)]
        lanes.arrived("x", k, got, X_)
        lanes.start("cx", k, lambda got=got: (got, got), C_)
    project((1 - x) * 2 + c)
    for k in range(2):
        lanes.arrived("cx", k, X4.at[(1 - x) * 2 + 1 - c, pl.ds(k * half, half)], C_)
    project((1 - x) * 2 + 1 - c)

    b_round(1)

    quarter_send = lanes.base["o"]

    def quarter2(r):
        def body(h, carry):
            tops = []
            for i in (2 * r, 2 * r + 1):
                tops.append(score_pass(i, h, i % 2, blocks, kn, qh, low_ref, S))
            for i in (2 * r, 2 * r + 1):
                value_pass(i, h, i % 2, tops[i % 2], qh, S, o_ref, L_ref)
            return carry

        lax.fori_loop(0, heads, body, 0)

        def out_copy():
            return pltpu.make_async_remote_copy(
                src_ref=o_ref.at[r],
                dst_ref=oin.at[t],
                send_sem=send.at[quarter_send + r],
                recv_sem=recv.at[quarter_send + t],
                device_id=(dp, r),
                device_id_type=MESH,
            )

        @pl.when(t == r)
        def _():
            oin[t] = o_ref[r]

        @pl.when(t != r)
        def _():
            out_copy().start()

        lanes.late.append((lambda: out_copy().wait_send(), lambda: t != r))

    quarter2(0)
    b_corner(0)
    b_round(2)
    b_corner(1)
    quarter2(1)
    b_round(3)
    quarter2(2)
    b_corner(2)
    quarter2(3)
    b_corner(3)
    for zi in range(NZ):
        got = W2g.at[1 - x, zi * 2 + 1 - y]
        lanes.arrived("bxy", zi, got.at[:, 0:CUT], Y_)
        lanes.arrived("byx", zi, got.at[:, CUT:], X_)
    wide = W2g.shape[3]
    lanes.start("w", 0, lambda: (W2g.at[:, :, :, wide - 256 :], wox), C_)
    lanes.arrived("cc", 0, cot2, C_)
    for there in ((1 - x) * 2 + c, x * 2 + 1 - c, (1 - x) * 2 + 1 - c):
        lanes.arrived("o", there, oin.at[there], (dp, there))
    lanes.arrived("w", 0, wox, C_)
    lanes.finish()


N_SEM1 = 48
VM = pl.BlockSpec(memory_space=pltpu.VMEM)


def params(cid):
    return pltpu.CompilerParams(collective_id=cid, has_side_effects=True, vmem_limit_bytes=60 * 2**20)


def pack_weights(w_query, w_key, w_value, w_output, w_hidden, w_back, gain_one, gain_two):
    part, width = w_query.shape
    heads = width // E
    joined = jnp.stack([w.reshape(part, heads, E) for w in (w_query, w_key, w_value)], axis=2).reshape(part, 3 * width)
    gains = jnp.pad(jnp.stack([gain_one, gain_two], axis=1), ((0, 0), (0, 62)))
    w1 = jnp.concatenate([joined, gains], axis=1)
    w2 = jnp.concatenate([w_hidden, w_back.T, jnp.pad(w_output.T, ((0, 0), (0, 64)))], axis=1)
    return w1, w2


def run_fwd(xo, w1, w2, cot, seg):
    rows, dm = xo.shape
    total = seg.shape[1]
    heads = 3
    part = w1.shape[0]
    s = jax.ShapeDtypeStruct
    return pl.pallas_call(
        fwd_kernel,
        out_shape=(
            s((total, dm), bf), s((heads, 3 * E, total), bf), s((4, heads * E, rows), bf), s((4, heads * E, rows), bf),
            s((heads, 8, total), f32), s((8, total), jnp.int32), s((w1.shape[1], dm), bf),
            s((2, 8, part, w2.shape[1]), bf), s((rows, dm), bf), s((2, 8, part, 256), bf),
        ),
        in_specs=[VM] * 5,
        out_specs=(VM,) * 10,
        scratch_shapes=[
            pltpu.VMEM((4, rows, dm), bf),
            pltpu.VMEM((8, part, w1.shape[1]), bf),
            pltpu.VMEM((heads, total, E), bf),
            pltpu.VMEM((2, WINDOW + B, B), f32),
            pltpu.SemaphoreType.DMA((N_SEM1,)),
            pltpu.SemaphoreType.DMA((N_SEM1,)),
        ],
        compiler_params=params(1),
    )(xo, w1, w2, cot, seg)


def gelu_and_slope(u):
    root = 0.7978845608028654
    square = u * u
    th = jnp.tanh(u * (root + (root * 0.044715) * square))
    half = 0.5 + 0.5 * th
    slope = half + (0.5 * u) * (1.0 - th * th) * (root + (3.0 * root * 0.044715) * square)
    return u * half, slope


def norm_pull(value, gain, grad):
    inv = lax.rsqrt(jnp.mean(value * value, axis=-1, keepdims=True) + 1e-05)
    scaled = grad * gain
    return inv * scaled - value * (inv * inv * inv * jnp.mean(value * scaled, axis=-1, keepdims=True))


HB = 256


def mid_kernel(xo, cot, cot2, oin, W2g, wox, W1T, G, do_ref, dx1, result,
               wo, x1, n2b, cb, n2T, cT, res, dn2, sres, sdn, rres, rdn, dsend, gws, gwr, send, recv):
    me = Place()
    dp, t, x, c = me.dp, me.t, me.x, me.c
    rows, dm = xo.shape
    width = oin.shape[1]
    C_ = me.at(c=1 - c)
    lanes = Lanes(send, recv)
    for name, count in (("n2", 1), ("dn", 1), ("rs", 1), ("gw", 1), ("do", 4)):
        lanes.block(name, count)
    me.greet(True)
    wide = W2g.shape[2]
    ff = (wide - 256) // 2
    for xs in range(2):
        wo[pl.ds(pl.multiple_of((xs * 2 + c) * width, width), width), :] = W2g[xs, :, 2 * ff : 2 * ff + width].T
        wo[pl.ds(pl.multiple_of((xs * 2 + 1 - c) * width, width), width), :] = wox[xs, :, 0:width].T
    gains = W1T[3 * width : 3 * width + 16, :].astype(f32)
    gain = gains[1:2]
    mid = xo[...].astype(f32) + tn(oin[...].reshape(4 * width, rows), wo[...])
    x1[...] = mid
    inv = lax.rsqrt(jnp.mean(mid * mid, axis=-1, keepdims=True) + 1e-05)
    n2b[0:rows, :] = (mid * inv * gain).astype(bf)
    lanes.start("n2", 0, lambda: (n2b.at[pl.ds(0, rows)], n2b.at[pl.ds(rows, rows)]), C_)
    cb[0:rows, :] = cot[...]
    cb[rows:, :] = cot2[...]
    cT[...] = cb[...].T
    res[...] = jnp.zeros_like(res)
    dn2[...] = jnp.zeros_like(dn2)
    n2T[:, 0:rows] = n2b[0:rows, :].T
    lanes.arrived("n2", 0, n2b.at[pl.ds(rows, rows)], C_)
    n2T[:, rows:] = n2b[rows:, :].T
    per = ff // HB

    def body(k, carry):
        xs = lax.rem(x + lax.div(k, per), 2)
        col = pl.multiple_of(lax.rem(k, per) * HB, HB)
        wh = W2g[xs, :, pl.ds(col, HB)]
        wb = W2g[xs, :, pl.ds(ff + col, HB)]
        u = nn(n2b[...], wh)
        act, slope = gelu_and_slope(u)
        act = act.astype(bf)
        du = (nn(cb[...], wb) * slope).astype(bf)
        dn2[...] += nt(du, wh)
        res[...] += nt(act, wb)
        G[xs, :, pl.ds(col, HB)] = nn(n2T[...], du).astype(bf)
        G[xs, :, pl.ds(ff + col, HB)] = nn(cT[...], act).astype(bf)
        return carry

    lax.fori_loop(0, 2 * per, body, 0)
    sdn[...] = dn2[rows:, :].astype(bf)
    lanes.start("dn", 0, lambda: (sdn, rdn), C_)
    sres[...] = res[rows:, :].astype(bf)
    lanes.start("rs", 0, lambda: (sres, rres), C_)
    lanes.arrived("dn", 0, rdn, C_)
    back = cot[...].astype(f32) + norm_pull(x1[...], gain, dn2[0:rows, :] + rdn[...].astype(f32))
    dx1[...] = back
    back = back.astype(bf)
    out = nt(wo[...], back).astype(bf)
    for r in range(4):
        dsend[r] = out[r * width : (r + 1) * width]

        def to_owner(r=r):
            i = lanes.base["do"]
            return pltpu.make_async_remote_copy(
                src_ref=dsend.at[r], dst_ref=do_ref.at[t], send_sem=send.at[i + r], recv_sem=recv.at[i + t],
                device_id=(dp, r), device_id_type=MESH,
            )

        @pl.when(t == r)
        def _():
            do_ref[t] = dsend[r]

        pl.when(t != r)(lambda: to_owner().start())
        lanes.late.append((lambda r=r, f=to_owner: f(r).wait_send(), lambda r=r: t != r))
    gw = nt(back.T, oin[...].reshape(4 * width, rows)).astype(bf)
    for xs in range(2):
        even, odd = gw[:, 2 * xs * width : (2 * xs + 1) * width], gw[:, (2 * xs + 1) * width : (2 * xs + 2) * width]
        G[xs, :, 2 * ff : 2 * ff + width] = jnp.where(c == 0, even, odd)
        G[xs, :, 2 * ff + width :] = jnp.zeros((dm, wide - 2 * ff - width), bf)
        gws[xs, :, 0:width] = jnp.where(c == 0, odd, even)
        gws[xs, :, width:] = jnp.zeros((dm, 256 - width), bf)
    lanes.start("gw", 0, lambda: (gws, gwr), C_)
    lanes.arrived("rs", 0, rres, C_)
    result[...] = (x1[...] + res[0:rows, :] + rres[...].astype(f32)).astype(bf)
    lanes.arrived("gw", 0, gwr, C_)
    for xs in range(2):
        cols = slice(2 * ff, 2 * ff + width)
        G[xs, :, cols] = (G[xs, :, cols].astype(f32) + gwr[xs, :, 0:width].astype(f32)).astype(bf)
    for there in ((1 - x) * 2 + c, x * 2 + 1 - c, (1 - x) * 2 + 1 - c):
        lanes.arrived("do", there, do_ref.at[there], (dp, there))
    lanes.finish()


def run_mid(xo, cot, cot2, oin, W2g, wox, W1T):
    rows, dm = xo.shape
    wide = W2g.shape[2]
    width = oin.shape[1]
    s = jax.ShapeDtypeStruct
    v = pltpu.VMEM
    return pl.pallas_call(
        mid_kernel,
        out_shape=(s((2, dm, wide), bf), s((4, width, rows), bf), s((rows, dm), f32), s((rows, dm), bf)),
        in_specs=[VM] * 7,
        out_specs=(VM,) * 4,
        scratch_shapes=[
            v((dm, dm), bf), v((rows, dm), f32), v((2 * rows, dm), bf), v((2 * rows, dm), bf),
            v((dm, 2 * rows), bf), v((dm, 2 * rows), bf), v((2 * rows, dm), f32), v((2 * rows, dm), f32),
            v((rows, dm), bf), v((rows, dm), bf), v((rows, dm), bf), v((rows, dm), bf),
            v((4, width, rows), bf), v((2, dm, 256), bf), v((2, dm, 256), bf),
            pltpu.SemaphoreType.DMA((8,)), pltpu.SemaphoreType.DMA((8,)),
        ],
        compiler_params=params(2),
    )(xo, cot, cot2, oin, W2g, wox, W1T)


def bwd_kernel(xo, dx1, n1, qh, o_ref, do_ref, L_ref, low_ref, W1T, G0, w1, w2,
               gin, g1s, g2s, gains, G, dqh, kn, vn, dk, dv, X4, R1, R2, G1, RY, RZ, RA, RB, RA2, RB2, ZL, ZR, gs, gr, send, recv):
    me = Place()
    dp, t, x, y, z, c = me.dp, me.t, me.x, me.y, me.z, me.c
    rows, dm = xo.shape
    total = n1.shape[0]
    blocks = total // B
    heads = qh.shape[0]
    part = w1.shape[0]
    X_, Y_, C_, XC_ = me.at(x=1 - x), me.at(y=1 - y), me.at(c=1 - c), me.at(x=1 - x, c=1 - c)
    left, right = me.at(z=z - 1), me.at(z=z + 1)
    lanes = Lanes(send, recv)
    for name, count in (
        ("ra", 8), ("rb", 8), ("ra2", 4), ("rb2", 4), ("zR", 4), ("zL", 4),
        ("d1", 2), ("d2", 1), ("y1", 4 * heads), ("z1", 3 * heads), ("g", 3),
    ):
        lanes.block(name, count)
    me.greet(True)
    G[...] = G0[...]

    pairs = [sides(me, rnd) for rnd in range(NZ)]

    def each(rnd, act):
        for zi, from_left, ok in pairs[rnd]:
            if ok is None:
                act(zi, from_left, None)
            else:
                pl.when(ok())(functools.partial(act, zi, from_left, ok))

    def first(zi, from_left, ok):
        for k in range(2):
            lanes.start("ra", lambda k=k: zi * 2 + k, lambda k=k: (G.at[k, zi * 2 + 1 - y, :, 0:CUT], RA.at[zi, k]), Y_, ok)
            lanes.start("rb", lambda k=k: zi * 2 + k, lambda k=k: (G.at[1 - x, zi * 2 + k, :, CUT:], RB.at[zi, k]), X_, ok)

    def add(xs, di, cols, *more):
        value = G[xs, di, :, cols].astype(f32)
        for m in more:
            value = value + m.astype(f32)
        G[xs, di, :, cols] = value.astype(bf)

    def second(zi, from_left, ok):
        A, Bc = slice(0, CUT), slice(CUT, None)
        for k in range(2):
            lanes.arrived("ra", zi * 2 + k, RA.at[zi, k], Y_)
            lanes.arrived("rb", zi * 2 + k, RB.at[zi, k], X_)
        add(1 - x, zi * 2 + y, A, RA[zi, 1 - x])
        lanes.start("ra2", zi, lambda: (G.at[1 - x, zi * 2 + y, :, 0:CUT], RA2.at[zi]), X_, ok)
        add(x, zi * 2 + 1 - y, Bc, RB[zi, 1 - y])
        lanes.start("rb2", zi, lambda: (G.at[x, zi * 2 + 1 - y, :, CUT:], RB2.at[zi]), Y_, ok)
        add(x, zi * 2 + y, A, RA[zi, x])
        add(x, zi * 2 + y, Bc, RB[zi, y])

    def third(zi, from_left, ok):
        lanes.arrived("ra2", zi, RA2.at[zi], X_)
        lanes.arrived("rb2", zi, RB2.at[zi], Y_)
        add(x, zi * 2 + y, slice(0, CUT), RA2[zi])
        add(x, zi * 2 + y, slice(CUT, None), RB2[zi])

    def chain(zi, to_left, ok):
        @pl.when(z < NZ - 1 if to_left else z > 0)
        def _():
            lane, buf, there = ("zL", ZR, right) if to_left else ("zR", ZL, left)
            lanes.arrived(lane, zi, buf.at[zi], there)
            add(x, zi * 2 + y, slice(None), buf[zi])

        def ends():
            return G.at[x, zi * 2 + y], (ZR if to_left else ZL).at[zi]

        lanes.start("zL" if to_left else "zR", zi, ends, left if to_left else right, ok)

    def last():
        @pl.when(z < NZ - 1)
        def _():
            lanes.arrived("zL", z, ZR.at[z], right)
            add(x, dp, slice(None), ZR[z])

        @pl.when(z > 0)
        def _():
            lanes.arrived("zR", z, ZL.at[z], left)
            add(x, dp, slice(None), ZL[z])

        g2s[...] = G[x, dp].astype(f32)

    for rnd in (3, 2, 1, 0):
        each(rnd, first)

    def one_y(h):
        for zi in range(NZ):
            lanes.start_at("y1", h * 4 + zi, G1.at[h, zi * 2 + 1 - y], RY.at[h, zi], Y_)

    def one_z(h):
        for step in range(NZ):
            zi = lax.rem(z + step, NZ)
            lanes.arrived("y1", h * 4 + zi, RY.at[h, zi], Y_)
            G1[h, zi * 2 + y] = (G1[h, zi * 2 + y].astype(f32) + RY[h, zi].astype(f32)).astype(bf)
            if step:
                lanes.start_at("z1", h * 3 + step - 1, G1.at[h, zi * 2 + y], RZ.at[h, step - 1], me.at(z=zi))

    def one_last(h):
        value = G1[h, dp].astype(f32)
        for step in range(1, NZ):
            lanes.arrived("z1", h * 3 + step - 1, RZ.at[h, step - 1], me.at(z=lax.rem(z + NZ - step, NZ)))
            value = value + RZ[h, step - 1].astype(f32)
        g1s[:, h * 256 : (h + 1) * 256] = value
        return value

    def rows_first(r):
        xr, cr = r // 2, r % 2
        piece = dqh[:, :, r * rows : (r + 1) * rows].reshape(heads * 3 * E, rows)
        X4[r] = tn(piece, W1T[0 : heads * 3 * E, :]).astype(bf)
        pl.when(c != cr)(lambda: lanes.start_at("d1", xr, X4.at[r], R1.at[xr], C_))

    def rows_second(r):
        xr, cr = r // 2, r % 2

        @pl.when(c == cr)
        def _():
            lanes.arrived("d1", xr, R1.at[xr], C_)
            X4[r] = (X4[r].astype(f32) + R1[xr].astype(f32)).astype(bf)
            pl.when(x != xr)(lambda: lanes.start_at("d2", 0, X4.at[r], R2, X_))

    events = {
        (0, 7): [lambda: each(3, second)],
        (0, 6): [lambda: each(2, second)],
        (0, 5): [lambda: each(3, third), lambda: each(3, chain)],
        (0, 3): [lambda: each(1, second)],
        (0, 0): [lambda: each(2, third), lambda: each(2, chain)],
        (1, 6): [lambda: each(0, second)],
        (1, 4): [lambda: each(1, third), lambda: each(1, chain)],
        (1, 2): [lambda: each(0, third)],
    }

    def head(h, carry):
        kn[...] = qh[h, E : 2 * E, :].T
        vn[...] = qh[h, 2 * E : 3 * E, :].T
        for i in range(blocks)[::-1]:
            j0, js = spans(i)
            cols = slice(i * B, (i + 1) * B)
            half = slice((i % 2) * B, (i % 2 + 1) * B)
            hs = pl.ds(pl.multiple_of(h * E, E), E)
            qT, doT = qh[h, 0:E, cols], do_ref[i // 2, hs, half]
            low, L = low_ref[0:1, cols], L_ref[h, 0:1, cols]
            D = jnp.sum(doT.astype(f32) * o_ref[i // 2, hs, half].astype(f32), axis=0, keepdims=True)
            dq = jnp.zeros((E, B), f32)

            def front(j):
                ks = slice(j * B, (j + 1) * B)
                return nn(kn[ks, :], qT), nn(vn[ks, :], doT)

            queue = [front(j) for j in js[:2]]
            for n, j in enumerate(js):
                ks = slice(j * B, (j + 1) * B)
                if n + 2 < len(js):
                    queue.append(front(js[n + 2]))
                s, dp_ = queue.pop(0)
                p = jnp.exp2(s * (SCALE * LOG2E) - L)
                if masked(i, j, blocks):
                    p = keep(i, j, low, p, 0.0)
                ds = (p * (dp_ - D)).astype(bf)
                dvj, dkj = nt(doT, p.astype(bf)), nt(qT, ds)
                if i == min(blocks - 1, j + WINDOW // B):
                    dv[:, ks] = dvj
                    dk[:, ks] = dkj
                else:
                    dv[:, ks] += dvj
                    dk[:, ks] += dkj
                dq = dq + nn(qh[h, E : 2 * E, ks], ds)
            dqh[h, 0:E, cols] = (dq * SCALE).astype(bf)
            dqh[h, E : 2 * E, cols] = (dk[:, cols] * SCALE).astype(bf)
            dqh[h, 2 * E : 3 * E, cols] = dv[:, cols].astype(bf)
            for k in range(heads):
                for act in events.get((k, i), ()):
                    pl.when(h == k)(act)
            if i == 4:
                pl.when(h > 0)(lambda: one_z(h - 1))
            if i % 2 == 0:

                @pl.when(h == heads - 1)
                def _():
                    rows_first(i // 2)
                    if i // 2 < 3:
                        rows_second(i // 2 + 1)

        g = nn(dqh[h], n1[...]).T.astype(bf).reshape(8, part, 3 * E)
        G1[h, :, :, 0 : 3 * E] = g
        G1[h, :, :, 3 * E :] = jnp.zeros((8, part, 256 - 3 * E), bf)
        one_y(h)
        return carry

    lax.fori_loop(0, heads, head, 0)
    rows_second(0)
    one_z(heads - 1)
    last()
    w1v, w2v = w1[...].astype(f32), w2[...].astype(f32)
    sums = [one_last(h) for h in range(heads)]
    gain1 = sum(
        jnp.sum(sums[h][:, 0 : 3 * E] * w1v[:, h * 3 * E : (h + 1) * 3 * E], axis=1, keepdims=True) for h in range(heads)
    ) / w1v[:, heads * 3 * E : heads * 3 * E + 1]
    ff = (w2.shape[1] - 256) // 2
    gain2 = jnp.sum(g2s[:, 0:ff] * w2v[:, 0:ff], axis=1, keepdims=True) / w1v[:, heads * 3 * E + 1 : heads * 3 * E + 2]
    both_ = jnp.concatenate([gain1, gain2, jnp.zeros((part, 126), f32)], axis=1)
    both_ = jnp.concatenate([both_, jnp.zeros((128 - part, 128), f32)], axis=0).T[0:8]
    gs[...] = both_
    for k, there in enumerate((X_, C_, XC_)):
        lanes.start("g", k, lambda k=k: (gs, gr.at[k]), there)
    gain = W1T[heads * 3 * E : heads * 3 * E + 16, :].astype(f32)[0:1]
    lanes.arrived("d2", 0, R2, X_)
    dn1 = X4[t].astype(f32) + R2[...].astype(f32)
    gin[...] = (dx1[...] + norm_pull(xo[...].astype(f32), gain, dn1)).astype(bf)
    for k, there in enumerate((X_, C_, XC_)):
        lanes.arrived("g", k, gr.at[k], there)
    gains[...] = gs[...] + gr[0] + gr[1] + gr[2]
    for h in range(heads):
        for zi in range(NZ):
            lanes.copy("y1", h * 4 + zi, G1.at[h, zi * 2 + 1 - y], RY.at[h, zi], Y_).wait_send()
        for step in range(1, NZ):
            zi = lax.rem(z + step, NZ)
            lanes.copy("z1", h * 3 + step - 1, G1.at[h, zi * 2 + y], RZ.at[h, step - 1], me.at(z=zi)).wait_send()
    for r in range(4):
        xr, cr = r // 2, r % 2
        pl.when(c != cr)(lambda: lanes.copy("d1", xr, X4.at[r], R1.at[xr], C_).wait_send())
        pl.when(jnp.logical_and(c == cr, x != xr))(lambda: lanes.copy("d2", 0, X4.at[r], R2, X_).wait_send())
    lanes.finish()


def start_at(self, name, k, src, dst, there):
    self.copy(name, k, src, dst, there).start()


Lanes.start_at = start_at


def run_bwd(xo, dx1, n1, qh, o, do, L, low, W1T, G, w1, w2):
    rows, dm = xo.shape
    total = n1.shape[0]
    heads = qh.shape[0]
    part, wide = w2.shape
    s, v = jax.ShapeDtypeStruct, pltpu.VMEM
    return pl.pallas_call(
        bwd_kernel,
        out_shape=(s((rows, dm), bf), s((part, heads * 256), f32), s((part, wide), f32), s((8, 128), f32)),
        in_specs=[VM] * 12,
        out_specs=(VM,) * 4,
        scratch_shapes=[
            v(G.shape, bf), v(qh.shape, bf), v((total, E), bf), v((total, E), bf), v((E, total), f32), v((E, total), f32),
            v((4, rows, dm), bf), v((2, rows, dm), bf), v((rows, dm), bf),
            v((heads, 8, part, 256), bf), v((heads, 4, part, 256), bf), v((heads, 3, part, 256), bf),
            v((4, 2, part, CUT), bf), v((4, 2, part, wide - CUT), bf), v((4, part, CUT), bf), v((4, part, wide - CUT), bf),
            v((4, part, wide), bf), v((4, part, wide), bf), v((8, 128), f32), v((3, 8, 128), f32),
            pltpu.SemaphoreType.DMA((64,)), pltpu.SemaphoreType.DMA((64,)),
        ],
        compiler_params=params(3),
    )(xo, dx1, n1, qh, o, do, L, low, W1T, G, w1, w2)


def block(inputs, segments, w_query, w_key, w_value, w_output, w_hidden, w_back, gain_one, gain_two, cotangent):
    w1, w2 = pack_weights(w_query, w_key, w_value, w_output, w_hidden, w_back, gain_one, gain_two)
    n1, qh, o, oin, L, low, W1T, W2g, cot2, wox = run_fwd(inputs, w1, w2, cotangent, segments.reshape(1, -1))
    part, wide = w2.shape
    dm = inputs.shape[1]
    G, do, dx1, result = run_mid(inputs, cotangent, cot2, oin, W2g.reshape(2, dm, wide), wox.reshape(2, dm, 256), W1T)
    gin, g1s, g2s, gains = run_bwd(inputs, dx1, n1, qh, o, do, L, low, W1T, G.reshape(2, 8, part, wide), w1, w2)
    width = w_query.shape[1]
    heads = width // E
    ff = w_hidden.shape[1]
    g1s = g1s.reshape(part, heads, 256)[:, :, : 3 * E].reshape(part, heads, 3, E)
    gq, gk, gv = (g1s[:, :, k].reshape(part, width) for k in range(3))
    mine = lax.dynamic_slice_in_dim(gains, lax.axis_index("tensor") * (part // 4), part // 4, axis=1)
    return (result, gin, gq, gk, gv, g2s[:, 2 * ff : 2 * ff + width].T, g2s[:, :ff], g2s[:, ff : 2 * ff].T, mine[0], mine[1])


def normed(value, gain):
    return value * lax.rsqrt(jnp.mean(value * value, axis=-1, keepdims=True) + 1e-05) * gain


def gelu_local(value):
    return jax.nn.gelu(value, approximate=True)


def scores_for(query_block, key_rows, segment_ids, block_start, block_rows):
    positions = jnp.arange(key_rows.shape[0], dtype=jnp.int32)
    query_pos = block_start + jnp.arange(block_rows, dtype=jnp.int32)
    query_seg = lax.dynamic_slice_in_dim(segment_ids, block_start, block_rows)
    scores = jnp.einsum(
        "qhe,khe->hqk", query_block, key_rows, preferred_element_type=jnp.float32
    ) * E ** (-0.5)
    distance = query_pos[:, None] - positions[None, :]
    allowed = (query_seg[:, None] == segment_ids[None, :]) & (distance >= 0) & (distance < WINDOW)
    return jnp.where(allowed[None], scores, -1e30)


def shards(
    inputs,
    segments,
    w_query,
    w_key,
    w_value,
    w_output,
    w_hidden,
    w_back,
    gain_one,
    gain_two,
    cotangent,
):
    owned = (w_query, w_key, w_value, w_output, w_hidden, w_back, gain_one, gain_two)
    gathered = (
        lax.all_gather(owned[0], "dp", axis=0, tiled=True),
        lax.all_gather(owned[1], "dp", axis=0, tiled=True),
        lax.all_gather(owned[2], "dp", axis=0, tiled=True),
        lax.all_gather(owned[3], "dp", axis=1, tiled=True),
        lax.all_gather(owned[4], "dp", axis=0, tiled=True),
        lax.all_gather(owned[5], "dp", axis=1, tiled=True),
        lax.all_gather(owned[6], "dp", axis=0, tiled=True),
        lax.all_gather(owned[7], "dp", axis=0, tiled=True),
    )
    total_rows = segments.shape[0]
    block_rows = min(512, total_rows)
    blocks = total_rows // block_rows
    width = gathered[0].shape[1]
    heads_here = width // E
    scale = E ** (-0.5)
    starts = jnp.arange(blocks, dtype=jnp.int32) * block_rows
    w_joined = jnp.concatenate([gathered[0], gathered[1], gathered[2]], axis=1)
    gain_first = gathered[6].astype(jnp.float32)
    gain_second = gathered[7].astype(jnp.float32)
    inputs_f = inputs.astype(jnp.float32)
    normed_one = normed(inputs_f, gain_first).astype(jnp.bfloat16)
    full_one = lax.all_gather(normed_one, "tensor", axis=0, tiled=True)
    joined = jnp.dot(full_one, w_joined, preferred_element_type=jnp.float32).astype(jnp.bfloat16)
    query_rows = joined[:, :width].reshape(total_rows, heads_here, E)
    key_rows = joined[:, width : 2 * width].reshape(total_rows, heads_here, E)
    value_rows = joined[:, 2 * width :].reshape(total_rows, heads_here, E)
    query_blocks = query_rows.reshape(blocks, block_rows, heads_here, E)

    def forward_block(packed):
        query_block, block_start = packed
        scores = scores_for(query_block, key_rows, segments, block_start, block_rows)
        row_top = jnp.max(scores, axis=-1, keepdims=True)
        weights_exp = jnp.exp(scores - row_top)
        totals = jnp.sum(weights_exp, axis=-1, keepdims=True)
        probability = (weights_exp / totals).astype(jnp.bfloat16)
        attended_block = jnp.einsum(
            "hqk,khe->qhe", probability, value_rows, preferred_element_type=jnp.float32
        )
        return (attended_block.astype(jnp.bfloat16), (row_top + jnp.log(totals))[..., 0])

    attended, log_sums = lax.map(forward_block, (query_blocks, starts))
    attended = attended.reshape(total_rows, width)
    w_out_full = gathered[3]
    own_attended = lax.all_to_all(attended, "tensor", split_axis=0, concat_axis=1, tiled=True)
    w_out_all = lax.all_gather(w_out_full, "tensor", axis=0, tiled=True)
    attn_branch = jnp.dot(own_attended, w_out_all, preferred_element_type=jnp.float32)
    middle = inputs_f + attn_branch
    normed_two = normed(middle, gain_second).astype(jnp.bfloat16)
    full_two = lax.all_gather(normed_two, "tensor", axis=0, tiled=True)
    hidden = jnp.dot(full_two, gathered[4], preferred_element_type=jnp.float32)
    active = gelu_local(hidden).astype(jnp.bfloat16)
    w_back_full = gathered[5]
    result = middle + lax.psum_scatter(
        jnp.dot(active, w_back_full, preferred_element_type=jnp.float32).astype(jnp.bfloat16),
        "tensor",
        scatter_dimension=0,
        tiled=True,
    ).astype(jnp.float32)
    gathered = (
        lax.all_gather(owned[0], "dp", axis=0, tiled=True),
        lax.all_gather(owned[1], "dp", axis=0, tiled=True),
        lax.all_gather(owned[2], "dp", axis=0, tiled=True),
        lax.all_gather(owned[3], "dp", axis=1, tiled=True),
        lax.all_gather(owned[4], "dp", axis=0, tiled=True),
        lax.all_gather(owned[5], "dp", axis=1, tiled=True),
        lax.all_gather(owned[6], "dp", axis=0, tiled=True),
        lax.all_gather(owned[7], "dp", axis=0, tiled=True),
    )
    w_joined = jnp.concatenate([gathered[0], gathered[1], gathered[2]], axis=1)
    grad_out = cotangent.astype(jnp.float32)
    full_grad = lax.all_gather(cotangent, "tensor", axis=0, tiled=True)
    grad_w_back = jnp.einsum("rf,rd->fd", active, full_grad, preferred_element_type=jnp.float32)
    grad_active = jnp.einsum(
        "rd,fd->rf", full_grad, gathered[5], preferred_element_type=jnp.float32
    )
    gelu_pull = jax.vjp(gelu_local, hidden)[1]
    grad_hidden_rows = gelu_pull(grad_active)[0].astype(jnp.bfloat16)
    grad_w_hidden = jnp.einsum(
        "rd,rf->df", full_two, grad_hidden_rows, preferred_element_type=jnp.float32
    )
    w_hidden_full = gathered[4]
    piece = grad_hidden_rows
    grad_normed_two = lax.psum_scatter(
        jnp.einsum("rf,df->rd", piece, w_hidden_full, preferred_element_type=jnp.float32).astype(
            jnp.bfloat16
        ),
        "tensor",
        scatter_dimension=0,
        tiled=True,
    ).astype(jnp.float32)
    second_pull = jax.vjp(normed, middle, gain_second)[1]
    grad_mid_norm, grad_second = second_pull(grad_normed_two)
    grad_middle = grad_out + grad_mid_norm
    full_middle = lax.all_gather(grad_middle.astype(jnp.bfloat16), "tensor", axis=0, tiled=True)
    grad_w_output = jnp.einsum(
        "rh,rd->hd", attended, full_middle, preferred_element_type=jnp.float32
    )
    grad_attended = jnp.einsum(
        "rd,hd->rh", full_middle, gathered[3], preferred_element_type=jnp.float32
    ).astype(jnp.bfloat16)

    def backward_block(carry, packed):
        grad_keys, grad_values = carry
        query_block, grad_block, log_block, block_start = packed
        scores = scores_for(query_block, key_rows, segments, block_start, block_rows)
        probability = jnp.exp(scores - log_block[..., None])
        grad_values = grad_values + jnp.einsum(
            "hqk,qhe->khe",
            probability.astype(jnp.bfloat16),
            grad_block,
            preferred_element_type=jnp.float32,
        )
        grad_probs = jnp.einsum(
            "qhe,khe->hqk", grad_block, value_rows, preferred_element_type=jnp.float32
        )
        delta_rows = jnp.sum(grad_probs * probability, axis=-1, keepdims=True)
        grad_scores = (probability * (grad_probs - delta_rows)).astype(jnp.bfloat16)
        grad_query_block = (
            jnp.einsum("hqk,khe->qhe", grad_scores, key_rows, preferred_element_type=jnp.float32)
            * scale
        )
        grad_keys = (
            grad_keys
            + jnp.einsum(
                "hqk,qhe->khe", grad_scores, query_block, preferred_element_type=jnp.float32
            )
            * scale
        )
        return ((grad_keys, grad_values), grad_query_block)

    zero_state = jnp.zeros((total_rows, heads_here, E), jnp.float32)
    grad_blocks = grad_attended.reshape(blocks, block_rows, heads_here, E)
    (grad_keys, grad_values), grad_queries = lax.scan(
        backward_block, (zero_state, zero_state), (query_blocks, grad_blocks, log_sums, starts)
    )
    grad_joined = jnp.concatenate(
        [
            grad_queries.reshape(total_rows, width),
            grad_keys.reshape(total_rows, width),
            grad_values.reshape(total_rows, width),
        ],
        axis=1,
    ).astype(jnp.bfloat16)
    grad_w_joined = jnp.einsum(
        "rd,rc->dc", full_one, grad_joined, preferred_element_type=jnp.float32
    )
    piece = grad_joined
    grad_normed_one = lax.psum_scatter(
        jnp.einsum("rc,dc->rd", piece, w_joined, preferred_element_type=jnp.float32).astype(
            jnp.bfloat16
        ),
        "tensor",
        scatter_dimension=0,
        tiled=True,
    ).astype(jnp.float32)
    first_pull = jax.vjp(normed, inputs_f, gain_first)[1]
    grad_in_norm, grad_first = first_pull(grad_normed_one)
    grad_inputs = grad_middle + grad_in_norm
    weight_sums = (
        lax.psum_scatter(grad_w_joined[:, :width], "dp", scatter_dimension=0, tiled=True),
        lax.psum_scatter(
            grad_w_joined[:, width : 2 * width], "dp", scatter_dimension=0, tiled=True
        ),
        lax.psum_scatter(grad_w_joined[:, 2 * width :], "dp", scatter_dimension=0, tiled=True),
        lax.psum_scatter(grad_w_output, "dp", scatter_dimension=1, tiled=True),
        lax.psum_scatter(grad_w_hidden, "dp", scatter_dimension=0, tiled=True),
        lax.psum_scatter(grad_w_back, "dp", scatter_dimension=1, tiled=True),
    )
    gain_sums = (
        lax.psum_scatter(grad_first, ("dp", "tensor"), scatter_dimension=0, tiled=True),
        lax.psum_scatter(grad_second, ("dp", "tensor"), scatter_dimension=0, tiled=True),
    )
    return (
        result.astype(jnp.bfloat16),
        grad_inputs.astype(jnp.bfloat16),
        weight_sums[0],
        weight_sums[1],
        weight_sums[2],
        weight_sums[3],
        weight_sums[4],
        weight_sums[5],
        gain_sums[0],
        gain_sums[1],
    )


def solution(mesh):
    rows, cols = P(("dp", "tensor"), None), P("dp", "tensor")
    turned, part = P("tensor", "dp"), P("dp")
    in_specs = (rows, part, cols, cols, cols, turned, cols, turned, part, part, rows)
    out_specs = (rows, rows, cols, cols, cols, turned, cols, turned, P(("dp", "tensor")), P(("dp", "tensor")))
    here = mesh.shape["dp"] == 2 * NZ and mesh.shape["tensor"] == 4
    body = block if here else shards
    return jax.shard_map(body, mesh=mesh, in_specs=in_specs, out_specs=out_specs, check_vma=False)
```

```python
import functools

import jax
import jax.numpy as jnp
from jax import lax
from jax.experimental import pallas as pl
from jax.experimental.pallas import tpu as pltpu
from jax.sharding import PartitionSpec as P

MESH = pl.DeviceIdType.MESH
f32, bf = jnp.float32, jnp.bfloat16
E = 64
WINDOW = 1536
B = 256
LOG2E = 1.4426950408889634
SCALE = E**-0.5
FILL = -1e30
NZ = 4
HB = 256
UNIT = 2 * HB


def nn(a, b):
    return lax.dot_general(a, b, (((1,), (0,)), ((), ())), preferred_element_type=f32)


def nt(a, b):
    return lax.dot_general(a, b, (((1,), (1,)), ((), ())), preferred_element_type=f32)


def tn(a, b):
    return lax.dot_general(a, b, (((0,), (0,)), ((), ())), preferred_element_type=f32)


class Place:
    def __init__(self):
        self.dp = lax.axis_index("dp")
        self.t = lax.axis_index("tensor")
        self.z, self.y = lax.div(self.dp, 2), lax.rem(self.dp, 2)
        self.x, self.c = lax.div(self.t, 2), lax.rem(self.t, 2)
        self.left, self.right = self.at(z=self.z - 1), self.at(z=self.z + 1)
        self.sides = [sides(self, rnd) for rnd in range(NZ)]

    def at(self, z=None, y=None, x=None, c=None):
        z = self.z if z is None else z
        y = self.y if y is None else y
        x = self.x if x is None else x
        c = self.c if c is None else c
        return (z * 2 + y, x * 2 + c)

    def greet(self, far_z):
        barrier = pltpu.get_barrier_semaphore()
        x, y, z, c = self.x, self.y, self.z, self.c
        near = [self.at(y=1 - y), self.at(x=1 - x), self.at(c=1 - c), self.at(x=1 - x, c=1 - c)]
        for there in near:
            pl.semaphore_signal(barrier, inc=1, device_id=there, device_id_type=MESH)
        for step in range(1, NZ):
            pl.semaphore_signal(
                barrier, inc=1, device_id=self.at(z=lax.rem(z + step, NZ)), device_id_type=MESH
            )
        pl.semaphore_wait(barrier, len(near) + NZ - 1)


class Lanes:
    def __init__(self, send, recv):
        self.send, self.recv, self.n, self.base, self.late = send, recv, 0, {}, []

    def block(self, name, count):
        self.base[name] = self.n
        self.n += count

    def copy(self, name, k, src, dst, there):
        i = self.base[name] + k
        return pltpu.make_async_remote_copy(
            src_ref=src,
            dst_ref=dst,
            send_sem=self.send.at[i],
            recv_sem=self.recv.at[i],
            device_id=there,
            device_id_type=MESH,
        )

    def start(self, name, k, ends, there, when=None):
        at = k if callable(k) else lambda: k
        self.copy(name, at(), *ends(), there).start()

        def finish():
            self.copy(name, at(), *ends(), there).wait_send()

        self.late.append((finish, when))

    def start_at(self, name, k, src, dst, there):
        self.copy(name, k, src, dst, there).start()

    def arrived(self, name, k, dst, there):
        self.copy(name, k, dst, dst, there).wait_recv()

    def finish(self):
        for act, when in self.late:
            if when is None:
                act()
            else:
                pl.when(when())(act)


def sides(me, rnd):
    z = me.z
    if rnd == 0:
        return [(z, None, None)]
    return [(z - rnd, True, lambda: z >= rnd), (z + rnd, False, lambda: z + rnd < NZ)]


def line_round(me, lanes, name, rnd, ref_of, arrive):
    z = me.z
    left, right = me.left, me.right

    def go(zi, to_right, when):
        def side():
            return z < NZ - 1 if to_right else z > 0

        def whole():
            return side() if when is None else jnp.logical_and(when(), side())

        lane, there = name + ("R" if to_right else "L"), right if to_right else left

        def copy():
            return lanes.copy(lane, zi, ref_of(zi), ref_of(zi), there)

        pl.when(side())(lambda: copy().start())
        lanes.late.append((lambda: copy().wait_send(), whole))

    for zi, from_left, ok in me.sides[rnd]:
        if rnd == 0:
            go(zi, True, None)
            go(zi, False, None)
            arrive(zi, None)
            continue

        @pl.when(ok())
        def _(zi=zi, from_left=from_left, ok=ok):
            lanes.arrived(name + ("R" if from_left else "L"), zi, ref_of(zi), left if from_left else right)
            go(zi, from_left, ok)
            arrive(zi, ok)


def masked(i, j, blocks):
    return j == i or j == 0 or i >= blocks - 2 or i - j >= WINDOW // B


def keep(i, j, low, value, fill):
    key_pos = lax.broadcasted_iota(jnp.int32, value.shape, 0) + j * B
    ok = key_pos >= low
    if i == j:
        ok = ok & (key_pos <= lax.broadcasted_iota(jnp.int32, value.shape, 1) + i * B)
    return jnp.where(ok, value, fill)


def spans(i):
    first = max(0, i - WINDOW // B)
    return first, list(range(first, i + 1))


def score_pass(i, h, slot, blocks, kn, qh, low_ref, S):
    j0, js = spans(i)
    cols = slice(i * B, (i + 1) * B)
    qT = qh[h, 0:E, cols]
    low = low_ref[0:1, cols]
    top = jnp.full((1, B), FILL, f32)
    for j in js:
        s = nn(kn[h, j * B : (j + 1) * B, :], qT)
        if masked(i, j, blocks):
            s = keep(i, j, low, s, FILL)
        S[slot, (j - j0) * B : (j - j0 + 1) * B, :] = s
        top = jnp.maximum(top, jnp.max(s, axis=0, keepdims=True))
    return top * (SCALE * LOG2E)


def value_pass(i, h, slot, top, qh, S, o_ref, L_ref):
    j0, js = spans(i)
    total = jnp.zeros((1, B), f32)
    out = jnp.zeros((E, B), f32)
    for j in js:
        p = jnp.exp2(S[slot, (j - j0) * B : (j - j0 + 1) * B, :] * (SCALE * LOG2E) - top)
        total = total + jnp.sum(p, axis=0, keepdims=True)
        out = out + nn(qh[h, 2 * E : 3 * E, j * B : (j + 1) * B], p.astype(bf))
    half = i % 2
    o_ref[i // 2, pl.ds(pl.multiple_of(h * E, E), E), half * B : (half + 1) * B] = (out / total).astype(bf)
    L_ref[h, :, i * B : (i + 1) * B] = jnp.broadcast_to(top + jnp.log2(total), (8, B))


def lows(seg, total):
    pos = lax.broadcasted_iota(jnp.int32, (1, total), 1)
    low = jnp.maximum(pos - (WINDOW - 1), 0)
    first = seg[0:1, 0:1]
    for d in range(1, 5):
        begin = jnp.sum((seg < first + d).astype(f32), axis=1, keepdims=True).astype(jnp.int32)
        low = jnp.where(seg >= first + d, jnp.maximum(low, begin), low)
    return low


def gelu_and_slope(u):
    root = 0.7978845608028654
    square = u * u
    th = jnp.tanh(u * (root + (root * 0.044715) * square))
    half = 0.5 + 0.5 * th
    slope = half + (0.5 * u) * (1.0 - th * th) * (root + (3.0 * root * 0.044715) * square)
    return u * half, slope


def norm_pull(value, gain, grad):
    inv = lax.rsqrt(jnp.mean(value * value, axis=-1, keepdims=True) + 1e-05)
    scaled = grad * gain
    return inv * scaled - value * (inv * inv * inv * jnp.mean(value * scaled, axis=-1, keepdims=True))


def kernel(xo, cot, seg, wq, wk, wv, wo, wh, wb, g1, g2,
           gin, result, g1s, g2s, gains,
           X4, n1, W1, W1T, W5, G5, WO, qh, o_ref, oin, L_ref, low_ref, cb, n2b, x1, rdn, rres, dsend, do_ref,
           gws, gwr, gwx, R1, R2, G1, RY, RZ, RA, RB, RA2, RB2, RZ2, gs, gr, send, recv):
    me = Place()
    dp, t, x, y, z, c = me.dp, me.t, me.x, me.y, me.z, me.c
    rows, dm = xo.shape
    total = n1.shape[0]
    blocks = total // B
    heads = qh.shape[0]
    part, width = wq.shape
    ff = wh.shape[1]
    units = ff // HB
    X_, Y_, C_, XC_ = me.at(x=1 - x), me.at(y=1 - y), me.at(c=1 - c), me.at(x=1 - x, c=1 - c)
    far = [None] + [me.at(z=lax.rem(z + step, NZ)) for step in range(1, NZ)]
    near_t, cross_t, core_t = (1 - x) * 2 + c, (1 - x) * 2 + 1 - c, x * 2 + 1 - c
    lanes = Lanes(send, recv)
    for name, count in (
        ("aR", 4), ("aL", 4), ("ay", 4), ("x", 2), ("cx", 2), ("co", 1), ("cc", 1),
        ("wz", 3), ("wy", 1), ("wx", 1), ("wc", 2),
        ("bz", 3 * units), ("by", units), ("bx", units), ("bxy", units), ("byx", 1), ("o", 4),
        ("n2", 1), ("dn", 1), ("rs", 1), ("gw", 1), ("gx", 1), ("do", 4),
        ("ra", 2 * units), ("rb", 1), ("ra2", units), ("rb2", 1), ("z2", 3 * units),
        ("d1", 2), ("d2", 1), ("y1", 4 * (heads + 1)), ("z1", 3 * (heads + 1)), ("g", 3),
    ):
        lanes.block(name, count)

    def unit(u):
        return pl.ds(u * UNIT, UNIT)

    def first_route(u):
        return pl.ds(u * UNIT, UNIT if u < units - 1 else HB)

    other_route = pl.ds((units - 1) * UNIT + HB, HB)

    me.greet(True)
    zeros = jnp.zeros((part, 56), f32)
    both_gains = jnp.concatenate([g1[...].astype(f32), g2[...].astype(f32), jnp.zeros((6, part), f32)], axis=0)
    both_gains = jnp.concatenate([both_gains, jnp.zeros((8, 128 - part), f32)], axis=1).T[0:part]
    pieces = []
    for h in range(heads):
        for w in (wq, wk, wv):
            pieces.append(w[:, h * E : (h + 1) * E])
    pieces.append(jnp.concatenate([both_gains, zeros], axis=1).astype(bf))
    W1[dp] = jnp.concatenate(pieces, axis=1)

    def a_ref(zi):
        return W1.at[zi * 2 + y]

    def a_arrive(zi, when):
        lanes.start("ay", zi, lambda: (a_ref(zi), a_ref(zi)), Y_, when)

    half = rows // 2
    line_round(me, lanes, "a", 0, a_ref, a_arrive)
    for k in range(2):
        lanes.start("x", k, lambda k=k: (xo.at[pl.ds(k * half, half)], X4.at[t, pl.ds(k * half, half)]), X_)
    lanes.start("co", 0, lambda: (xo, X4.at[t]), C_)
    lanes.start("cc", 0, lambda: (cot, cb.at[pl.ds(rows, rows)]), C_)
    WO[t, z, y] = jnp.concatenate([wo[...].T, jnp.zeros((part, 256 - width), bf)], axis=1)
    back_T = wb[...].T
    for u in range(units):
        W5[x, z, y, :, u * UNIT : u * UNIT + HB] = wh[:, u * HB : (u + 1) * HB]
        W5[x, z, y, :, u * UNIT + HB : (u + 1) * UNIT] = back_T[:, u * HB : (u + 1) * HB]
    low_ref[...] = jnp.broadcast_to(lows(seg[...], total), low_ref.shape)
    X4[t] = xo[...]
    cb[0:rows, :] = cot[...]

    def w_z():
        for step in range(1, NZ):
            lanes.start("wz", step - 1, lambda: (WO.at[t, z, y],) * 2, far[step])

    def from_z(step):
        return lax.rem(z + NZ - step, NZ)

    def w_y():
        for step in range(1, NZ):
            lanes.arrived("wz", step - 1, WO.at[t, from_z(step), y], far[NZ - step])
        lanes.start("wy", 0, lambda: (WO.at[t, :, y],) * 2, Y_)

    def w_x():
        lanes.arrived("wy", 0, WO.at[t, :, 1 - y], Y_)
        lanes.start("wx", 0, lambda: (WO.at[t],) * 2, X_)
        lanes.start("wc", 0, lambda: (WO.at[t],) * 2, C_)

    def w_c():
        lanes.arrived("wx", 0, WO.at[near_t], X_)
        lanes.start("wc", 1, lambda: (WO.at[near_t],) * 2, C_)

    def w_end():
        lanes.arrived("wc", 0, WO.at[core_t], C_)
        lanes.arrived("wc", 1, WO.at[cross_t], C_)

    def b_z(u):
        for step in range(1, NZ):
            lanes.start("bz", u * 3 + step - 1, lambda: (W5.at[x, z, y, :, unit(u)],) * 2, far[step])

    def b_y(u):
        for step in range(1, NZ):
            lanes.arrived("bz", u * 3 + step - 1, W5.at[x, from_z(step), y, :, unit(u)], far[NZ - step])
        lanes.start("by", u, lambda: (W5.at[x, :, y, :, unit(u)],) * 2, Y_)

    def b_x(u):
        lanes.start("bx", u, lambda: (W5.at[x, :, y, :, unit(u)],) * 2, X_)

    def b_corner(u):
        lanes.arrived("bx", u, W5.at[1 - x, :, y, :, unit(u)], X_)
        lanes.start("bxy", u, lambda: (W5.at[1 - x, :, y, :, first_route(u)],) * 2, Y_)

    def b_near(u):
        lanes.arrived("by", u, W5.at[x, :, 1 - y, :, unit(u)], Y_)
        if u == units - 1:
            lanes.start("byx", 0, lambda: (W5.at[x, :, 1 - y, :, other_route],) * 2, X_)

    def b_end(u):
        lanes.arrived("bxy", u, W5.at[1 - x, :, 1 - y, :, first_route(u)], Y_)
        if u == units - 1:
            lanes.arrived("byx", 0, W5.at[1 - x, :, 1 - y, :, other_route], X_)

    def quarter(r, kn, S, events):
        def body(h, carry):
            tops = []
            for i in (2 * r, 2 * r + 1):
                tops.append(score_pass(i, h, i % 2, blocks, kn, qh, low_ref, S))
            for i in (2 * r, 2 * r + 1):
                value_pass(i, h, i % 2, tops[i % 2], qh, S, o_ref, L_ref)
            for k in range(heads):
                if k in events:
                    pl.when(h == k)(lambda: [act() for act in events[k]] and None)
            return carry

        lax.fori_loop(0, heads, body, 0)

        def out_copy():
            base = lanes.base["o"]
            return pltpu.make_async_remote_copy(
                src_ref=o_ref.at[r], dst_ref=oin.at[t], send_sem=send.at[base + r], recv_sem=recv.at[base + t],
                device_id=(dp, r), device_id_type=MESH,
            )

        @pl.when(t == r)
        def _():
            oin[t] = o_ref[r]

        pl.when(t != r)(lambda: out_copy().start())
        lanes.late.append((lambda: out_copy().wait_send(), lambda: t != r))

    def forward(kn, S):
        line_round(me, lanes, "a", 1, a_ref, a_arrive)
        line_round(me, lanes, "a", 2, a_ref, a_arrive)
        w_z()
        line_round(me, lanes, "a", 3, a_ref, a_arrive)
        b_z(0)
        for zi in range(NZ):
            lanes.arrived("ay", zi, W1.at[zi * 2 + 1 - y], Y_)
        w_y()
        W1T[...] = W1[...].reshape(2 * NZ * part, W1.shape[2]).T

        def project(blk):
            base = pl.multiple_of(blk * rows, rows)
            gain = W1T[heads * 3 * E : heads * 3 * E + 16, :].astype(f32)[0:1]
            value = X4[blk].astype(f32)
            inv = lax.rsqrt(jnp.mean(value * value, axis=-1, keepdims=True) + 1e-05)
            normed = (value * inv * gain).astype(bf)
            n1[pl.ds(base, rows), :] = normed
            out = nt(W1T[0 : heads * 3 * E, :], normed).astype(bf)
            for h in range(heads):
                qh[h, :, pl.ds(base, rows)] = out[h * 3 * E : (h + 1) * 3 * E]
                kn[h, pl.ds(base, rows), :] = out[h * 3 * E + E : h * 3 * E + 2 * E].T

        project(t)
        lanes.arrived("co", 0, X4.at[core_t], C_)
        project(core_t)
        b_y(0)
        b_z(1)
        for k in range(2):
            got = X4.at[near_t, pl.ds(k * half, half)]
            lanes.arrived("x", k, got, X_)
            lanes.start_at("cx", k, got, got, C_)
        w_x()
        project(near_t)
        for k in range(2):
            lanes.arrived("cx", k, X4.at[cross_t, pl.ds(k * half, half)], C_)
        project(cross_t)
        b_x(0)
        quarter(0, kn, S, {})
        b_y(1)
        b_z(2)
        w_c()
        b_x(1)
        quarter(1, kn, S, {})
        b_corner(0)
        quarter(2, kn, S, {0: [lambda: b_y(2)]})
        b_x(2)
        b_near(0)
        b_corner(1)
        quarter(3, kn, S, {})

    pl.run_scoped(forward, pltpu.VMEM((heads, total, E), bf), pltpu.VMEM((2, WINDOW + B, B), f32))

    r_unit = lanes.base["ra"]

    def sum_first(xs, u):
        lanes.start_at("ra", xs * units + u, G5.at[xs, :, 1 - y, :, first_route(u)], RA.at[xs, :, :, first_route(u)], Y_)

    def middle(wof, n2T, cT, res, dn2):
        w_end()
        for k in range(4):
            wof[k * width : (k + 1) * width, :] = WO[k].reshape(dm, 256)[:, 0:width].T
        gain = W1T[heads * 3 * E : heads * 3 * E + 16, :].astype(f32)[1:2]
        lanes.arrived("cc", 0, cb.at[pl.ds(rows, rows)], C_)
        cT[...] = cb[...].T
        for there in (near_t, core_t, cross_t):
            lanes.arrived("o", there, oin.at[there], (dp, there))
        mid = xo[...].astype(f32) + tn(oin[...].reshape(4 * width, rows), wof[...])
        x1[...] = mid
        inv = lax.rsqrt(jnp.mean(mid * mid, axis=-1, keepdims=True) + 1e-05)
        n2b[0:rows, :] = (mid * inv * gain).astype(bf)
        lanes.copy("n2", 0, n2b.at[pl.ds(0, rows)], n2b.at[pl.ds(rows, rows)], C_).start()
        res[...] = jnp.zeros_like(res)
        dn2[...] = jnp.zeros_like(dn2)
        n2T[:, 0:rows] = n2b[0:rows, :].T
        lanes.arrived("n2", 0, n2b.at[pl.ds(rows, rows)], C_)
        n2T[:, rows:] = n2b[rows:, :].T

        def step(xs, u):
            col = u * UNIT
            w_h = W5[xs, :, :, :, col : col + HB].reshape(dm, HB)
            w_b = W5[xs, :, :, :, col + HB : col + UNIT].reshape(dm, HB)
            hid = nn(n2b[...], w_h)
            act, slope = gelu_and_slope(hid)
            act = act.astype(bf)
            du = (nn(cb[...], w_b) * slope).astype(bf)
            dn2[...] += nt(du, w_h)
            res[...] += nt(act, w_b)
            G5[xs, :, :, :, col : col + HB] = nn(n2T[...], du).astype(bf).reshape(NZ, 2, part, HB)
            G5[xs, :, :, :, col + HB : col + UNIT] = nn(cT[...], act).astype(bf).reshape(NZ, 2, part, HB)

        for k in range(2):
            xs = x if k == 0 else 1 - x
            for u in range(units):
                if k == 0 and u > 0:
                    b_near(u)
                if k == 0 and u == 1:
                    b_corner(2)
                if k == 1:
                    b_end(u)
                step(xs, u)
                sum_first(xs, u)
        lanes.start_at("rb", 0, G5.at[1 - x, :, :, :, other_route], RB, X_)
        lanes.copy("n2", 0, n2b.at[pl.ds(0, rows)], n2b.at[pl.ds(rows, rows)], C_).wait_send()
        n2b[0:rows, :] = dn2[rows:, :].astype(bf)
        lanes.start("dn", 0, lambda: (n2b.at[pl.ds(0, rows)], rdn), C_)
        n2b[rows:, :] = res[rows:, :].astype(bf)
        lanes.start("rs", 0, lambda: (n2b.at[pl.ds(rows, rows)], rres), C_)
        lanes.arrived("dn", 0, rdn, C_)
        back = cot[...].astype(f32) + norm_pull(x1[...], gain, dn2[0:rows, :] + rdn[...].astype(f32))
        lanes.arrived("rs", 0, rres, C_)
        result[...] = (x1[...] + res[0:rows, :] + rres[...].astype(f32)).astype(bf)
        x1[...] = back
        back = back.astype(bf)
        out = nt(wof[...], back).astype(bf)
        for r in range(4):
            dsend[r] = out[r * width : (r + 1) * width]

            def to_owner(r=r):
                i = lanes.base["do"]
                return pltpu.make_async_remote_copy(
                    src_ref=dsend.at[r], dst_ref=do_ref.at[t], send_sem=send.at[i + r], recv_sem=recv.at[i + t],
                    device_id=(dp, r), device_id_type=MESH,
                )

            @pl.when(t == r)
            def _():
                do_ref[t] = dsend[r]

            pl.when(t != r)(lambda: to_owner().start())
            lanes.late.append((lambda r=r, f=to_owner: f(r).wait_send(), lambda r=r: t != r))
        gw = nt(back.T, oin[...].reshape(4 * width, rows)).astype(bf)
        pad = jnp.zeros((dm, 256 - width), bf)
        for xs in range(2):
            even, odd = gw[:, 2 * xs * width : (2 * xs + 1) * width], gw[:, (2 * xs + 1) * width : (2 * xs + 2) * width]
            gws[xs] = jnp.concatenate([jnp.where(c == 0, odd, even), pad], axis=1)
            gws[2 + xs] = jnp.concatenate([jnp.where(c == 0, even, odd), pad], axis=1)
        lanes.start("gw", 0, lambda: (gws.at[pl.ds(0, 2)], gwr), C_)

    pl.run_scoped(
        middle, pltpu.VMEM((dm, dm), bf), pltpu.VMEM((dm, 2 * rows), bf), pltpu.VMEM((dm, 2 * rows), bf),
        pltpu.VMEM((2 * rows, dm), f32), pltpu.VMEM((2 * rows, dm), f32),
    )

    def w_back_x():
        lanes.arrived("gw", 0, gwr, C_)
        gws[2 + 1 - x] = (gws[2 + 1 - x].astype(f32) + gwr[1 - x].astype(f32)).astype(bf)
        lanes.start("gx", 0, lambda: (gws.at[2 + 1 - x], gwx), X_)
        gws[2 + x] = (gws[2 + x].astype(f32) + gwr[x].astype(f32)).astype(bf)

    def w_back_y():
        lanes.arrived("gx", 0, gwx, X_)
        G1[heads] = (gws[2 + x].astype(f32) + gwx[...].astype(f32)).astype(bf).reshape(2 * NZ, part, 256)
        one_y(heads)

    def add(ref_at, *more):
        value = ref_at[...].astype(f32)
        for m in more:
            value = value + m.astype(f32)
        ref_at[...] = value.astype(bf)

    def second(u):
        lanes.arrived("ra", (1 - x) * units + u, RA.at[1 - x, :, :, first_route(u)], Y_)
        add(G5.at[1 - x, :, y, :, first_route(u)], RA[1 - x, :, :, first_route(u)])
        lanes.start_at("ra2", u, G5.at[1 - x, :, y, :, first_route(u)], RA2.at[:, :, first_route(u)], X_)

    def second_other():
        lanes.arrived("rb", 0, RB, X_)
        add(G5.at[x, :, 1 - y, :, other_route], RB[:, 1 - y])
        lanes.start_at("rb2", 0, G5.at[x, :, 1 - y, :, other_route], RB2, Y_)

    def third(u):
        lanes.arrived("ra", x * units + u, RA.at[x, :, :, first_route(u)], Y_)
        lanes.arrived("ra2", u, RA2.at[:, :, first_route(u)], X_)
        add(G5.at[x, :, y, :, first_route(u)], RA[x, :, :, first_route(u)], RA2[:, :, first_route(u)])
        if u == units - 1:
            lanes.arrived("rb2", 0, RB2, Y_)
            add(G5.at[x, :, y, :, other_route], RB[:, y], RB2[...])
        for step in range(1, NZ):
            zi = lax.rem(z + step, NZ)
            lanes.start_at("z2", u * 3 + step - 1, G5.at[x, zi, y, :, unit(u)], RZ2.at[step - 1, :, unit(u)], far[step])

    def last():
        value = G5[x, z, y].astype(f32)
        for step in range(1, NZ):
            for u in range(units):
                lanes.arrived("z2", u * 3 + step - 1, RZ2.at[step - 1, :, unit(u)], far[NZ - step])
            value = value + RZ2[step - 1].astype(f32)
        g2s[...] = value

    def one_y(h):
        for zi in range(NZ):
            lanes.start_at("y1", h * 4 + zi, G1.at[h, zi * 2 + 1 - y], RY.at[h, zi], Y_)

    def one_z(h):
        for step in range(NZ):
            zi = lax.rem(z + step, NZ)
            lanes.arrived("y1", h * 4 + zi, RY.at[h, zi], Y_)
            G1[h, zi * 2 + y] = (G1[h, zi * 2 + y].astype(f32) + RY[h, zi].astype(f32)).astype(bf)
            if step:
                lanes.start_at("z1", h * 3 + step - 1, G1.at[h, zi * 2 + y], RZ.at[h, step - 1], far[step])

    def one_last(h):
        value = G1[h, dp].astype(f32)
        for step in range(1, NZ):
            lanes.arrived("z1", h * 3 + step - 1, RZ.at[h, step - 1], far[NZ - step])
            value = value + RZ[h, step - 1].astype(f32)
        g1s[:, h * 256 : (h + 1) * 256] = value
        return value

    def backward(kn, vn, dk, dv):
        def rows_first(r):
            xr, cr = r // 2, r % 2
            piece = qh[:, :, r * rows : (r + 1) * rows].reshape(heads * 3 * E, rows)
            X4[r] = tn(piece, W1T[0 : heads * 3 * E, :]).astype(bf)
            pl.when(c != cr)(lambda: lanes.start_at("d1", xr, X4.at[r], R1.at[xr], C_))

        def rows_second(r):
            xr, cr = r // 2, r % 2

            @pl.when(c == cr)
            def _():
                lanes.arrived("d1", xr, R1.at[xr], C_)
                X4[r] = (X4[r].astype(f32) + R1[xr].astype(f32)).astype(bf)
                pl.when(x != xr)(lambda: lanes.start_at("d2", 0, X4.at[r], R2, X_))

        events = {
            (0, 7): [w_back_x],
            (0, 5): [w_back_y],
            (0, 3): [],
            (0, 0): [lambda: one_z(heads), lambda: second(0)],
            (1, 6): [],
            (1, 4): [lambda: second(1)],
            (1, 2): [second_other],
            (1, 1): [lambda: second(2)],
            (2, 7): [lambda: third(0)],
            (2, 4): [lambda: third(1)],
        }

        def head(h, carry):
            kn[...] = qh[h, E : 2 * E, :].T
            vn[...] = qh[h, 2 * E : 3 * E, :].T
            for i in range(blocks)[::-1]:
                j0, js = spans(i)
                cols = slice(i * B, (i + 1) * B)
                half = slice((i % 2) * B, (i % 2 + 1) * B)
                hs = pl.ds(pl.multiple_of(h * E, E), E)
                qT, doT = qh[h, 0:E, cols], do_ref[i // 2, hs, half]
                low, L = low_ref[0:1, cols], L_ref[h, 0:1, cols]
                D = jnp.sum(doT.astype(f32) * o_ref[i // 2, hs, half].astype(f32), axis=0, keepdims=True)
                dq = jnp.zeros((E, B), f32)

                def front(j):
                    ks = slice(j * B, (j + 1) * B)
                    return nn(kn[ks, :], qT), nn(vn[ks, :], doT)

                queue = [front(j) for j in js[:2]]
                for n, j in enumerate(js):
                    ks = slice(j * B, (j + 1) * B)
                    if n + 2 < len(js):
                        queue.append(front(js[n + 2]))
                    s, dp_ = queue.pop(0)
                    p = jnp.exp2(s * (SCALE * LOG2E) - L)
                    if masked(i, j, blocks):
                        p = keep(i, j, low, p, 0.0)
                    ds = (p * (dp_ - D)).astype(bf)
                    dvj, dkj = nt(doT, p.astype(bf)), nt(qT, ds)
                    if i == min(blocks - 1, j + WINDOW // B):
                        dv[:, ks] = dvj
                        dk[:, ks] = dkj
                    else:
                        dv[:, ks] += dvj
                        dk[:, ks] += dkj
                    dq = dq + nn(qh[h, E : 2 * E, ks], ds)
                qh[h, 0:E, cols] = (dq * SCALE).astype(bf)
                qh[h, E : 2 * E, cols] = (dk[:, cols] * SCALE).astype(bf)
                qh[h, 2 * E : 3 * E, cols] = dv[:, cols].astype(bf)
                for k in range(heads):
                    for act in events.get((k, i), ()):
                        pl.when(h == k)(act)
                if i == 4:
                    pl.when(h > 0)(lambda: one_z(h - 1))
                if i % 2 == 0:

                    @pl.when(h == heads - 1)
                    def _():
                        rows_first(i // 2)
                        if i // 2 < 3:
                            rows_second(i // 2 + 1)

            g = nn(qh[h], n1[...]).T.astype(bf).reshape(2 * NZ, part, 3 * E)
            G1[h, :, :, 0 : 3 * E] = g
            G1[h, :, :, 3 * E :] = jnp.zeros((2 * NZ, part, 256 - 3 * E), bf)
            one_y(h)
            return carry

        lax.fori_loop(0, heads, head, 0)
        rows_second(0)

    for k in range(2):
        got = X4.at[near_t, pl.ds(k * half, half)]
        lanes.copy("cx", k, got, got, C_).wait_send()
    for there in (core_t, near_t, cross_t):
        lanes.arrived("do", there, do_ref.at[there], (dp, there))
    pl.run_scoped(
        backward, pltpu.VMEM((total, E), bf), pltpu.VMEM((total, E), bf), pltpu.VMEM((E, total), f32), pltpu.VMEM((E, total), f32)
    )
    third(2)
    one_z(heads - 1)
    last()
    w1v = W1[dp].astype(f32)
    sums = [one_last(h) for h in range(heads + 1)]
    gain1 = sum(
        jnp.sum(sums[h][:, 0 : 3 * E] * w1v[:, h * 3 * E : (h + 1) * 3 * E], axis=1, keepdims=True) for h in range(heads)
    ) / w1v[:, heads * 3 * E : heads * 3 * E + 1]
    gain2 = sum(
        jnp.sum(g2s[:, u * UNIT : u * UNIT + HB] * wh[:, u * HB : (u + 1) * HB].astype(f32), axis=1, keepdims=True)
        for u in range(units)
    ) / w1v[:, heads * 3 * E + 1 : heads * 3 * E + 2]
    both_ = jnp.concatenate([gain1, gain2, jnp.zeros((part, 126), f32)], axis=1)
    gs[...] = jnp.concatenate([both_, jnp.zeros((128 - part, 128), f32)], axis=0).T[0:8]
    for k, there in enumerate((X_, C_, XC_)):
        lanes.start("g", k, lambda k=k: (gs, gr.at[k]), there)
    gain = W1T[heads * 3 * E : heads * 3 * E + 16, :].astype(f32)[0:1]
    lanes.arrived("d2", 0, R2, X_)
    dn1 = X4[t].astype(f32) + R2[...].astype(f32)
    gin[...] = (x1[...] + norm_pull(xo[...].astype(f32), gain, dn1)).astype(bf)
    for k, there in enumerate((X_, C_, XC_)):
        lanes.arrived("g", k, gr.at[k], there)
    gains[...] = gs[...] + gr[0] + gr[1] + gr[2]
    for xs in range(2):
        for u in range(units):
            lanes.copy("ra", xs * units + u, G5.at[xs, :, 1 - y, :, first_route(u)], RA.at[xs, :, :, first_route(u)], Y_).wait_send()
    lanes.copy("rb", 0, G5.at[1 - x, :, :, :, other_route], RB, X_).wait_send()
    lanes.copy("rb2", 0, G5.at[x, :, 1 - y, :, other_route], RB2, Y_).wait_send()
    for u in range(units):
        lanes.copy("ra2", u, G5.at[1 - x, :, y, :, first_route(u)], RA2.at[:, :, first_route(u)], X_).wait_send()
        for step in range(1, NZ):
            zi = lax.rem(z + step, NZ)
            lanes.copy("z2", u * 3 + step - 1, G5.at[x, zi, y, :, unit(u)], RZ2.at[step - 1, :, unit(u)], far[step]).wait_send()
    for h in range(heads + 1):
        for zi in range(NZ):
            lanes.copy("y1", h * 4 + zi, G1.at[h, zi * 2 + 1 - y], RY.at[h, zi], Y_).wait_send()
        for step in range(1, NZ):
            zi = lax.rem(z + step, NZ)
            lanes.copy("z1", h * 3 + step - 1, G1.at[h, zi * 2 + y], RZ.at[h, step - 1], far[step]).wait_send()
    for r in range(4):
        xr, cr = r // 2, r % 2
        pl.when(c != cr)(lambda: lanes.copy("d1", xr, X4.at[r], R1.at[xr], C_).wait_send())
        pl.when(jnp.logical_and(c == cr, x != xr))(lambda: lanes.copy("d2", 0, X4.at[r], R2, X_).wait_send())
    lanes.finish()


VM = pl.BlockSpec(memory_space=pltpu.VMEM)


def unpack_kernel(gin, result, g1s, g2s, gains, o_result, o_gin, gq, gk, gv, go, gh, gb, gg1, gg2):
    o_result[...] = result[...]
    o_gin[...] = gin[...]
    heads = gq.shape[1] // E
    for h in range(heads):
        base = h * 256
        for k, out in enumerate((gq, gk, gv)):
            out[:, h * E : (h + 1) * E] = g1s[:, base + k * E : base + (k + 1) * E]
    go[...] = g1s[:, heads * 256 : (heads + 1) * 256].T[0 : go.shape[0]]
    units = gh.shape[1] // HB
    for u in range(units):
        gh[:, u * HB : (u + 1) * HB] = g2s[:, u * UNIT : u * UNIT + HB]
        gb[u * HB : (u + 1) * HB, :] = g2s[:, u * UNIT + HB : (u + 1) * UNIT].T
    gg1[...] = gains[0:1, :]
    gg2[...] = gains[1:2, :]


def block(inputs, segments, w_query, w_key, w_value, w_output, w_hidden, w_back, gain_one, gain_two, cotangent):
    rows, dm = inputs.shape
    total = segments.shape[0]
    part, width = w_query.shape
    heads = width // E
    ff = w_hidden.shape[1]
    units = ff // HB
    s, v = jax.ShapeDtypeStruct, pltpu.VMEM
    first = (units - 1) * UNIT + HB
    gin, result, g1s, g2s, gains = pl.pallas_call(
        kernel,
        out_shape=(
            s((rows, dm), bf), s((rows, dm), bf), s((part, (heads + 1) * 256), f32), s((part, 2 * ff), f32), s((8, 128), f32),
        ),
        in_specs=[VM] * 11,
        out_specs=(VM,) * 5,
        scratch_shapes=[
            v((4, rows, dm), bf), v((total, dm), bf), v((2 * NZ, part, 640), bf), v((640, dm), bf),
            v((2, NZ, 2, part, 2 * ff), bf), v((2, NZ, 2, part, 2 * ff), bf), v((4, NZ, 2, part, 256), bf),
            v((heads, 3 * E, total), bf), v((4, width, rows), bf), v((4, width, rows), bf),
            v((heads, 8, total), f32), v((8, total), jnp.int32), v((2 * rows, dm), bf), v((2 * rows, dm), bf), v((rows, dm), f32),
            v((rows, dm), bf), v((rows, dm), bf), v((4, width, rows), bf), v((4, width, rows), bf),
            v((4, dm, 256), bf), v((2, dm, 256), bf), v((dm, 256), bf), v((2, rows, dm), bf), v((rows, dm), bf),
            v((heads + 1, 2 * NZ, part, 256), bf), v((heads + 1, NZ, part, 256), bf), v((heads + 1, 3, part, 256), bf),
            v((2, NZ, part, first), bf), v((NZ, 2, part, HB), bf), v((NZ, part, first), bf), v((NZ, part, HB), bf),
            v((3, part, 2 * ff), bf), v((8, 128), f32), v((3, 8, 128), f32),
            pltpu.SemaphoreType.DMA((144,)), pltpu.SemaphoreType.DMA((144,)),
        ],
        compiler_params=pltpu.CompilerParams(collective_id=1, has_side_effects=True, vmem_limit_bytes=63 * 2**20),
    )(
        inputs, cotangent, segments.reshape(1, total), w_query, w_key, w_value, w_output, w_hidden, w_back,
        gain_one.reshape(1, part), gain_two.reshape(1, part),
    )
    outs = pl.pallas_call(
        unpack_kernel,
        out_shape=(
            s((rows, dm), bf), s((rows, dm), bf), s((part, width), f32), s((part, width), f32), s((part, width), f32),
            s((width, part), f32), s((part, ff), f32), s((ff, part), f32), s((1, 128), f32), s((1, 128), f32),
        ),
        in_specs=[VM] * 5,
        out_specs=(VM,) * 10,
    )(gin, result, g1s, g2s, gains)
    mine = lax.axis_index("tensor") * (part // 4)
    return (*outs[:8], *(lax.dynamic_slice(g, (0, mine), (1, part // 4)).reshape(part // 4) for g in outs[8:]))


def normed(value, gain):
    return value * lax.rsqrt(jnp.mean(value * value, axis=-1, keepdims=True) + 1e-05) * gain


def gelu_local(value):
    return jax.nn.gelu(value, approximate=True)


def scores_for(query_block, key_rows, segment_ids, block_start, block_rows):
    positions = jnp.arange(key_rows.shape[0], dtype=jnp.int32)
    query_pos = block_start + jnp.arange(block_rows, dtype=jnp.int32)
    query_seg = lax.dynamic_slice_in_dim(segment_ids, block_start, block_rows)
    scores = jnp.einsum(
        "qhe,khe->hqk", query_block, key_rows, preferred_element_type=jnp.float32
    ) * E ** (-0.5)
    distance = query_pos[:, None] - positions[None, :]
    allowed = (query_seg[:, None] == segment_ids[None, :]) & (distance >= 0) & (distance < WINDOW)
    return jnp.where(allowed[None], scores, -1e30)


def shards(
    inputs,
    segments,
    w_query,
    w_key,
    w_value,
    w_output,
    w_hidden,
    w_back,
    gain_one,
    gain_two,
    cotangent,
):
    owned = (w_query, w_key, w_value, w_output, w_hidden, w_back, gain_one, gain_two)
    gathered = (
        lax.all_gather(owned[0], "dp", axis=0, tiled=True),
        lax.all_gather(owned[1], "dp", axis=0, tiled=True),
        lax.all_gather(owned[2], "dp", axis=0, tiled=True),
        lax.all_gather(owned[3], "dp", axis=1, tiled=True),
        lax.all_gather(owned[4], "dp", axis=0, tiled=True),
        lax.all_gather(owned[5], "dp", axis=1, tiled=True),
        lax.all_gather(owned[6], "dp", axis=0, tiled=True),
        lax.all_gather(owned[7], "dp", axis=0, tiled=True),
    )
    total_rows = segments.shape[0]
    block_rows = min(512, total_rows)
    blocks = total_rows // block_rows
    width = gathered[0].shape[1]
    heads_here = width // E
    scale = E ** (-0.5)
    starts = jnp.arange(blocks, dtype=jnp.int32) * block_rows
    w_joined = jnp.concatenate([gathered[0], gathered[1], gathered[2]], axis=1)
    gain_first = gathered[6].astype(jnp.float32)
    gain_second = gathered[7].astype(jnp.float32)
    inputs_f = inputs.astype(jnp.float32)
    normed_one = normed(inputs_f, gain_first).astype(jnp.bfloat16)
    full_one = lax.all_gather(normed_one, "tensor", axis=0, tiled=True)
    joined = jnp.dot(full_one, w_joined, preferred_element_type=jnp.float32).astype(jnp.bfloat16)
    query_rows = joined[:, :width].reshape(total_rows, heads_here, E)
    key_rows = joined[:, width : 2 * width].reshape(total_rows, heads_here, E)
    value_rows = joined[:, 2 * width :].reshape(total_rows, heads_here, E)
    query_blocks = query_rows.reshape(blocks, block_rows, heads_here, E)

    def forward_block(packed):
        query_block, block_start = packed
        scores = scores_for(query_block, key_rows, segments, block_start, block_rows)
        row_top = jnp.max(scores, axis=-1, keepdims=True)
        weights_exp = jnp.exp(scores - row_top)
        totals = jnp.sum(weights_exp, axis=-1, keepdims=True)
        probability = (weights_exp / totals).astype(jnp.bfloat16)
        attended_block = jnp.einsum(
            "hqk,khe->qhe", probability, value_rows, preferred_element_type=jnp.float32
        )
        return (attended_block.astype(jnp.bfloat16), (row_top + jnp.log(totals))[..., 0])

    attended, log_sums = lax.map(forward_block, (query_blocks, starts))
    attended = attended.reshape(total_rows, width)
    w_out_full = gathered[3]
    own_attended = lax.all_to_all(attended, "tensor", split_axis=0, concat_axis=1, tiled=True)
    w_out_all = lax.all_gather(w_out_full, "tensor", axis=0, tiled=True)
    attn_branch = jnp.dot(own_attended, w_out_all, preferred_element_type=jnp.float32)
    middle = inputs_f + attn_branch
    normed_two = normed(middle, gain_second).astype(jnp.bfloat16)
    full_two = lax.all_gather(normed_two, "tensor", axis=0, tiled=True)
    hidden = jnp.dot(full_two, gathered[4], preferred_element_type=jnp.float32)
    active = gelu_local(hidden).astype(jnp.bfloat16)
    w_back_full = gathered[5]
    result = middle + lax.psum_scatter(
        jnp.dot(active, w_back_full, preferred_element_type=jnp.float32).astype(jnp.bfloat16),
        "tensor",
        scatter_dimension=0,
        tiled=True,
    ).astype(jnp.float32)
    gathered = (
        lax.all_gather(owned[0], "dp", axis=0, tiled=True),
        lax.all_gather(owned[1], "dp", axis=0, tiled=True),
        lax.all_gather(owned[2], "dp", axis=0, tiled=True),
        lax.all_gather(owned[3], "dp", axis=1, tiled=True),
        lax.all_gather(owned[4], "dp", axis=0, tiled=True),
        lax.all_gather(owned[5], "dp", axis=1, tiled=True),
        lax.all_gather(owned[6], "dp", axis=0, tiled=True),
        lax.all_gather(owned[7], "dp", axis=0, tiled=True),
    )
    w_joined = jnp.concatenate([gathered[0], gathered[1], gathered[2]], axis=1)
    grad_out = cotangent.astype(jnp.float32)
    full_grad = lax.all_gather(cotangent, "tensor", axis=0, tiled=True)
    grad_w_back = jnp.einsum("rf,rd->fd", active, full_grad, preferred_element_type=jnp.float32)
    grad_active = jnp.einsum(
        "rd,fd->rf", full_grad, gathered[5], preferred_element_type=jnp.float32
    )
    gelu_pull = jax.vjp(gelu_local, hidden)[1]
    grad_hidden_rows = gelu_pull(grad_active)[0].astype(jnp.bfloat16)
    grad_w_hidden = jnp.einsum(
        "rd,rf->df", full_two, grad_hidden_rows, preferred_element_type=jnp.float32
    )
    w_hidden_full = gathered[4]
    piece = grad_hidden_rows
    grad_normed_two = lax.psum_scatter(
        jnp.einsum("rf,df->rd", piece, w_hidden_full, preferred_element_type=jnp.float32).astype(
            jnp.bfloat16
        ),
        "tensor",
        scatter_dimension=0,
        tiled=True,
    ).astype(jnp.float32)
    second_pull = jax.vjp(normed, middle, gain_second)[1]
    grad_mid_norm, grad_second = second_pull(grad_normed_two)
    grad_middle = grad_out + grad_mid_norm
    full_middle = lax.all_gather(grad_middle.astype(jnp.bfloat16), "tensor", axis=0, tiled=True)
    grad_w_output = jnp.einsum(
        "rh,rd->hd", attended, full_middle, preferred_element_type=jnp.float32
    )
    grad_attended = jnp.einsum(
        "rd,hd->rh", full_middle, gathered[3], preferred_element_type=jnp.float32
    ).astype(jnp.bfloat16)

    def backward_block(carry, packed):
        grad_keys, grad_values = carry
        query_block, grad_block, log_block, block_start = packed
        scores = scores_for(query_block, key_rows, segments, block_start, block_rows)
        probability = jnp.exp(scores - log_block[..., None])
        grad_values = grad_values + jnp.einsum(
            "hqk,qhe->khe",
            probability.astype(jnp.bfloat16),
            grad_block,
            preferred_element_type=jnp.float32,
        )
        grad_probs = jnp.einsum(
            "qhe,khe->hqk", grad_block, value_rows, preferred_element_type=jnp.float32
        )
        delta_rows = jnp.sum(grad_probs * probability, axis=-1, keepdims=True)
        grad_scores = (probability * (grad_probs - delta_rows)).astype(jnp.bfloat16)
        grad_query_block = (
            jnp.einsum("hqk,khe->qhe", grad_scores, key_rows, preferred_element_type=jnp.float32)
            * scale
        )
        grad_keys = (
            grad_keys
            + jnp.einsum(
                "hqk,qhe->khe", grad_scores, query_block, preferred_element_type=jnp.float32
            )
            * scale
        )
        return ((grad_keys, grad_values), grad_query_block)

    zero_state = jnp.zeros((total_rows, heads_here, E), jnp.float32)
    grad_blocks = grad_attended.reshape(blocks, block_rows, heads_here, E)
    (grad_keys, grad_values), grad_queries = lax.scan(
        backward_block, (zero_state, zero_state), (query_blocks, grad_blocks, log_sums, starts)
    )
    grad_joined = jnp.concatenate(
        [
            grad_queries.reshape(total_rows, width),
            grad_keys.reshape(total_rows, width),
            grad_values.reshape(total_rows, width),
        ],
        axis=1,
    ).astype(jnp.bfloat16)
    grad_w_joined = jnp.einsum(
        "rd,rc->dc", full_one, grad_joined, preferred_element_type=jnp.float32
    )
    piece = grad_joined
    grad_normed_one = lax.psum_scatter(
        jnp.einsum("rc,dc->rd", piece, w_joined, preferred_element_type=jnp.float32).astype(
            jnp.bfloat16
        ),
        "tensor",
        scatter_dimension=0,
        tiled=True,
    ).astype(jnp.float32)
    first_pull = jax.vjp(normed, inputs_f, gain_first)[1]
    grad_in_norm, grad_first = first_pull(grad_normed_one)
    grad_inputs = grad_middle + grad_in_norm
    weight_sums = (
        lax.psum_scatter(grad_w_joined[:, :width], "dp", scatter_dimension=0, tiled=True),
        lax.psum_scatter(
            grad_w_joined[:, width : 2 * width], "dp", scatter_dimension=0, tiled=True
        ),
        lax.psum_scatter(grad_w_joined[:, 2 * width :], "dp", scatter_dimension=0, tiled=True),
        lax.psum_scatter(grad_w_output, "dp", scatter_dimension=1, tiled=True),
        lax.psum_scatter(grad_w_hidden, "dp", scatter_dimension=0, tiled=True),
        lax.psum_scatter(grad_w_back, "dp", scatter_dimension=1, tiled=True),
    )
    gain_sums = (
        lax.psum_scatter(grad_first, ("dp", "tensor"), scatter_dimension=0, tiled=True),
        lax.psum_scatter(grad_second, ("dp", "tensor"), scatter_dimension=0, tiled=True),
    )
    return (
        result.astype(jnp.bfloat16),
        grad_inputs.astype(jnp.bfloat16),
        weight_sums[0],
        weight_sums[1],
        weight_sums[2],
        weight_sums[3],
        weight_sums[4],
        weight_sums[5],
        gain_sums[0],
        gain_sums[1],
    )


def solution(mesh):
    rows, cols = P(("dp", "tensor"), None), P("dp", "tensor")
    turned, part = P("tensor", "dp"), P("dp")
    in_specs = (rows, part, cols, cols, cols, turned, cols, turned, part, part, rows)
    out_specs = (rows, rows, cols, cols, cols, turned, cols, turned, P(("dp", "tensor")), P(("dp", "tensor")))
    here = mesh.shape["dp"] == 2 * NZ and mesh.shape["tensor"] == 4
    body = block if here else shards
    return jax.shard_map(body, mesh=mesh, in_specs=in_specs, out_specs=out_specs, check_vma=False)
```

```python
import functools

import jax
import jax.numpy as jnp
from jax import lax
from jax.experimental import pallas as pl
from jax.experimental.pallas import tpu as pltpu
from jax.sharding import PartitionSpec as P

MESH = pl.DeviceIdType.MESH
f32, bf = jnp.float32, jnp.bfloat16
E = 64
WINDOW = 1536
B = 256
LOG2E = 1.4426950408889634
SCALE = E**-0.5
FILL = -1e30
NZ = 4
HB = 256
UNIT = 2 * HB


def nn(a, b):
    return lax.dot_general(a, b, (((1,), (0,)), ((), ())), preferred_element_type=f32)


def nt(a, b):
    return lax.dot_general(a, b, (((1,), (1,)), ((), ())), preferred_element_type=f32)


def tn(a, b):
    return lax.dot_general(a, b, (((0,), (0,)), ((), ())), preferred_element_type=f32)


class Place:
    def __init__(self):
        self.dp = lax.axis_index("dp")
        self.t = lax.axis_index("tensor")
        self.z, self.y = lax.div(self.dp, 2), lax.rem(self.dp, 2)
        self.x, self.c = lax.div(self.t, 2), lax.rem(self.t, 2)
        self.left, self.right = self.at(z=self.z - 1), self.at(z=self.z + 1)
        self.sides = [sides(self, rnd) for rnd in range(NZ)]

    def at(self, z=None, y=None, x=None, c=None):
        z = self.z if z is None else z
        y = self.y if y is None else y
        x = self.x if x is None else x
        c = self.c if c is None else c
        return (z * 2 + y, x * 2 + c)

    def greet(self, far_z):
        barrier = pltpu.get_barrier_semaphore()
        x, y, z, c = self.x, self.y, self.z, self.c
        near = [self.at(y=1 - y), self.at(x=1 - x), self.at(c=1 - c), self.at(x=1 - x, c=1 - c)]
        for there in near:
            pl.semaphore_signal(barrier, inc=1, device_id=there, device_id_type=MESH)
        for step in range(1, NZ):
            pl.semaphore_signal(
                barrier, inc=1, device_id=self.at(z=lax.rem(z + step, NZ)), device_id_type=MESH
            )
        pl.semaphore_wait(barrier, len(near) + NZ - 1)


class Lanes:
    def __init__(self, send, recv):
        self.send, self.recv, self.n, self.base, self.late = send, recv, 0, {}, []

    def block(self, name, count):
        self.base[name] = self.n
        self.n += count

    def copy(self, name, k, src, dst, there, land=None):
        i = self.base[name]
        return pltpu.make_async_remote_copy(
            src_ref=src,
            dst_ref=dst,
            send_sem=self.send.at[i + k],
            recv_sem=self.recv.at[i + (k if land is None else land)],
            device_id=there,
            device_id_type=MESH,
        )

    def start(self, name, k, ends, there, when=None):
        at = k if callable(k) else lambda: k
        self.copy(name, at(), *ends(), there).start()

        def finish():
            self.copy(name, at(), *ends(), there).wait_send()

        self.late.append((finish, when))

    def start_at(self, name, k, src, dst, there):
        self.copy(name, k, src, dst, there).start()

    def arrived(self, name, k, dst, there):
        self.copy(name, k, dst, dst, there).wait_recv()

    def finish(self):
        for act, when in self.late:
            if when is None:
                act()
            else:
                pl.when(when())(act)


def sides(me, rnd):
    z = me.z
    if rnd == 0:
        return [(z, None, None)]
    return [(z - rnd, True, lambda: z >= rnd), (z + rnd, False, lambda: z + rnd < NZ)]


def line_round(me, lanes, name, rnd, ref_of, arrive):
    z = me.z
    left, right = me.left, me.right

    def go(zi, to_right, when):
        def side():
            return z < NZ - 1 if to_right else z > 0

        def whole():
            return side() if when is None else jnp.logical_and(when(), side())

        lane, there = name + ("R" if to_right else "L"), right if to_right else left

        def copy():
            return lanes.copy(lane, zi, ref_of(zi), ref_of(zi), there)

        pl.when(side())(lambda: copy().start())
        lanes.late.append((lambda: copy().wait_send(), whole))

    for zi, from_left, ok in me.sides[rnd]:
        if rnd == 0:
            go(zi, True, None)
            go(zi, False, None)
            arrive(zi, None)
            continue

        @pl.when(ok())
        def _(zi=zi, from_left=from_left, ok=ok):
            lanes.arrived(name + ("R" if from_left else "L"), zi, ref_of(zi), left if from_left else right)
            go(zi, from_left, ok)
            arrive(zi, ok)


def masked(i, j, blocks):
    return j == i or j == 0 or i >= blocks - 2 or i - j >= WINDOW // B


def keep(i, j, low, value, fill):
    key_pos = lax.broadcasted_iota(jnp.int32, value.shape, 0) + j * B
    ok = key_pos >= low
    if i == j:
        ok = ok & (key_pos <= lax.broadcasted_iota(jnp.int32, value.shape, 1) + i * B)
    return jnp.where(ok, value, fill)


def spans(i):
    first = max(0, i - WINDOW // B)
    return first, list(range(first, i + 1))


def score_pass(i, h, slot, blocks, kn, qh, low_ref, S):
    j0, js = spans(i)
    cols = slice(i * B, (i + 1) * B)
    qT = qh[h, 0:E, cols]
    low = low_ref[0:1, cols]
    top = jnp.full((1, B), FILL, f32)
    for j in js:
        s = nn(kn[h, j * B : (j + 1) * B, :], qT)
        if masked(i, j, blocks):
            s = keep(i, j, low, s, FILL)
        S[slot, (j - j0) * B : (j - j0 + 1) * B, :] = s
        top = jnp.maximum(top, jnp.max(s, axis=0, keepdims=True))
    return top * (SCALE * LOG2E)


def value_pass(i, h, slot, top, qh, S, o_ref, L_ref):
    j0, js = spans(i)
    total = jnp.zeros((1, B), f32)
    out = jnp.zeros((E, B), f32)
    for j in js:
        p = jnp.exp2(S[slot, (j - j0) * B : (j - j0 + 1) * B, :] * (SCALE * LOG2E) - top)
        total = total + jnp.sum(p, axis=0, keepdims=True)
        out = out + nn(qh[h, 2 * E : 3 * E, j * B : (j + 1) * B], p.astype(bf))
    half = i % 2
    o_ref[i // 2, pl.ds(pl.multiple_of(h * E, E), E), half * B : (half + 1) * B] = (out / total).astype(bf)
    L_ref[h, :, i * B : (i + 1) * B] = jnp.broadcast_to(top + jnp.log2(total), (8, B))


def lows(seg, total):
    pos = lax.broadcasted_iota(jnp.int32, (1, total), 1)
    low = jnp.maximum(pos - (WINDOW - 1), 0)
    first = seg[0:1, 0:1]
    for d in range(1, 5):
        begin = jnp.sum((seg < first + d).astype(f32), axis=1, keepdims=True).astype(jnp.int32)
        low = jnp.where(seg >= first + d, jnp.maximum(low, begin), low)
    return low


def pack(v):
    n = v.shape[-2] // 2
    tail = v[..., 128:192]
    return jnp.concatenate([v[..., 0:128], jnp.concatenate([tail[..., 0:n, :], tail[..., n:, :]], axis=-1)], axis=-2)


def unpack(v):
    n = v.shape[-2] // 3
    low = v[..., 2 * n :, :]
    return jnp.concatenate([v[..., 0 : 2 * n, :], jnp.concatenate([low[..., 0:64], low[..., 64:]], axis=-2)], axis=-1)


def gelu_and_slope(u):
    root = 0.7978845608028654
    square = u * u
    th = jnp.tanh(u * (root + (root * 0.044715) * square))
    half = 0.5 + 0.5 * th
    slope = half + (0.5 * u) * (1.0 - th * th) * (root + (3.0 * root * 0.044715) * square)
    return u * half, slope


def norm_pull(value, gain, grad):
    inv = lax.rsqrt(jnp.mean(value * value, axis=-1, keepdims=True) + 1e-05)
    scaled = grad * gain
    return inv * scaled - value * (inv * inv * inv * jnp.mean(value * scaled, axis=-1, keepdims=True))


def kernel(xo, cot, seg, wq, wk, wv, wo, wh, wb, g1, g2,
           gin, result, g1s, g2s, gains,
           X4, n1, W1, W1T, W5, G5, WO, qh, o_ref, oin, L_ref, low_ref, cb, n2b, x1, rdn, rres, dsend, do_ref,
           gws, gwr, gwx, R1, R2, G1, RY, RZ, RA, RA2, RZ2, RC, RX, RYc, gs, gr, send, recv):
    me = Place()
    dp, t, x, y, z, c = me.dp, me.t, me.x, me.y, me.z, me.c
    rows, dm = xo.shape
    total = n1.shape[0]
    blocks = total // B
    heads = qh.shape[0]
    part, width = wq.shape
    ff = wh.shape[1]
    units = ff // HB
    routed = 2 * ff - HB
    X_, Y_, C_, XC_ = me.at(x=1 - x), me.at(y=1 - y), me.at(c=1 - c), me.at(x=1 - x, c=1 - c)
    far = [None] + [me.at(z=lax.rem(z + step, NZ)) for step in range(1, NZ)]
    near_t, cross_t, core_t = (1 - x) * 2 + c, (1 - x) * 2 + 1 - c, x * 2 + 1 - c
    lanes = Lanes(send, recv)
    for name, count in (
        ("aR", 4), ("aL", 4), ("ay", 4), ("x", 2), ("cx", 2), ("co", 1), ("cc", 1),
        ("wz", 3), ("wy", 1), ("wx", 1), ("wc", 2),
        ("bz", 3 * units), ("by", 3 * units), ("bo", 1), ("bx", units), ("bxy", units), ("o", 4),
        ("fy", 1), ("fx", 1), ("fz", 3), ("hz", 3), ("hx", 1), ("hy", 1),
        ("n2", 1), ("dn", 1), ("rs", 1), ("gw", 1), ("gx", 1), ("do", 4),
        ("ra", 2 * units), ("ra2", units), ("z2", 3 * units),
        ("d1", 2), ("d2", 1), ("y1", 4 * (heads + 1)), ("z1", 3 * (heads + 1)), ("g", 3),
    ):
        lanes.block(name, count)

    def unit(u):
        return pl.ds(u * UNIT, UNIT if u < units - 1 else HB)

    rest = pl.ds((units - 1) * UNIT + HB, HB)

    me.greet(True)
    half = rows // 2
    for k in range(2):
        lanes.start("x", k, lambda k=k: (xo.at[pl.ds(k * half, half)], X4.at[t, pl.ds(k * half, half)]), X_)
    zeros = jnp.zeros((part, 56), f32)
    both_gains = jnp.concatenate([g1[...].astype(f32), g2[...].astype(f32), jnp.zeros((6, part), f32)], axis=0)
    both_gains = jnp.concatenate([both_gains, jnp.zeros((8, 128 - part), f32)], axis=1).T[0:part]
    pieces = []
    for h in range(heads):
        for w in (wq, wk, wv):
            pieces.append(w[:, h * E : (h + 1) * E])
    pieces.append(jnp.concatenate([both_gains, zeros], axis=1).astype(bf))
    W1[dp] = jnp.concatenate(pieces, axis=1)

    def a_ref(zi):
        return W1.at[zi * 2 + y]

    def a_arrive(zi, when):
        lanes.start("ay", zi, lambda: (a_ref(zi), a_ref(zi)), Y_, when)

    line_round(me, lanes, "a", 0, a_ref, a_arrive)
    lanes.start("co", 0, lambda: (xo, X4.at[t]), C_)
    lanes.start("cc", 0, lambda: (cot, cb.at[pl.ds(rows, rows)]), C_)
    WO[t, z, y] = pack(wo[...].T)
    back_T = wb[...]
    for u in range(units):
        W5[x, z, y, :, u * UNIT : u * UNIT + HB] = wh[:, u * HB : (u + 1) * HB]
        W5[x, z, y, :, u * UNIT + HB : (u + 1) * UNIT] = back_T[:, u * HB : (u + 1) * HB]
    low_ref[...] = jnp.broadcast_to(lows(seg[...], total), low_ref.shape)
    X4[t] = xo[...]
    cb[0:rows, :] = cot[...]

    def w_z():
        for step in range(1, NZ):
            lanes.start("wz", step - 1, lambda: (WO.at[t, z, y],) * 2, far[step])

    zs = [None] + [lax.rem(z + NZ - step, NZ) for step in range(1, NZ)]

    def from_z(step):
        return lax.rem(z + NZ - step, NZ)

    def w_y():
        for step in range(1, NZ):
            lanes.arrived("wz", step - 1, WO.at[t, from_z(step), y], far[NZ - step])
        lanes.start("wy", 0, lambda: (WO.at[t, :, y],) * 2, Y_)

    def w_x():
        lanes.arrived("wy", 0, WO.at[t, :, 1 - y], Y_)
        lanes.start("wx", 0, lambda: (WO.at[t],) * 2, X_)
        lanes.start("wc", 0, lambda: (WO.at[t],) * 2, C_)

    def w_c():
        lanes.arrived("wx", 0, WO.at[near_t], X_)
        lanes.start("wc", 1, lambda: (WO.at[near_t],) * 2, C_)

    def w_end():
        lanes.arrived("wc", 0, WO.at[core_t], C_)
        lanes.arrived("wc", 1, WO.at[cross_t], C_)

    def b_z(u):
        for step in range(1, NZ):
            lanes.start("bz", u * 3 + step - 1, lambda: (W5.at[x, z, y, :, unit(u)],) * 2, far[step])

    def b_y(u):
        for step in range(1, NZ):
            lanes.arrived("bz", u * 3 + step - 1, W5.at[x, from_z(step), y, :, unit(u)], far[NZ - step])
        for step in range(1, NZ):
            zi = zs[step]
            lanes.start("by", u * 3 + step - 1, lambda zi=zi: (W5.at[x, zi, y, :, unit(u)],) * 2, Y_)

    def b_own():
        lanes.start("bo", 0, lambda: (W5.at[x, z, y, :, pl.ds(0, routed)],) * 2, Y_)

    def b_x(u):
        lanes.start("bx", u, lambda: (W5.at[x, :, y, :, unit(u)],) * 2, X_)

    def b_corner(u):
        lanes.arrived("bx", u, W5.at[1 - x, :, y, :, unit(u)], X_)
        lanes.start("bxy", u, lambda: (W5.at[1 - x, :, y, :, unit(u)],) * 2, Y_)

    def b_near(u):
        for step in range(1, NZ):
            lanes.arrived("by", u * 3 + step - 1, W5.at[x, zs[step], 1 - y, :, unit(u)], Y_)
        if u == 0:
            lanes.arrived("bo", 0, W5.at[x, z, 1 - y, :, pl.ds(0, routed)], Y_)

    def b_end(u):
        lanes.arrived("bxy", u, W5.at[1 - x, :, 1 - y, :, unit(u)], Y_)

    def f_y():
        lanes.start("fy", 0, lambda: (W5.at[x, z, y, :, rest],) * 2, Y_)

    def f_x():
        lanes.arrived("fy", 0, W5.at[x, z, 1 - y, :, rest], Y_)
        lanes.start("fx", 0, lambda: (W5.at[x, z, :, :, rest],) * 2, X_)

    def f_z():
        lanes.arrived("fx", 0, W5.at[1 - x, z, :, :, rest], X_)
        for step in range(1, NZ):
            lanes.start("fz", step - 1, lambda: (W5.at[:, z, :, :, rest],) * 2, far[step])

    def f_end():
        for step in range(1, NZ):
            lanes.arrived("fz", step - 1, W5.at[:, from_z(step), :, :, rest], far[NZ - step])

    def quarter(r, kn, S, events):
        def body(h, carry):
            tops = []
            for i in (2 * r, 2 * r + 1):
                tops.append(score_pass(i, h, i % 2, blocks, kn, qh, low_ref, S))
            for i in (2 * r, 2 * r + 1):
                value_pass(i, h, i % 2, tops[i % 2], qh, S, o_ref, L_ref)
            for k in range(heads):
                if k in events:
                    pl.when(h == k)(lambda: [act() for act in events[k]] and None)
            return carry

        lax.fori_loop(0, heads, body, 0)

        def out_copy():
            return lanes.copy("o", r, o_ref.at[r], oin.at[t], (dp, r), land=t)

        @pl.when(t == r)
        def _():
            oin[t] = o_ref[r]

        pl.when(t != r)(lambda: out_copy().start())
        lanes.late.append((lambda: out_copy().wait_send(), lambda: t != r))

    def forward(kn, S):
        line_round(me, lanes, "a", 1, a_ref, a_arrive)
        line_round(me, lanes, "a", 2, a_ref, a_arrive)
        w_z()
        line_round(me, lanes, "a", 3, a_ref, a_arrive)
        b_z(0)
        b_z(1)
        b_z(2)
        for zi in range(NZ):
            lanes.arrived("ay", zi, W1.at[zi * 2 + 1 - y], Y_)
        w_y()
        f_y()
        b_own()
        W1T[...] = W1[...].reshape(2 * NZ * part, W1.shape[2]).T

        def project(blk):
            base = pl.multiple_of(blk * rows, rows)
            gain = W1T[heads * 3 * E : heads * 3 * E + 16, :].astype(f32)[0:1]
            value = X4[blk].astype(f32)
            inv = lax.rsqrt(jnp.mean(value * value, axis=-1, keepdims=True) + 1e-05)
            normed = (value * inv * gain).astype(bf)
            n1[pl.ds(base, rows), :] = normed
            out = nt(W1T[0 : heads * 3 * E, :], normed).astype(bf)
            for h in range(heads):
                qh[h, :, pl.ds(base, rows)] = out[h * 3 * E : (h + 1) * 3 * E]
                kn[h, pl.ds(base, rows), :] = out[h * 3 * E + E : h * 3 * E + 2 * E].T

        project(t)
        lanes.arrived("co", 0, X4.at[core_t], C_)
        project(core_t)
        for k in range(2):
            got = X4.at[near_t, pl.ds(k * half, half)]
            lanes.arrived("x", k, got, X_)
            lanes.start_at("cx", k, got, got, C_)
        f_x()
        w_x()
        project(near_t)
        b_y(0)
        b_x(0)
        for k in range(2):
            lanes.arrived("cx", k, X4.at[cross_t, pl.ds(k * half, half)], C_)
        project(cross_t)
        f_z()
        quarter(0, kn, S, {})
        b_y(1)
        quarter(1, kn, S, {})
        w_c()
        b_x(1)
        b_y(2)
        quarter(2, kn, S, {})
        b_corner(0)
        quarter(3, kn, S, {})

    pl.run_scoped(forward, pltpu.VMEM((heads, total, E), bf), pltpu.VMEM((2, WINDOW + B, B), f32))

    r_unit = lanes.base["ra"]

    def sum_first(xs, u):
        lanes.start_at("ra", xs * units + u, G5.at[xs, :, 1 - y, :, unit(u)], RA.at[xs, :, :, unit(u)], Y_)

    def middle(wof, n2T, cT, res, dn2):
        w_end()
        for k in range(4):
            wof[k * width : (k + 1) * width, :] = unpack(WO[k].reshape(2 * NZ, 144, 128)).reshape(dm, width).T
        gain = W1T[heads * 3 * E : heads * 3 * E + 16, :].astype(f32)[1:2]
        lanes.arrived("cc", 0, cb.at[pl.ds(rows, rows)], C_)
        cT[...] = cb[...].T
        for there in (near_t, core_t, cross_t):
            lanes.arrived("o", there, oin.at[there], (dp, there))
        b_x(2)
        b_corner(1)
        mid = xo[...].astype(f32) + tn(oin[...].reshape(4 * width, rows), wof[...])
        x1[...] = mid
        inv = lax.rsqrt(jnp.mean(mid * mid, axis=-1, keepdims=True) + 1e-05)
        n2b[0:rows, :] = (mid * inv * gain).astype(bf)
        lanes.copy("n2", 0, n2b.at[pl.ds(0, rows)], n2b.at[pl.ds(rows, rows)], C_).start()
        n2T[:, 0:rows] = n2b[0:rows, :].T
        lanes.arrived("n2", 0, n2b.at[pl.ds(rows, rows)], C_)
        n2T[:, rows:] = n2b[rows:, :].T
        b_near(0)

        def weights(xs, u):
            col = u * UNIT
            return (W5[xs, :, :, :, col + k * HB : col + (k + 1) * HB].reshape(dm, HB) for k in range(2))

        def through(xs, u):
            w_h, w_b = weights(xs, u)
            hid = nn(n2b[...], w_h)
            act, slope = gelu_and_slope(hid)
            act = act.astype(bf)
            du = (nn(cb[...], w_b) * slope).astype(bf)
            return act, du, w_h, w_b

        def grads(xs, u, act, du):
            col = u * UNIT
            G5[xs, :, :, :, col : col + HB] = nn(n2T[...], du).astype(bf).reshape(NZ, 2, part, HB)
            G5[xs, :, :, :, col + HB : col + UNIT] = nn(cT[...], act).astype(bf).reshape(NZ, 2, part, HB)

        for u in range(units):
            if u > 0:
                b_near(u)
            if u == 1:
                b_corner(2)
            if u == units - 1:
                f_end()
            act, du, w_h, w_b = through(x, u)
            if u == 0:
                dn2[...] = nt(du, w_h)
                res[...] = nt(act, w_b)
            else:
                dn2[...] += nt(du, w_h)
                res[...] += nt(act, w_b)
            grads(x, u, act, du)
        for k in range(2):
            got = X4.at[near_t, pl.ds(k * half, half)]
            lanes.copy("cx", k, got, got, C_).wait_send()
        for u in range(units):
            b_end(u)
            if u == 0:
                sum_first(x, 0)
            cols = slice(u * HB, (u + 1) * HB)
            act, du, w_h, w_b = through(1 - x, u)
            dn2[...] += nt(du, w_h)
            if u < 2:
                grads(1 - x, u, act, du)
                sum_first(1 - x, u)
            for k in range(2):
                X4[k, :, cols] = act[k * rows : (k + 1) * rows]
                X4[2 + k, :, cols] = du[k * rows : (k + 1) * rows]

        def kept(k, u):
            return X4[2 * k : 2 * k + 2, :, u * HB : (u + 1) * HB].reshape(2 * rows, HB)

        lanes.copy("n2", 0, n2b.at[pl.ds(0, rows)], n2b.at[pl.ds(rows, rows)], C_).wait_send()
        n2b[0:rows, :] = dn2[rows:, :].astype(bf)
        lanes.start("dn", 0, lambda: (n2b.at[pl.ds(0, rows)], rdn), C_)
        for u in range(units):
            w_h, w_b = weights(1 - x, u)
            res[...] += nt(kept(0, u), w_b)
        n2b[rows:, :] = res[rows:, :].astype(bf)
        lanes.start("rs", 0, lambda: (n2b.at[pl.ds(rows, rows)], rres), C_)
        lanes.arrived("dn", 0, rdn, C_)
        back = cot[...].astype(f32) + norm_pull(x1[...], gain, dn2[0:rows, :] + rdn[...].astype(f32))
        lanes.arrived("rs", 0, rres, C_)
        result[...] = (x1[...] + res[0:rows, :] + rres[...].astype(f32)).astype(bf)
        x1[...] = back
        back = back.astype(bf)
        out = nt(wof[...], back).astype(bf)
        for r in range(4):
            dsend[r] = out[r * width : (r + 1) * width]

            def to_owner(r=r):
                return lanes.copy("do", r, dsend.at[r], do_ref.at[t], (dp, r), land=t)

            @pl.when(t == r)
            def _():
                do_ref[t] = dsend[r]

            pl.when(t != r)(lambda: to_owner().start())
            lanes.late.append((lambda r=r, f=to_owner: f(r).wait_send(), lambda r=r: t != r))
        for u in range(units):
            if u == 2:
                grads(1 - x, u, kept(0, u), kept(1, u))
                sum_first(1 - x, u)
        for step in range(1, NZ):
            zi = lax.rem(z + step, NZ)
            lanes.start_at("hz", step - 1, G5.at[:, zi, :, :, rest], RC.at[step - 1], far[step])
        gw = nt(back.T, oin[...].reshape(4 * width, rows)).astype(bf)
        quarters = [pack(gw[:, k * width : (k + 1) * width].reshape(2 * NZ, part, width)) for k in range(4)]
        for xs in range(2):
            even, odd = quarters[2 * xs], quarters[2 * xs + 1]
            gws[xs] = jnp.where(c == 0, odd, even)
            gws[2 + xs] = jnp.where(c == 0, even, odd)
        lanes.start("gw", 0, lambda: (gws.at[pl.ds(0, 2)], gwr), C_)

    pl.run_scoped(
        middle, pltpu.VMEM((dm, dm), bf), pltpu.VMEM((dm, 2 * rows), bf), pltpu.VMEM((dm, 2 * rows), bf),
        pltpu.VMEM((2 * rows, dm), f32), pltpu.VMEM((2 * rows, dm), f32),
    )

    def w_back_x():
        lanes.arrived("gw", 0, gwr, C_)
        gws[2 + 1 - x] = (gws[2 + 1 - x].astype(f32) + gwr[1 - x].astype(f32)).astype(bf)
        lanes.start("gx", 0, lambda: (gws.at[2 + 1 - x], gwx), X_)
        gws[2 + x] = (gws[2 + x].astype(f32) + gwr[x].astype(f32)).astype(bf)

    def w_back_y():
        lanes.arrived("gx", 0, gwx, X_)
        G1[heads] = (gws[2 + x].astype(f32) + gwx[...].astype(f32)).astype(bf)
        one_y(heads)

    def add(ref_at, *more):
        value = ref_at[...].astype(f32)
        for m in more:
            value = value + m.astype(f32)
        ref_at[...] = value.astype(bf)

    def second(u):
        lanes.arrived("ra", (1 - x) * units + u, RA.at[1 - x, :, :, unit(u)], Y_)
        add(G5.at[1 - x, :, y, :, unit(u)], RA[1 - x, :, :, unit(u)])
        lanes.start_at("ra2", u, G5.at[1 - x, :, y, :, unit(u)], RA2.at[:, :, unit(u)], X_)

    def rest_x():
        for step in range(1, NZ):
            lanes.arrived("hz", step - 1, RC.at[step - 1], far[NZ - step])
        add(G5.at[:, z, :, :, rest], RC[0], RC[1], RC[2])
        lanes.start_at("hx", 0, G5.at[1 - x, z, :, :, rest], RX, X_)

    def rest_y():
        lanes.arrived("hx", 0, RX, X_)
        add(G5.at[x, z, :, :, rest], RX[...])
        lanes.start_at("hy", 0, G5.at[x, z, 1 - y, :, rest], RYc, Y_)

    def third(u):
        lanes.arrived("ra", x * units + u, RA.at[x, :, :, unit(u)], Y_)
        lanes.arrived("ra2", u, RA2.at[:, :, unit(u)], X_)
        add(G5.at[x, :, y, :, unit(u)], RA[x, :, :, unit(u)], RA2[:, :, unit(u)])
        for step in range(1, NZ):
            zi = lax.rem(z + step, NZ)
            lanes.start_at("z2", u * 3 + step - 1, G5.at[x, zi, y, :, unit(u)], RZ2.at[step - 1, :, unit(u)], far[step])

    def last():
        value = G5[x, z, y, :, 0:routed].astype(f32)
        for step in range(1, NZ):
            for u in range(units):
                lanes.arrived("z2", u * 3 + step - 1, RZ2.at[step - 1, :, unit(u)], far[NZ - step])
            value = value + RZ2[step - 1].astype(f32)
        g2s[:, 0:routed] = value
        lanes.arrived("hy", 0, RYc, Y_)
        g2s[:, routed:] = G5[x, z, y, :, routed:].astype(f32) + RYc[...].astype(f32)

    def one_y(h):
        for zi in range(NZ):
            lanes.start_at("y1", h * 4 + zi, G1.at[h, zi * 2 + 1 - y], RY.at[h, zi], Y_)

    def one_z(h):
        for step in range(NZ):
            zi = lax.rem(z + step, NZ)
            lanes.arrived("y1", h * 4 + zi, RY.at[h, zi], Y_)
            G1[h, zi * 2 + y] = (G1[h, zi * 2 + y].astype(f32) + RY[h, zi].astype(f32)).astype(bf)
            if step:
                lanes.start_at("z1", h * 3 + step - 1, G1.at[h, zi * 2 + y], RZ.at[h, step - 1], far[step])

    def one_last(h):
        value = G1[h, dp].astype(f32)
        for step in range(1, NZ):
            lanes.arrived("z1", h * 3 + step - 1, RZ.at[h, step - 1], far[NZ - step])
            value = value + RZ[h, step - 1].astype(f32)
        value = unpack(value)
        g1s[:, h * 256 : h * 256 + 3 * E] = value
        return value

    def backward(kn, vn, dk, dv):
        def rows_first(r):
            xr, cr = r // 2, r % 2
            piece = qh[:, :, r * rows : (r + 1) * rows].reshape(heads * 3 * E, rows)
            X4[r] = tn(piece, W1T[0 : heads * 3 * E, :]).astype(bf)
            pl.when(c != cr)(lambda: lanes.start_at("d1", xr, X4.at[r], R1.at[xr], C_))

        def rows_second(r):
            xr, cr = r // 2, r % 2

            @pl.when(c == cr)
            def _():
                lanes.arrived("d1", xr, R1.at[xr], C_)
                X4[r] = (X4[r].astype(f32) + R1[xr].astype(f32)).astype(bf)
                pl.when(x != xr)(lambda: lanes.start_at("d2", 0, X4.at[r], R2, X_))

        events = {
            (0, 7): [lambda: second(0), lambda: sum_first(x, 1)],
            (0, 5): [lambda: second(1), lambda: sum_first(x, 2)],
            (0, 2): [lambda: second(2), rest_x],
            (1, 7): [lambda: third(0), w_back_x],
            (1, 4): [rest_y],
            (1, 2): [lambda: third(1)],
            (2, 7): [w_back_y],
            (2, 5): [lambda: third(2)],
            (2, 1): [lambda: one_z(heads)],
        }

        def head(h, carry):
            kn[...] = qh[h, E : 2 * E, :].T
            vn[...] = qh[h, 2 * E : 3 * E, :].T
            for i in range(blocks)[::-1]:
                j0, js = spans(i)
                cols = slice(i * B, (i + 1) * B)
                half = slice((i % 2) * B, (i % 2 + 1) * B)
                hs = pl.ds(pl.multiple_of(h * E, E), E)
                qT, doT = qh[h, 0:E, cols], do_ref[i // 2, hs, half]
                low, L = low_ref[0:1, cols], L_ref[h, 0:1, cols]
                D = jnp.sum(doT.astype(f32) * o_ref[i // 2, hs, half].astype(f32), axis=0, keepdims=True)
                dq = jnp.zeros((E, B), f32)

                def front(j):
                    ks = slice(j * B, (j + 1) * B)
                    return nn(kn[ks, :], qT), nn(vn[ks, :], doT)

                queue = [front(j) for j in js[:2]]
                for n, j in enumerate(js):
                    ks = slice(j * B, (j + 1) * B)
                    if n + 2 < len(js):
                        queue.append(front(js[n + 2]))
                    s, dp_ = queue.pop(0)
                    p = jnp.exp2(s * (SCALE * LOG2E) - L)
                    if masked(i, j, blocks):
                        p = keep(i, j, low, p, 0.0)
                    ds = (p * (dp_ - D)).astype(bf)
                    dvj, dkj = nt(doT, p.astype(bf)), nt(qT, ds)
                    if i == min(blocks - 1, j + WINDOW // B):
                        dv[:, ks] = dvj
                        dk[:, ks] = dkj
                    else:
                        dv[:, ks] += dvj
                        dk[:, ks] += dkj
                    dq = dq + nn(qh[h, E : 2 * E, ks], ds)
                qh[h, 0:E, cols] = (dq * SCALE).astype(bf)
                qh[h, E : 2 * E, cols] = (dk[:, cols] * SCALE).astype(bf)
                qh[h, 2 * E : 3 * E, cols] = dv[:, cols].astype(bf)
                for k in range(heads):
                    for act in events.get((k, i), ()):
                        pl.when(h == k)(act)
                if i == 4:
                    pl.when(h > 0)(lambda: one_z(h - 1))
                if i % 2 == 0:

                    @pl.when(h == heads - 1)
                    def _():
                        rows_first(i // 2)
                        if i // 2 < 3:
                            rows_second(i // 2 + 1)

            G1[h] = pack(nn(qh[h], n1[...]).T.astype(bf).reshape(2 * NZ, part, 3 * E))
            one_y(h)
            return carry

        lax.fori_loop(0, heads, head, 0)
        rows_second(0)

    for there in (core_t, near_t, cross_t):
        lanes.arrived("do", there, do_ref.at[there], (dp, there))
    pl.run_scoped(
        backward, pltpu.VMEM((total, E), bf), pltpu.VMEM((total, E), bf), pltpu.VMEM((E, total), f32), pltpu.VMEM((E, total), f32)
    )
    one_z(heads - 1)
    last()
    w1v = W1[dp].astype(f32)
    sums = [one_last(h) for h in range(heads + 1)]
    gain1 = sum(
        jnp.sum(sums[h][:, 0 : 3 * E] * w1v[:, h * 3 * E : (h + 1) * 3 * E], axis=1, keepdims=True) for h in range(heads)
    ) / w1v[:, heads * 3 * E : heads * 3 * E + 1]
    gain2 = sum(
        jnp.sum(g2s[:, u * UNIT : u * UNIT + HB] * wh[:, u * HB : (u + 1) * HB].astype(f32), axis=1, keepdims=True)
        for u in range(units)
    ) / w1v[:, heads * 3 * E + 1 : heads * 3 * E + 2]
    both_ = jnp.concatenate([gain1, gain2, jnp.zeros((part, 126), f32)], axis=1)
    gs[...] = jnp.concatenate([both_, jnp.zeros((128 - part, 128), f32)], axis=0).T[0:8]
    for k, there in enumerate((X_, C_, XC_)):
        lanes.start("g", k, lambda k=k: (gs, gr.at[k]), there)
    gain = W1T[heads * 3 * E : heads * 3 * E + 16, :].astype(f32)[0:1]
    lanes.arrived("d2", 0, R2, X_)
    dn1 = X4[t].astype(f32) + R2[...].astype(f32)
    gin[...] = (x1[...] + norm_pull(xo[...].astype(f32), gain, dn1)).astype(bf)
    for k, there in enumerate((X_, C_, XC_)):
        lanes.arrived("g", k, gr.at[k], there)
    gains[...] = gs[...] + gr[0] + gr[1] + gr[2]
    for xs in range(2):
        for u in range(units):
            lanes.copy("ra", xs * units + u, G5.at[xs, :, 1 - y, :, unit(u)], RA.at[xs, :, :, unit(u)], Y_).wait_send()
    for step in range(1, NZ):
        zi = lax.rem(z + step, NZ)
        lanes.copy("hz", step - 1, G5.at[:, zi, :, :, rest], RC.at[step - 1], far[step]).wait_send()
    lanes.copy("hx", 0, G5.at[1 - x, z, :, :, rest], RX, X_).wait_send()
    lanes.copy("hy", 0, G5.at[x, z, 1 - y, :, rest], RYc, Y_).wait_send()
    for u in range(units):
        lanes.copy("ra2", u, G5.at[1 - x, :, y, :, unit(u)], RA2.at[:, :, unit(u)], X_).wait_send()
        for step in range(1, NZ):
            zi = lax.rem(z + step, NZ)
            lanes.copy("z2", u * 3 + step - 1, G5.at[x, zi, y, :, unit(u)], RZ2.at[step - 1, :, unit(u)], far[step]).wait_send()
    for h in range(heads + 1):
        for zi in range(NZ):
            lanes.copy("y1", h * 4 + zi, G1.at[h, zi * 2 + 1 - y], RY.at[h, zi], Y_).wait_send()
        for step in range(1, NZ):
            zi = lax.rem(z + step, NZ)
            lanes.copy("z1", h * 3 + step - 1, G1.at[h, zi * 2 + y], RZ.at[h, step - 1], far[step]).wait_send()
    for r in range(4):
        xr, cr = r // 2, r % 2
        pl.when(c != cr)(lambda: lanes.copy("d1", xr, X4.at[r], R1.at[xr], C_).wait_send())
        pl.when(jnp.logical_and(c == cr, x != xr))(lambda: lanes.copy("d2", 0, X4.at[r], R2, X_).wait_send())
    lanes.finish()


VM = pl.BlockSpec(memory_space=pltpu.VMEM)


def unpack_kernel(gin, result, g1s, g2s, gains, o_result, o_gin, gq, gk, gv, go, gh, gb, gg1, gg2):
    o_result[...] = result[...]
    o_gin[...] = gin[...]
    heads = gq.shape[1] // E
    for h in range(heads):
        base = h * 256
        for k, out in enumerate((gq, gk, gv)):
            out[:, h * E : (h + 1) * E] = g1s[:, base + k * E : base + (k + 1) * E]
    go[...] = g1s[:, heads * 256 : (heads + 1) * 256].T[0 : go.shape[0]]
    units = gh.shape[1] // HB
    for u in range(units):
        gh[:, u * HB : (u + 1) * HB] = g2s[:, u * UNIT : u * UNIT + HB]
        gb[:, u * HB : (u + 1) * HB] = g2s[:, u * UNIT + HB : (u + 1) * UNIT]
    gg1[...] = gains[0:1, :]
    gg2[...] = gains[1:2, :]


def block(inputs, segments, w_query, w_key, w_value, w_output, w_hidden, w_back, gain_one, gain_two, cotangent):
    rows, dm = inputs.shape
    total = segments.shape[0]
    part, width = w_query.shape
    heads = width // E
    ff = w_hidden.shape[1]
    units = ff // HB
    s, v = jax.ShapeDtypeStruct, pltpu.VMEM
    first = (units - 1) * UNIT + HB
    gin, result, g1s, g2s, gains = pl.pallas_call(
        kernel,
        out_shape=(
            s((rows, dm), bf), s((rows, dm), bf), s((part, (heads + 1) * 256), f32), s((part, 2 * ff), f32), s((8, 128), f32),
        ),
        in_specs=[VM] * 11,
        out_specs=(VM,) * 5,
        scratch_shapes=[
            v((4, rows, dm), bf), v((total, dm), bf), v((2 * NZ, part, 640), bf), v((640, dm), bf),
            v((2, NZ, 2, part, 2 * ff), bf), v((2, NZ, 2, part, 2 * ff), bf), v((4, NZ, 2, 144, 128), bf),
            v((heads, 3 * E, total), bf), v((4, width, rows), bf), v((4, width, rows), bf),
            v((heads, 8, total), f32), v((8, total), jnp.int32), v((2 * rows, dm), bf), v((2 * rows, dm), bf), v((rows, dm), f32),
            v((rows, dm), bf), v((rows, dm), bf), v((4, width, rows), bf), v((4, width, rows), bf),
            v((4, 2 * NZ, 144, 128), bf), v((2, 2 * NZ, 144, 128), bf), v((2 * NZ, 144, 128), bf), v((2, rows, dm), bf), v((rows, dm), bf),
            v((heads + 1, 2 * NZ, 144, 128), bf), v((heads + 1, NZ, 144, 128), bf), v((heads + 1, 3, 144, 128), bf),
            v((2, NZ, part, first), bf), v((NZ, part, first), bf), v((3, part, first), bf),
            v((3, 2, 2, part, HB), bf), v((2, part, HB), bf), v((part, HB), bf), v((8, 128), f32), v((3, 8, 128), f32),
            pltpu.SemaphoreType.DMA((144,)), pltpu.SemaphoreType.DMA((144,)),
        ],
        compiler_params=pltpu.CompilerParams(collective_id=1, has_side_effects=True, vmem_limit_bytes=63 * 2**20),
    )(
        inputs, cotangent, segments.reshape(1, total), w_query, w_key, w_value, w_output, w_hidden, w_back.T,
        gain_one.reshape(1, part), gain_two.reshape(1, part),
    )
    outs = pl.pallas_call(
        unpack_kernel,
        out_shape=(
            s((rows, dm), bf), s((rows, dm), bf), s((part, width), f32), s((part, width), f32), s((part, width), f32),
            s((width, part), f32), s((part, ff), f32), s((part, ff), f32), s((1, 128), f32), s((1, 128), f32),
        ),
        in_specs=[VM] * 5,
        out_specs=(VM,) * 10,
    )(gin, result, g1s, g2s, gains)
    mine = lax.axis_index("tensor") * (part // 4)
    return (*outs[:7], outs[7].T, *(lax.dynamic_slice(g, (0, mine), (1, part // 4)).reshape(part // 4) for g in outs[8:]))


def normed(value, gain):
    return value * lax.rsqrt(jnp.mean(value * value, axis=-1, keepdims=True) + 1e-05) * gain


def gelu_local(value):
    return jax.nn.gelu(value, approximate=True)


def scores_for(query_block, key_rows, segment_ids, block_start, block_rows):
    positions = jnp.arange(key_rows.shape[0], dtype=jnp.int32)
    query_pos = block_start + jnp.arange(block_rows, dtype=jnp.int32)
    query_seg = lax.dynamic_slice_in_dim(segment_ids, block_start, block_rows)
    scores = jnp.einsum(
        "qhe,khe->hqk", query_block, key_rows, preferred_element_type=jnp.float32
    ) * E ** (-0.5)
    distance = query_pos[:, None] - positions[None, :]
    allowed = (query_seg[:, None] == segment_ids[None, :]) & (distance >= 0) & (distance < WINDOW)
    return jnp.where(allowed[None], scores, -1e30)


def shards(
    inputs,
    segments,
    w_query,
    w_key,
    w_value,
    w_output,
    w_hidden,
    w_back,
    gain_one,
    gain_two,
    cotangent,
):
    owned = (w_query, w_key, w_value, w_output, w_hidden, w_back, gain_one, gain_two)
    gathered = (
        lax.all_gather(owned[0], "dp", axis=0, tiled=True),
        lax.all_gather(owned[1], "dp", axis=0, tiled=True),
        lax.all_gather(owned[2], "dp", axis=0, tiled=True),
        lax.all_gather(owned[3], "dp", axis=1, tiled=True),
        lax.all_gather(owned[4], "dp", axis=0, tiled=True),
        lax.all_gather(owned[5], "dp", axis=1, tiled=True),
        lax.all_gather(owned[6], "dp", axis=0, tiled=True),
        lax.all_gather(owned[7], "dp", axis=0, tiled=True),
    )
    total_rows = segments.shape[0]
    block_rows = min(512, total_rows)
    blocks = total_rows // block_rows
    width = gathered[0].shape[1]
    heads_here = width // E
    scale = E ** (-0.5)
    starts = jnp.arange(blocks, dtype=jnp.int32) * block_rows
    w_joined = jnp.concatenate([gathered[0], gathered[1], gathered[2]], axis=1)
    gain_first = gathered[6].astype(jnp.float32)
    gain_second = gathered[7].astype(jnp.float32)
    inputs_f = inputs.astype(jnp.float32)
    normed_one = normed(inputs_f, gain_first).astype(jnp.bfloat16)
    full_one = lax.all_gather(normed_one, "tensor", axis=0, tiled=True)
    joined = jnp.dot(full_one, w_joined, preferred_element_type=jnp.float32).astype(jnp.bfloat16)
    query_rows = joined[:, :width].reshape(total_rows, heads_here, E)
    key_rows = joined[:, width : 2 * width].reshape(total_rows, heads_here, E)
    value_rows = joined[:, 2 * width :].reshape(total_rows, heads_here, E)
    query_blocks = query_rows.reshape(blocks, block_rows, heads_here, E)

    def forward_block(packed):
        query_block, block_start = packed
        scores = scores_for(query_block, key_rows, segments, block_start, block_rows)
        row_top = jnp.max(scores, axis=-1, keepdims=True)
        weights_exp = jnp.exp(scores - row_top)
        totals = jnp.sum(weights_exp, axis=-1, keepdims=True)
        probability = (weights_exp / totals).astype(jnp.bfloat16)
        attended_block = jnp.einsum(
            "hqk,khe->qhe", probability, value_rows, preferred_element_type=jnp.float32
        )
        return (attended_block.astype(jnp.bfloat16), (row_top + jnp.log(totals))[..., 0])

    attended, log_sums = lax.map(forward_block, (query_blocks, starts))
    attended = attended.reshape(total_rows, width)
    w_out_full = gathered[3]
    own_attended = lax.all_to_all(attended, "tensor", split_axis=0, concat_axis=1, tiled=True)
    w_out_all = lax.all_gather(w_out_full, "tensor", axis=0, tiled=True)
    attn_branch = jnp.dot(own_attended, w_out_all, preferred_element_type=jnp.float32)
    middle = inputs_f + attn_branch
    normed_two = normed(middle, gain_second).astype(jnp.bfloat16)
    full_two = lax.all_gather(normed_two, "tensor", axis=0, tiled=True)
    hidden = jnp.dot(full_two, gathered[4], preferred_element_type=jnp.float32)
    active = gelu_local(hidden).astype(jnp.bfloat16)
    w_back_full = gathered[5]
    result = middle + lax.psum_scatter(
        jnp.dot(active, w_back_full, preferred_element_type=jnp.float32).astype(jnp.bfloat16),
        "tensor",
        scatter_dimension=0,
        tiled=True,
    ).astype(jnp.float32)
    gathered = (
        lax.all_gather(owned[0], "dp", axis=0, tiled=True),
        lax.all_gather(owned[1], "dp", axis=0, tiled=True),
        lax.all_gather(owned[2], "dp", axis=0, tiled=True),
        lax.all_gather(owned[3], "dp", axis=1, tiled=True),
        lax.all_gather(owned[4], "dp", axis=0, tiled=True),
        lax.all_gather(owned[5], "dp", axis=1, tiled=True),
        lax.all_gather(owned[6], "dp", axis=0, tiled=True),
        lax.all_gather(owned[7], "dp", axis=0, tiled=True),
    )
    w_joined = jnp.concatenate([gathered[0], gathered[1], gathered[2]], axis=1)
    grad_out = cotangent.astype(jnp.float32)
    full_grad = lax.all_gather(cotangent, "tensor", axis=0, tiled=True)
    grad_w_back = jnp.einsum("rf,rd->fd", active, full_grad, preferred_element_type=jnp.float32)
    grad_active = jnp.einsum(
        "rd,fd->rf", full_grad, gathered[5], preferred_element_type=jnp.float32
    )
    gelu_pull = jax.vjp(gelu_local, hidden)[1]
    grad_hidden_rows = gelu_pull(grad_active)[0].astype(jnp.bfloat16)
    grad_w_hidden = jnp.einsum(
        "rd,rf->df", full_two, grad_hidden_rows, preferred_element_type=jnp.float32
    )
    w_hidden_full = gathered[4]
    piece = grad_hidden_rows
    grad_normed_two = lax.psum_scatter(
        jnp.einsum("rf,df->rd", piece, w_hidden_full, preferred_element_type=jnp.float32).astype(
            jnp.bfloat16
        ),
        "tensor",
        scatter_dimension=0,
        tiled=True,
    ).astype(jnp.float32)
    second_pull = jax.vjp(normed, middle, gain_second)[1]
    grad_mid_norm, grad_second = second_pull(grad_normed_two)
    grad_middle = grad_out + grad_mid_norm
    full_middle = lax.all_gather(grad_middle.astype(jnp.bfloat16), "tensor", axis=0, tiled=True)
    grad_w_output = jnp.einsum(
        "rh,rd->hd", attended, full_middle, preferred_element_type=jnp.float32
    )
    grad_attended = jnp.einsum(
        "rd,hd->rh", full_middle, gathered[3], preferred_element_type=jnp.float32
    ).astype(jnp.bfloat16)

    def backward_block(carry, packed):
        grad_keys, grad_values = carry
        query_block, grad_block, log_block, block_start = packed
        scores = scores_for(query_block, key_rows, segments, block_start, block_rows)
        probability = jnp.exp(scores - log_block[..., None])
        grad_values = grad_values + jnp.einsum(
            "hqk,qhe->khe",
            probability.astype(jnp.bfloat16),
            grad_block,
            preferred_element_type=jnp.float32,
        )
        grad_probs = jnp.einsum(
            "qhe,khe->hqk", grad_block, value_rows, preferred_element_type=jnp.float32
        )
        delta_rows = jnp.sum(grad_probs * probability, axis=-1, keepdims=True)
        grad_scores = (probability * (grad_probs - delta_rows)).astype(jnp.bfloat16)
        grad_query_block = (
            jnp.einsum("hqk,khe->qhe", grad_scores, key_rows, preferred_element_type=jnp.float32)
            * scale
        )
        grad_keys = (
            grad_keys
            + jnp.einsum(
                "hqk,qhe->khe", grad_scores, query_block, preferred_element_type=jnp.float32
            )
            * scale
        )
        return ((grad_keys, grad_values), grad_query_block)

    zero_state = jnp.zeros((total_rows, heads_here, E), jnp.float32)
    grad_blocks = grad_attended.reshape(blocks, block_rows, heads_here, E)
    (grad_keys, grad_values), grad_queries = lax.scan(
        backward_block, (zero_state, zero_state), (query_blocks, grad_blocks, log_sums, starts)
    )
    grad_joined = jnp.concatenate(
        [
            grad_queries.reshape(total_rows, width),
            grad_keys.reshape(total_rows, width),
            grad_values.reshape(total_rows, width),
        ],
        axis=1,
    ).astype(jnp.bfloat16)
    grad_w_joined = jnp.einsum(
        "rd,rc->dc", full_one, grad_joined, preferred_element_type=jnp.float32
    )
    piece = grad_joined
    grad_normed_one = lax.psum_scatter(
        jnp.einsum("rc,dc->rd", piece, w_joined, preferred_element_type=jnp.float32).astype(
            jnp.bfloat16
        ),
        "tensor",
        scatter_dimension=0,
        tiled=True,
    ).astype(jnp.float32)
    first_pull = jax.vjp(normed, inputs_f, gain_first)[1]
    grad_in_norm, grad_first = first_pull(grad_normed_one)
    grad_inputs = grad_middle + grad_in_norm
    weight_sums = (
        lax.psum_scatter(grad_w_joined[:, :width], "dp", scatter_dimension=0, tiled=True),
        lax.psum_scatter(
            grad_w_joined[:, width : 2 * width], "dp", scatter_dimension=0, tiled=True
        ),
        lax.psum_scatter(grad_w_joined[:, 2 * width :], "dp", scatter_dimension=0, tiled=True),
        lax.psum_scatter(grad_w_output, "dp", scatter_dimension=1, tiled=True),
        lax.psum_scatter(grad_w_hidden, "dp", scatter_dimension=0, tiled=True),
        lax.psum_scatter(grad_w_back, "dp", scatter_dimension=1, tiled=True),
    )
    gain_sums = (
        lax.psum_scatter(grad_first, ("dp", "tensor"), scatter_dimension=0, tiled=True),
        lax.psum_scatter(grad_second, ("dp", "tensor"), scatter_dimension=0, tiled=True),
    )
    return (
        result.astype(jnp.bfloat16),
        grad_inputs.astype(jnp.bfloat16),
        weight_sums[0],
        weight_sums[1],
        weight_sums[2],
        weight_sums[3],
        weight_sums[4],
        weight_sums[5],
        gain_sums[0],
        gain_sums[1],
    )


def solution(mesh):
    rows, cols = P(("dp", "tensor"), None), P("dp", "tensor")
    turned, part = P("tensor", "dp"), P("dp")
    in_specs = (rows, part, cols, cols, cols, turned, cols, turned, part, part, rows)
    out_specs = (rows, rows, cols, cols, cols, turned, cols, turned, P(("dp", "tensor")), P(("dp", "tensor")))
    here = mesh.shape["dp"] == 2 * NZ and mesh.shape["tensor"] == 4
    body = block if here else shards
    return jax.shard_map(body, mesh=mesh, in_specs=in_specs, out_specs=out_specs, check_vma=False)
```

```python
import functools

import jax
import jax.numpy as jnp
from jax import lax
from jax.experimental import pallas as pl
from jax.experimental.pallas import tpu as pltpu
from jax.sharding import PartitionSpec as P

MESH = pl.DeviceIdType.MESH
f32, bf = jnp.float32, jnp.bfloat16
E = 64
WINDOW = 1536
B = 256
LOG2E = 1.4426950408889634
SCALE = E**-0.5
FILL = -1e30
NZ = 4
HB = 256
UNIT = 2 * HB


def nn(a, b):
    return lax.dot_general(a, b, (((1,), (0,)), ((), ())), preferred_element_type=f32)


def nt(a, b):
    return lax.dot_general(a, b, (((1,), (1,)), ((), ())), preferred_element_type=f32)


def tn(a, b):
    return lax.dot_general(a, b, (((0,), (0,)), ((), ())), preferred_element_type=f32)


class Place:
    def __init__(self):
        self.dp = lax.axis_index("dp")
        self.t = lax.axis_index("tensor")
        self.z, self.y = lax.div(self.dp, 2), lax.rem(self.dp, 2)
        self.x, self.c = lax.div(self.t, 2), lax.rem(self.t, 2)
        self.left, self.right = self.at(z=self.z - 1), self.at(z=self.z + 1)
        self.sides = [sides(self, rnd) for rnd in range(NZ)]

    def at(self, z=None, y=None, x=None, c=None):
        z = self.z if z is None else z
        y = self.y if y is None else y
        x = self.x if x is None else x
        c = self.c if c is None else c
        return (z * 2 + y, x * 2 + c)

    def greet(self, far_z):
        barrier = pltpu.get_barrier_semaphore()
        x, y, z, c = self.x, self.y, self.z, self.c
        near = [self.at(y=1 - y), self.at(x=1 - x), self.at(c=1 - c), self.at(x=1 - x, c=1 - c)]
        for there in near:
            pl.semaphore_signal(barrier, inc=1, device_id=there, device_id_type=MESH)
        for step in range(1, NZ):
            pl.semaphore_signal(
                barrier, inc=1, device_id=self.at(z=lax.rem(z + step, NZ)), device_id_type=MESH
            )
        pl.semaphore_wait(barrier, len(near) + NZ - 1)


class Lanes:
    def __init__(self, send, recv):
        self.send, self.recv, self.n, self.base, self.late = send, recv, 0, {}, []

    def block(self, name, count):
        self.base[name] = self.n
        self.n += count

    def copy(self, name, k, src, dst, there, land=None):
        i = self.base[name]
        return pltpu.make_async_remote_copy(
            src_ref=src,
            dst_ref=dst,
            send_sem=self.send.at[i + k],
            recv_sem=self.recv.at[i + (k if land is None else land)],
            device_id=there,
            device_id_type=MESH,
        )

    def start(self, name, k, ends, there, when=None):
        at = k if callable(k) else lambda: k
        self.copy(name, at(), *ends(), there).start()

        def finish():
            self.copy(name, at(), *ends(), there).wait_send()

        self.late.append((finish, when))

    def start_at(self, name, k, src, dst, there):
        self.copy(name, k, src, dst, there).start()

    def arrived(self, name, k, dst, there):
        self.copy(name, k, dst, dst, there).wait_recv()

    def finish(self):
        for act, when in self.late:
            if when is None:
                act()
            else:
                pl.when(when())(act)


def sides(me, rnd):
    z = me.z
    if rnd == 0:
        return [(z, None, None)]
    return [(z - rnd, True, lambda: z >= rnd), (z + rnd, False, lambda: z + rnd < NZ)]


def line_round(me, lanes, name, rnd, ref_of, arrive):
    z = me.z
    left, right = me.left, me.right

    def go(zi, to_right, when):
        def side():
            return z < NZ - 1 if to_right else z > 0

        def whole():
            return side() if when is None else jnp.logical_and(when(), side())

        lane, there = name + ("R" if to_right else "L"), right if to_right else left

        def copy():
            return lanes.copy(lane, zi, ref_of(zi), ref_of(zi), there)

        pl.when(side())(lambda: copy().start())
        lanes.late.append((lambda: copy().wait_send(), whole))

    for zi, from_left, ok in me.sides[rnd]:
        if rnd == 0:
            go(zi, True, None)
            go(zi, False, None)
            arrive(zi, None)
            continue

        @pl.when(ok())
        def _(zi=zi, from_left=from_left, ok=ok):
            lanes.arrived(name + ("R" if from_left else "L"), zi, ref_of(zi), left if from_left else right)
            go(zi, from_left, ok)
            arrive(zi, ok)


def masked(i, j, blocks):
    return j == i or j == 0 or i >= blocks - 2 or i - j >= WINDOW // B


def keep(i, j, low, value, fill):
    key_pos = lax.broadcasted_iota(jnp.int32, value.shape, 0) + j * B
    ok = key_pos >= low
    if i == j:
        ok = ok & (key_pos <= lax.broadcasted_iota(jnp.int32, value.shape, 1) + i * B)
    return jnp.where(ok, value, fill)


def spans(i):
    first = max(0, i - WINDOW // B)
    return first, list(range(first, i + 1))


def score_pass(i, h, slot, blocks, kn, qh, low_ref, S):
    j0, js = spans(i)
    cols = slice(i * B, (i + 1) * B)
    qT = qh[h, 0:E, cols]
    low = low_ref[0:1, cols]
    top = jnp.full((1, B), FILL, f32)
    for j in js:
        s = nn(kn[h, j * B : (j + 1) * B, :], qT)
        if masked(i, j, blocks):
            s = keep(i, j, low, s, FILL)
        S[slot, (j - j0) * B : (j - j0 + 1) * B, :] = s
        top = jnp.maximum(top, jnp.max(s, axis=0, keepdims=True))
    return top * (SCALE * LOG2E)


def value_pass(i, h, slot, top, qh, S, o_ref, L_ref):
    j0, js = spans(i)
    total = jnp.zeros((1, B), f32)
    out = jnp.zeros((E, B), f32)
    for j in js:
        p = jnp.exp2(S[slot, (j - j0) * B : (j - j0 + 1) * B, :] * (SCALE * LOG2E) - top)
        total = total + jnp.sum(p, axis=0, keepdims=True)
        out = out + nn(qh[h, 2 * E : 3 * E, j * B : (j + 1) * B], p.astype(bf))
    half = i % 2
    o_ref[i // 2, pl.ds(pl.multiple_of(h * E, E), E), half * B : (half + 1) * B] = (out / total).astype(bf)
    L_ref[h, :, i * B : (i + 1) * B] = jnp.broadcast_to(top + jnp.log2(total), (8, B))


def lows(seg, total):
    pos = lax.broadcasted_iota(jnp.int32, (1, total), 1)
    low = jnp.maximum(pos - (WINDOW - 1), 0)
    first = seg[0:1, 0:1]
    for d in range(1, 5):
        begin = jnp.sum((seg < first + d).astype(f32), axis=1, keepdims=True).astype(jnp.int32)
        low = jnp.where(seg >= first + d, jnp.maximum(low, begin), low)
    return low


def pack(v):
    n = v.shape[-2] // 2
    tail = v[..., 128:192]
    return jnp.concatenate([v[..., 0:128], jnp.concatenate([tail[..., 0:n, :], tail[..., n:, :]], axis=-1)], axis=-2)


def unpack(v):
    n = v.shape[-2] // 3
    low = v[..., 2 * n :, :]
    return jnp.concatenate([v[..., 0 : 2 * n, :], jnp.concatenate([low[..., 0:64], low[..., 64:]], axis=-2)], axis=-1)


def gelu_and_slope(u):
    root = 0.7978845608028654
    square = u * u
    th = jnp.tanh(u * (root + (root * 0.044715) * square))
    half = 0.5 + 0.5 * th
    slope = half + (0.5 * u) * (1.0 - th * th) * (root + (3.0 * root * 0.044715) * square)
    return u * half, slope


def norm_pull(value, gain, grad):
    inv = lax.rsqrt(jnp.mean(value * value, axis=-1, keepdims=True) + 1e-05)
    scaled = grad * gain
    return inv * scaled - value * (inv * inv * inv * jnp.mean(value * scaled, axis=-1, keepdims=True))


def kernel(xo, cot, seg, wq, wk, wv, wo, wh, wb, g1, g2,
           gin, result, g1s, g2s, gains,
           X4, n1, W1, W1T, W5, G5, WO, qh, o_ref, oin, L_ref, low_ref, cb, n2b, x1, rdn, rres, dsend, do_ref,
           gws, gwr, gwx, R1, R2, G1, RY, RZ, RA, RA2, RZ2, RC, RX, RYc, gs, gr, send, recv):
    me = Place()
    dp, t, x, y, z, c = me.dp, me.t, me.x, me.y, me.z, me.c
    rows, dm = xo.shape
    total = n1.shape[0]
    blocks = total // B
    heads = qh.shape[0]
    part, width = wq.shape
    ff = wh.shape[1]
    units = ff // HB
    routed = 2 * ff - HB
    X_, Y_, C_, XC_ = me.at(x=1 - x), me.at(y=1 - y), me.at(c=1 - c), me.at(x=1 - x, c=1 - c)
    far = [None] + [me.at(z=lax.rem(z + step, NZ)) for step in range(1, NZ)]
    near_t, cross_t, core_t = (1 - x) * 2 + c, (1 - x) * 2 + 1 - c, x * 2 + 1 - c
    lanes = Lanes(send, recv)
    for name, count in (
        ("aR", 4), ("aL", 4), ("ay", 4), ("x", 2), ("cx", 2), ("co", 1), ("cc", 1),
        ("wz", 3), ("wy", 1), ("wx", 1), ("wc", 2),
        ("bz", 3 * units), ("by", 3 * units), ("bo", 1), ("bx", units), ("bxy", units), ("o", 4),
        ("fy", 1), ("fx", 1), ("fz", 3), ("hz", 3), ("hx", 1), ("hy", 1),
        ("n2", 1), ("dn", 1), ("rs", 1), ("gw", 1), ("gx", 1), ("do", 4),
        ("ra", 2 * units), ("ra2", units), ("z2", 3 * units),
        ("d1", 2), ("d2", 1), ("y1", 4 * (heads + 1)), ("z1", 3 * (heads + 1)), ("g", 3),
    ):
        lanes.block(name, count)

    def unit(u):
        return pl.ds(u * UNIT, UNIT if u < units - 1 else HB)

    rest = pl.ds((units - 1) * UNIT + HB, HB)

    me.greet(True)
    half = rows // 2
    for k in range(2):
        lanes.start("x", k, lambda k=k: (xo.at[pl.ds(k * half, half)], X4.at[t, pl.ds(k * half, half)]), X_)
    zeros = jnp.zeros((part, 56), f32)
    both_gains = jnp.concatenate([g1[...].astype(f32), g2[...].astype(f32), jnp.zeros((6, part), f32)], axis=0)
    both_gains = jnp.concatenate([both_gains, jnp.zeros((8, 128 - part), f32)], axis=1).T[0:part]
    pieces = []
    for h in range(heads):
        for w in (wq, wk, wv):
            pieces.append(w[:, h * E : (h + 1) * E])
    pieces.append(jnp.concatenate([both_gains, zeros], axis=1).astype(bf))
    W1[dp] = jnp.concatenate(pieces, axis=1)

    def a_ref(zi):
        return W1.at[zi * 2 + y]

    def a_arrive(zi, when):
        lanes.start("ay", zi, lambda: (a_ref(zi), a_ref(zi)), Y_, when)

    line_round(me, lanes, "a", 0, a_ref, a_arrive)
    lanes.start("co", 0, lambda: (xo, X4.at[t]), C_)
    lanes.start("cc", 0, lambda: (cot, cb.at[pl.ds(rows, rows)]), C_)
    WO[t, z, y] = pack(wo[...].T)
    back_T = wb[...]
    for u in range(units):
        W5[x, z, y, :, u * UNIT : u * UNIT + HB] = wh[:, u * HB : (u + 1) * HB]
        W5[x, z, y, :, u * UNIT + HB : (u + 1) * UNIT] = back_T[:, u * HB : (u + 1) * HB]
    low_ref[...] = jnp.broadcast_to(lows(seg[...], total), low_ref.shape)
    X4[t] = xo[...]
    cb[0:rows, :] = cot[...]

    def w_z():
        for step in range(1, NZ):
            lanes.start("wz", step - 1, lambda: (WO.at[t, z, y],) * 2, far[step])

    zs = [None] + [lax.rem(z + NZ - step, NZ) for step in range(1, NZ)]

    def from_z(step):
        return lax.rem(z + NZ - step, NZ)

    def w_y():
        for step in range(1, NZ):
            lanes.arrived("wz", step - 1, WO.at[t, from_z(step), y], far[NZ - step])
        lanes.start("wy", 0, lambda: (WO.at[t, :, y],) * 2, Y_)

    def w_x():
        lanes.arrived("wy", 0, WO.at[t, :, 1 - y], Y_)
        lanes.start("wx", 0, lambda: (WO.at[t],) * 2, X_)
        lanes.start("wc", 0, lambda: (WO.at[t],) * 2, C_)

    def w_c():
        lanes.arrived("wx", 0, WO.at[near_t], X_)
        lanes.start("wc", 1, lambda: (WO.at[near_t],) * 2, C_)

    def w_end():
        lanes.arrived("wc", 0, WO.at[core_t], C_)
        lanes.arrived("wc", 1, WO.at[cross_t], C_)

    def b_z(u):
        for step in range(1, NZ):
            lanes.start("bz", u * 3 + step - 1, lambda: (W5.at[x, z, y, :, unit(u)],) * 2, far[step])

    def b_y(u):
        for step in range(1, NZ):
            lanes.arrived("bz", u * 3 + step - 1, W5.at[x, from_z(step), y, :, unit(u)], far[NZ - step])
        for step in range(1, NZ):
            zi = zs[step]
            lanes.start("by", u * 3 + step - 1, lambda zi=zi: (W5.at[x, zi, y, :, unit(u)],) * 2, Y_)

    def b_own():
        lanes.start("bo", 0, lambda: (W5.at[x, z, y, :, pl.ds(0, routed)],) * 2, Y_)

    def b_x(u):
        lanes.start("bx", u, lambda: (W5.at[x, :, y, :, unit(u)],) * 2, X_)

    def b_corner(u):
        lanes.arrived("bx", u, W5.at[1 - x, :, y, :, unit(u)], X_)
        lanes.start("bxy", u, lambda: (W5.at[1 - x, :, y, :, unit(u)],) * 2, Y_)

    def b_near(u):
        for step in range(1, NZ):
            lanes.arrived("by", u * 3 + step - 1, W5.at[x, zs[step], 1 - y, :, unit(u)], Y_)
        if u == 0:
            lanes.arrived("bo", 0, W5.at[x, z, 1 - y, :, pl.ds(0, routed)], Y_)

    def b_end(u):
        lanes.arrived("bxy", u, W5.at[1 - x, :, 1 - y, :, unit(u)], Y_)

    def f_y():
        lanes.start("fy", 0, lambda: (W5.at[x, z, y, :, rest],) * 2, Y_)

    def f_x():
        lanes.arrived("fy", 0, W5.at[x, z, 1 - y, :, rest], Y_)
        lanes.start("fx", 0, lambda: (W5.at[x, z, :, :, rest],) * 2, X_)

    def f_z():
        lanes.arrived("fx", 0, W5.at[1 - x, z, :, :, rest], X_)
        for step in range(1, NZ):
            lanes.start("fz", step - 1, lambda: (W5.at[:, z, :, :, rest],) * 2, far[step])

    def f_end():
        for step in range(1, NZ):
            lanes.arrived("fz", step - 1, W5.at[:, from_z(step), :, :, rest], far[NZ - step])

    def quarter(r, kn, S, events):
        def body(h, carry):
            tops = []
            for i in (2 * r, 2 * r + 1):
                tops.append(score_pass(i, h, i % 2, blocks, kn, qh, low_ref, S))
            for i in (2 * r, 2 * r + 1):
                value_pass(i, h, i % 2, tops[i % 2], qh, S, o_ref, L_ref)
            for k in range(heads):
                if k in events:
                    pl.when(h == k)(lambda: [act() for act in events[k]] and None)
            return carry

        lax.fori_loop(0, heads, body, 0)

        def out_copy():
            return lanes.copy("o", r, o_ref.at[r], oin.at[t], (dp, r), land=t)

        @pl.when(t == r)
        def _():
            oin[t] = o_ref[r]

        pl.when(t != r)(lambda: out_copy().start())
        lanes.late.append((lambda: out_copy().wait_send(), lambda: t != r))

    def forward(kn, S):
        line_round(me, lanes, "a", 1, a_ref, a_arrive)
        line_round(me, lanes, "a", 2, a_ref, a_arrive)
        w_z()
        line_round(me, lanes, "a", 3, a_ref, a_arrive)
        b_z(0)
        b_z(1)
        b_z(2)
        for zi in range(NZ):
            lanes.arrived("ay", zi, W1.at[zi * 2 + 1 - y], Y_)
        w_y()
        f_y()
        b_own()
        W1T[...] = W1[...].reshape(2 * NZ * part, W1.shape[2]).T

        def project(blk):
            base = pl.multiple_of(blk * rows, rows)
            gain = W1T[heads * 3 * E : heads * 3 * E + 16, :].astype(f32)[0:1]
            value = X4[blk].astype(f32)
            inv = lax.rsqrt(jnp.mean(value * value, axis=-1, keepdims=True) + 1e-05)
            normed = (value * inv * gain).astype(bf)
            n1[pl.ds(base, rows), :] = normed
            out = nt(W1T[0 : heads * 3 * E, :], normed).astype(bf)
            for h in range(heads):
                qh[h, :, pl.ds(base, rows)] = out[h * 3 * E : (h + 1) * 3 * E]
                kn[h, pl.ds(base, rows), :] = out[h * 3 * E + E : h * 3 * E + 2 * E].T

        project(t)
        lanes.arrived("co", 0, X4.at[core_t], C_)
        project(core_t)
        for k in range(2):
            got = X4.at[near_t, pl.ds(k * half, half)]
            lanes.arrived("x", k, got, X_)
            lanes.start_at("cx", k, got, got, C_)
        f_x()
        w_x()
        project(near_t)
        b_y(0)
        b_x(0)
        for k in range(2):
            lanes.arrived("cx", k, X4.at[cross_t, pl.ds(k * half, half)], C_)
        project(cross_t)
        f_z()
        quarter(0, kn, S, {})
        b_y(1)
        quarter(1, kn, S, {})
        w_c()
        b_x(1)
        b_y(2)
        quarter(2, kn, S, {})
        b_corner(0)
        quarter(3, kn, S, {})

    pl.run_scoped(forward, pltpu.VMEM((heads, total, E), bf), pltpu.VMEM((2, WINDOW + B, B), f32))

    r_unit = lanes.base["ra"]

    def sum_first(xs, u):
        lanes.start_at("ra", xs * units + u, G5.at[xs, :, 1 - y, :, unit(u)], RA.at[xs, :, :, unit(u)], Y_)

    def middle(wof, n2T, cT, res, dn2):
        w_end()
        for k in range(4):
            wof[k * width : (k + 1) * width, :] = unpack(WO[k].reshape(2 * NZ, 144, 128)).reshape(dm, width).T
        gain = W1T[heads * 3 * E : heads * 3 * E + 16, :].astype(f32)[1:2]
        lanes.arrived("cc", 0, cb.at[pl.ds(rows, rows)], C_)
        cT[...] = cb[...].T
        for there in (near_t, core_t, cross_t):
            lanes.arrived("o", there, oin.at[there], (dp, there))
        b_x(2)
        b_corner(1)
        mid = xo[...].astype(f32) + tn(oin[...].reshape(4 * width, rows), wof[...])
        x1[...] = mid
        inv = lax.rsqrt(jnp.mean(mid * mid, axis=-1, keepdims=True) + 1e-05)
        n2b[0:rows, :] = (mid * inv * gain).astype(bf)
        lanes.copy("n2", 0, n2b.at[pl.ds(0, rows)], n2b.at[pl.ds(rows, rows)], C_).start()
        n2T[:, 0:rows] = n2b[0:rows, :].T
        lanes.arrived("n2", 0, n2b.at[pl.ds(rows, rows)], C_)
        n2T[:, rows:] = n2b[rows:, :].T
        b_near(0)

        def weights(xs, u):
            col = u * UNIT
            return (W5[xs, :, :, :, col + k * HB : col + (k + 1) * HB].reshape(dm, HB) for k in range(2))

        def through(xs, u):
            w_h, w_b = weights(xs, u)
            hid = nn(n2b[...], w_h)
            act, slope = gelu_and_slope(hid)
            act = act.astype(bf)
            du = (nn(cb[...], w_b) * slope).astype(bf)
            return act, du, w_h, w_b

        def grads(xs, u, act, du):
            col = u * UNIT
            G5[xs, :, :, :, col : col + HB] = nn(n2T[...], du).astype(bf).reshape(NZ, 2, part, HB)
            G5[xs, :, :, :, col + HB : col + UNIT] = nn(cT[...], act).astype(bf).reshape(NZ, 2, part, HB)

        for u in range(units):
            if u > 0:
                b_near(u)
            if u == 1:
                b_corner(2)
            if u == units - 1:
                f_end()
            act, du, w_h, w_b = through(x, u)
            if u == 0:
                dn2[...] = nt(du, w_h)
                res[...] = nt(act, w_b)
            else:
                dn2[...] += nt(du, w_h)
                res[...] += nt(act, w_b)
            grads(x, u, act, du)
        for k in range(2):
            got = X4.at[near_t, pl.ds(k * half, half)]
            lanes.copy("cx", k, got, got, C_).wait_send()
        for u in range(units):
            b_end(u)
            if u == 0:
                sum_first(x, 0)
            cols = slice(u * HB, (u + 1) * HB)
            act, du, w_h, w_b = through(1 - x, u)
            dn2[...] += nt(du, w_h)
            if u < 1:
                grads(1 - x, u, act, du)
                sum_first(1 - x, u)
            for k in range(2):
                X4[k, :, cols] = act[k * rows : (k + 1) * rows]
                X4[2 + k, :, cols] = du[k * rows : (k + 1) * rows]

        def kept(k, u):
            return X4[2 * k : 2 * k + 2, :, u * HB : (u + 1) * HB].reshape(2 * rows, HB)

        lanes.copy("n2", 0, n2b.at[pl.ds(0, rows)], n2b.at[pl.ds(rows, rows)], C_).wait_send()
        n2b[0:rows, :] = dn2[rows:, :].astype(bf)
        lanes.start("dn", 0, lambda: (n2b.at[pl.ds(0, rows)], rdn), C_)
        for u in range(1):
            w_h, w_b = weights(1 - x, u)
            res[...] += nt(kept(0, u), w_b)
        lanes.arrived("dn", 0, rdn, C_)
        back = cot[...].astype(f32) + norm_pull(x1[...], gain, dn2[0:rows, :] + rdn[...].astype(f32))
        dn2[0:rows, :] = back
        back = back.astype(bf)
        out = nt(wof[...], back).astype(bf)
        for r in range(4):
            dsend[r] = out[r * width : (r + 1) * width]

            def to_owner(r=r):
                return lanes.copy("do", r, dsend.at[r], do_ref.at[t], (dp, r), land=t)

            @pl.when(t == r)
            def _():
                do_ref[t] = dsend[r]

            pl.when(t != r)(lambda: to_owner().start())
            lanes.late.append((lambda r=r, f=to_owner: f(r).wait_send(), lambda r=r: t != r))
        for u in range(units):
            if u >= 1:
                grads(1 - x, u, kept(0, u), kept(1, u))
                sum_first(1 - x, u)
        for step in range(1, NZ):
            zi = lax.rem(z + step, NZ)
            lanes.start_at("hz", step - 1, G5.at[:, zi, :, :, rest], RC.at[step - 1], far[step])
        for u in range(1, units):
            w_h, w_b = weights(1 - x, u)
            res[...] += nt(kept(0, u), w_b)
        n2b[rows:, :] = res[rows:, :].astype(bf)
        lanes.start("rs", 0, lambda: (n2b.at[pl.ds(rows, rows)], rres), C_)
        gw = nt(back.T, oin[...].reshape(4 * width, rows)).astype(bf)
        quarters = [pack(gw[:, k * width : (k + 1) * width].reshape(2 * NZ, part, width)) for k in range(4)]
        for xs in range(2):
            even, odd = quarters[2 * xs], quarters[2 * xs + 1]
            gws[xs] = jnp.where(c == 0, odd, even)
            gws[2 + xs] = jnp.where(c == 0, even, odd)
        lanes.start("gw", 0, lambda: (gws.at[pl.ds(0, 2)], gwr), C_)
        lanes.arrived("rs", 0, rres, C_)
        result[...] = (x1[...] + res[0:rows, :] + rres[...].astype(f32)).astype(bf)
        x1[...] = dn2[0:rows, :]

    pl.run_scoped(
        middle, pltpu.VMEM((dm, dm), bf), pltpu.VMEM((dm, 2 * rows), bf), pltpu.VMEM((dm, 2 * rows), bf),
        pltpu.VMEM((2 * rows, dm), f32), pltpu.VMEM((2 * rows, dm), f32),
    )

    def w_back_x():
        lanes.arrived("gw", 0, gwr, C_)
        gws[2 + 1 - x] = (gws[2 + 1 - x].astype(f32) + gwr[1 - x].astype(f32)).astype(bf)
        lanes.start("gx", 0, lambda: (gws.at[2 + 1 - x], gwx), X_)
        gws[2 + x] = (gws[2 + x].astype(f32) + gwr[x].astype(f32)).astype(bf)

    def w_back_y():
        lanes.arrived("gx", 0, gwx, X_)
        G1[heads] = (gws[2 + x].astype(f32) + gwx[...].astype(f32)).astype(bf)
        one_y(heads)

    def add(ref_at, *more):
        value = ref_at[...].astype(f32)
        for m in more:
            value = value + m.astype(f32)
        ref_at[...] = value.astype(bf)

    def second(u):
        lanes.arrived("ra", (1 - x) * units + u, RA.at[1 - x, :, :, unit(u)], Y_)
        add(G5.at[1 - x, :, y, :, unit(u)], RA[1 - x, :, :, unit(u)])
        lanes.start_at("ra2", u, G5.at[1 - x, :, y, :, unit(u)], RA2.at[:, :, unit(u)], X_)

    def rest_x():
        for step in range(1, NZ):
            lanes.arrived("hz", step - 1, RC.at[step - 1], far[NZ - step])
        add(G5.at[:, z, :, :, rest], RC[0], RC[1], RC[2])
        lanes.start_at("hx", 0, G5.at[1 - x, z, :, :, rest], RX, X_)

    def rest_y():
        lanes.arrived("hx", 0, RX, X_)
        add(G5.at[x, z, :, :, rest], RX[...])
        lanes.start_at("hy", 0, G5.at[x, z, 1 - y, :, rest], RYc, Y_)

    def third(u):
        lanes.arrived("ra", x * units + u, RA.at[x, :, :, unit(u)], Y_)
        lanes.arrived("ra2", u, RA2.at[:, :, unit(u)], X_)
        add(G5.at[x, :, y, :, unit(u)], RA[x, :, :, unit(u)], RA2[:, :, unit(u)])
        for step in range(1, NZ):
            zi = lax.rem(z + step, NZ)
            lanes.start_at("z2", u * 3 + step - 1, G5.at[x, zi, y, :, unit(u)], RZ2.at[step - 1, :, unit(u)], far[step])

    def last():
        value = G5[x, z, y, :, 0:routed].astype(f32)
        for step in range(1, NZ):
            for u in range(units):
                lanes.arrived("z2", u * 3 + step - 1, RZ2.at[step - 1, :, unit(u)], far[NZ - step])
            value = value + RZ2[step - 1].astype(f32)
        g2s[:, 0:routed] = value
        lanes.arrived("hy", 0, RYc, Y_)
        g2s[:, routed:] = G5[x, z, y, :, routed:].astype(f32) + RYc[...].astype(f32)

    def one_y(h):
        for zi in range(NZ):
            lanes.start_at("y1", h * 4 + zi, G1.at[h, zi * 2 + 1 - y], RY.at[h, zi], Y_)

    def one_z(h):
        for step in range(NZ):
            zi = lax.rem(z + step, NZ)
            lanes.arrived("y1", h * 4 + zi, RY.at[h, zi], Y_)
            G1[h, zi * 2 + y] = (G1[h, zi * 2 + y].astype(f32) + RY[h, zi].astype(f32)).astype(bf)
            if step:
                lanes.start_at("z1", h * 3 + step - 1, G1.at[h, zi * 2 + y], RZ.at[h, step - 1], far[step])

    def one_last(h):
        value = G1[h, dp].astype(f32)
        for step in range(1, NZ):
            lanes.arrived("z1", h * 3 + step - 1, RZ.at[h, step - 1], far[NZ - step])
            value = value + RZ[h, step - 1].astype(f32)
        value = unpack(value)
        g1s[:, h * 256 : h * 256 + 3 * E] = value
        return value

    def backward(kn, vn, dk, dv):
        def rows_first(r):
            xr, cr = r // 2, r % 2
            piece = qh[:, :, r * rows : (r + 1) * rows].reshape(heads * 3 * E, rows)
            X4[r] = tn(piece, W1T[0 : heads * 3 * E, :]).astype(bf)
            pl.when(c != cr)(lambda: lanes.start_at("d1", xr, X4.at[r], R1.at[xr], C_))

        def rows_second(r):
            xr, cr = r // 2, r % 2

            @pl.when(c == cr)
            def _():
                lanes.arrived("d1", xr, R1.at[xr], C_)
                X4[r] = (X4[r].astype(f32) + R1[xr].astype(f32)).astype(bf)
                pl.when(x != xr)(lambda: lanes.start_at("d2", 0, X4.at[r], R2, X_))

        events = {
            (0, 7): [lambda: second(0), lambda: sum_first(x, 1)],
            (0, 5): [lambda: second(1), lambda: sum_first(x, 2)],
            (0, 2): [lambda: second(2), rest_x],
            (1, 7): [lambda: third(0), w_back_x],
            (1, 4): [rest_y],
            (1, 2): [lambda: third(1)],
            (2, 7): [w_back_y],
            (2, 5): [lambda: third(2)],
            (2, 1): [lambda: one_z(heads)],
        }

        def head(h, carry):
            kn[...] = qh[h, E : 2 * E, :].T
            vn[...] = qh[h, 2 * E : 3 * E, :].T
            for i in range(blocks)[::-1]:
                j0, js = spans(i)
                cols = slice(i * B, (i + 1) * B)
                half = slice((i % 2) * B, (i % 2 + 1) * B)
                hs = pl.ds(pl.multiple_of(h * E, E), E)
                qT, doT = qh[h, 0:E, cols], do_ref[i // 2, hs, half]
                low, L = low_ref[0:1, cols], L_ref[h, 0:1, cols]
                D = jnp.sum(doT.astype(f32) * o_ref[i // 2, hs, half].astype(f32), axis=0, keepdims=True)
                dq = jnp.zeros((E, B), f32)

                def front(j):
                    ks = slice(j * B, (j + 1) * B)
                    return nn(kn[ks, :], qT), nn(vn[ks, :], doT)

                queue = [front(j) for j in js[:2]]
                for n, j in enumerate(js):
                    ks = slice(j * B, (j + 1) * B)
                    if n + 2 < len(js):
                        queue.append(front(js[n + 2]))
                    s, dp_ = queue.pop(0)
                    p = jnp.exp2(s * (SCALE * LOG2E) - L)
                    if masked(i, j, blocks):
                        p = keep(i, j, low, p, 0.0)
                    ds = (p * (dp_ - D)).astype(bf)
                    dvj, dkj = nt(doT, p.astype(bf)), nt(qT, ds)
                    if i == min(blocks - 1, j + WINDOW // B):
                        dv[:, ks] = dvj
                        dk[:, ks] = dkj
                    else:
                        dv[:, ks] += dvj
                        dk[:, ks] += dkj
                    dq = dq + nn(qh[h, E : 2 * E, ks], ds)
                qh[h, 0:E, cols] = (dq * SCALE).astype(bf)
                qh[h, E : 2 * E, cols] = (dk[:, cols] * SCALE).astype(bf)
                qh[h, 2 * E : 3 * E, cols] = dv[:, cols].astype(bf)
                for k in range(heads):
                    for act in events.get((k, i), ()):
                        pl.when(h == k)(act)
                if i == 4:
                    pl.when(h > 0)(lambda: one_z(h - 1))
                if i % 2 == 0:

                    @pl.when(h == heads - 1)
                    def _():
                        rows_first(i // 2)
                        if i // 2 < 3:
                            rows_second(i // 2 + 1)

            G1[h] = pack(nn(qh[h], n1[...]).T.astype(bf).reshape(2 * NZ, part, 3 * E))
            one_y(h)
            return carry

        lax.fori_loop(0, heads, head, 0)
        rows_second(0)

    for there in (core_t, near_t, cross_t):
        lanes.arrived("do", there, do_ref.at[there], (dp, there))
    pl.run_scoped(
        backward, pltpu.VMEM((total, E), bf), pltpu.VMEM((total, E), bf), pltpu.VMEM((E, total), f32), pltpu.VMEM((E, total), f32)
    )
    one_z(heads - 1)
    last()
    w1v = W1[dp].astype(f32)
    sums = [one_last(h) for h in range(heads + 1)]
    gain1 = sum(
        jnp.sum(sums[h][:, 0 : 3 * E] * w1v[:, h * 3 * E : (h + 1) * 3 * E], axis=1, keepdims=True) for h in range(heads)
    ) / w1v[:, heads * 3 * E : heads * 3 * E + 1]
    gain2 = sum(
        jnp.sum(g2s[:, u * UNIT : u * UNIT + HB] * wh[:, u * HB : (u + 1) * HB].astype(f32), axis=1, keepdims=True)
        for u in range(units)
    ) / w1v[:, heads * 3 * E + 1 : heads * 3 * E + 2]
    both_ = jnp.concatenate([gain1, gain2, jnp.zeros((part, 126), f32)], axis=1)
    gs[...] = jnp.concatenate([both_, jnp.zeros((128 - part, 128), f32)], axis=0).T[0:8]
    for k, there in enumerate((X_, C_, XC_)):
        lanes.start("g", k, lambda k=k: (gs, gr.at[k]), there)
    gain = W1T[heads * 3 * E : heads * 3 * E + 16, :].astype(f32)[0:1]
    lanes.arrived("d2", 0, R2, X_)
    dn1 = X4[t].astype(f32) + R2[...].astype(f32)
    gin[...] = (x1[...] + norm_pull(xo[...].astype(f32), gain, dn1)).astype(bf)
    for k, there in enumerate((X_, C_, XC_)):
        lanes.arrived("g", k, gr.at[k], there)
    gains[...] = gs[...] + gr[0] + gr[1] + gr[2]
    for xs in range(2):
        for u in range(units):
            lanes.copy("ra", xs * units + u, G5.at[xs, :, 1 - y, :, unit(u)], RA.at[xs, :, :, unit(u)], Y_).wait_send()
    for step in range(1, NZ):
        zi = lax.rem(z + step, NZ)
        lanes.copy("hz", step - 1, G5.at[:, zi, :, :, rest], RC.at[step - 1], far[step]).wait_send()
    lanes.copy("hx", 0, G5.at[1 - x, z, :, :, rest], RX, X_).wait_send()
    lanes.copy("hy", 0, G5.at[x, z, 1 - y, :, rest], RYc, Y_).wait_send()
    for u in range(units):
        lanes.copy("ra2", u, G5.at[1 - x, :, y, :, unit(u)], RA2.at[:, :, unit(u)], X_).wait_send()
        for step in range(1, NZ):
            zi = lax.rem(z + step, NZ)
            lanes.copy("z2", u * 3 + step - 1, G5.at[x, zi, y, :, unit(u)], RZ2.at[step - 1, :, unit(u)], far[step]).wait_send()
    for h in range(heads + 1):
        for zi in range(NZ):
            lanes.copy("y1", h * 4 + zi, G1.at[h, zi * 2 + 1 - y], RY.at[h, zi], Y_).wait_send()
        for step in range(1, NZ):
            zi = lax.rem(z + step, NZ)
            lanes.copy("z1", h * 3 + step - 1, G1.at[h, zi * 2 + y], RZ.at[h, step - 1], far[step]).wait_send()
    for r in range(4):
        xr, cr = r // 2, r % 2
        pl.when(c != cr)(lambda: lanes.copy("d1", xr, X4.at[r], R1.at[xr], C_).wait_send())
        pl.when(jnp.logical_and(c == cr, x != xr))(lambda: lanes.copy("d2", 0, X4.at[r], R2, X_).wait_send())
    lanes.finish()


VM = pl.BlockSpec(memory_space=pltpu.VMEM)


def unpack_kernel(gin, result, g1s, g2s, gains, o_result, o_gin, gq, gk, gv, go, gh, gb, gg1, gg2):
    o_result[...] = result[...]
    o_gin[...] = gin[...]
    heads = gq.shape[1] // E
    for h in range(heads):
        base = h * 256
        for k, out in enumerate((gq, gk, gv)):
            out[:, h * E : (h + 1) * E] = g1s[:, base + k * E : base + (k + 1) * E]
    go[...] = g1s[:, heads * 256 : (heads + 1) * 256].T[0 : go.shape[0]]
    units = gh.shape[1] // HB
    for u in range(units):
        gh[:, u * HB : (u + 1) * HB] = g2s[:, u * UNIT : u * UNIT + HB]
        gb[:, u * HB : (u + 1) * HB] = g2s[:, u * UNIT + HB : (u + 1) * UNIT]
    n = gg1.shape[1]
    t = lax.axis_index("tensor")
    for k, out in enumerate((gg1, gg2)):
        value = gains[k : k + 1, 0:n]
        for at in range(1, 4):
            value = jnp.where(t == at, gains[k : k + 1, at * n : (at + 1) * n], value)
        out[...] = value


def block(inputs, segments, w_query, w_key, w_value, w_output, w_hidden, w_back, gain_one, gain_two, cotangent):
    rows, dm = inputs.shape
    total = segments.shape[0]
    part, width = w_query.shape
    heads = width // E
    ff = w_hidden.shape[1]
    units = ff // HB
    s, v = jax.ShapeDtypeStruct, pltpu.VMEM
    first = (units - 1) * UNIT + HB
    gin, result, g1s, g2s, gains = pl.pallas_call(
        kernel,
        out_shape=(
            s((rows, dm), bf), s((rows, dm), bf), s((part, (heads + 1) * 256), f32), s((part, 2 * ff), f32), s((8, 128), f32),
        ),
        in_specs=[VM] * 11,
        out_specs=(VM,) * 5,
        scratch_shapes=[
            v((4, rows, dm), bf), v((total, dm), bf), v((2 * NZ, part, 640), bf), v((640, dm), bf),
            v((2, NZ, 2, part, 2 * ff), bf), v((2, NZ, 2, part, 2 * ff), bf), v((4, NZ, 2, 144, 128), bf),
            v((heads, 3 * E, total), bf), v((4, width, rows), bf), v((4, width, rows), bf),
            v((heads, 8, total), f32), v((8, total), jnp.int32), v((2 * rows, dm), bf), v((2 * rows, dm), bf), v((rows, dm), f32),
            v((rows, dm), bf), v((rows, dm), bf), v((4, width, rows), bf), v((4, width, rows), bf),
            v((4, 2 * NZ, 144, 128), bf), v((2, 2 * NZ, 144, 128), bf), v((2 * NZ, 144, 128), bf), v((2, rows, dm), bf), v((rows, dm), bf),
            v((heads + 1, 2 * NZ, 144, 128), bf), v((heads + 1, NZ, 144, 128), bf), v((heads + 1, 3, 144, 128), bf),
            v((2, NZ, part, first), bf), v((NZ, part, first), bf), v((3, part, first), bf),
            v((3, 2, 2, part, HB), bf), v((2, part, HB), bf), v((part, HB), bf), v((8, 128), f32), v((3, 8, 128), f32),
            pltpu.SemaphoreType.DMA((144,)), pltpu.SemaphoreType.DMA((144,)),
        ],
        compiler_params=pltpu.CompilerParams(collective_id=1, has_side_effects=True, vmem_limit_bytes=63 * 2**20),
    )(
        inputs, cotangent, segments.reshape(1, total), w_query, w_key, w_value, w_output, w_hidden, w_back.T,
        gain_one.reshape(1, part), gain_two.reshape(1, part),
    )
    outs = pl.pallas_call(
        unpack_kernel,
        out_shape=(
            s((rows, dm), bf), s((rows, dm), bf), s((part, width), f32), s((part, width), f32), s((part, width), f32),
            s((width, part), f32), s((part, ff), f32), s((part, ff), f32), s((1, part // 4), f32), s((1, part // 4), f32),
        ),
        in_specs=[VM] * 5,
        out_specs=(VM,) * 10,
    )(gin, result, g1s, g2s, gains)
    return (*outs[:7], outs[7].T, *(g.reshape(part // 4) for g in outs[8:]))


def normed(value, gain):
    return value * lax.rsqrt(jnp.mean(value * value, axis=-1, keepdims=True) + 1e-05) * gain


def gelu_local(value):
    return jax.nn.gelu(value, approximate=True)


def scores_for(query_block, key_rows, segment_ids, block_start, block_rows):
    positions = jnp.arange(key_rows.shape[0], dtype=jnp.int32)
    query_pos = block_start + jnp.arange(block_rows, dtype=jnp.int32)
    query_seg = lax.dynamic_slice_in_dim(segment_ids, block_start, block_rows)
    scores = jnp.einsum(
        "qhe,khe->hqk", query_block, key_rows, preferred_element_type=jnp.float32
    ) * E ** (-0.5)
    distance = query_pos[:, None] - positions[None, :]
    allowed = (query_seg[:, None] == segment_ids[None, :]) & (distance >= 0) & (distance < WINDOW)
    return jnp.where(allowed[None], scores, -1e30)


def shards(
    inputs,
    segments,
    w_query,
    w_key,
    w_value,
    w_output,
    w_hidden,
    w_back,
    gain_one,
    gain_two,
    cotangent,
):
    owned = (w_query, w_key, w_value, w_output, w_hidden, w_back, gain_one, gain_two)
    gathered = (
        lax.all_gather(owned[0], "dp", axis=0, tiled=True),
        lax.all_gather(owned[1], "dp", axis=0, tiled=True),
        lax.all_gather(owned[2], "dp", axis=0, tiled=True),
        lax.all_gather(owned[3], "dp", axis=1, tiled=True),
        lax.all_gather(owned[4], "dp", axis=0, tiled=True),
        lax.all_gather(owned[5], "dp", axis=1, tiled=True),
        lax.all_gather(owned[6], "dp", axis=0, tiled=True),
        lax.all_gather(owned[7], "dp", axis=0, tiled=True),
    )
    total_rows = segments.shape[0]
    block_rows = min(512, total_rows)
    blocks = total_rows // block_rows
    width = gathered[0].shape[1]
    heads_here = width // E
    scale = E ** (-0.5)
    starts = jnp.arange(blocks, dtype=jnp.int32) * block_rows
    w_joined = jnp.concatenate([gathered[0], gathered[1], gathered[2]], axis=1)
    gain_first = gathered[6].astype(jnp.float32)
    gain_second = gathered[7].astype(jnp.float32)
    inputs_f = inputs.astype(jnp.float32)
    normed_one = normed(inputs_f, gain_first).astype(jnp.bfloat16)
    full_one = lax.all_gather(normed_one, "tensor", axis=0, tiled=True)
    joined = jnp.dot(full_one, w_joined, preferred_element_type=jnp.float32).astype(jnp.bfloat16)
    query_rows = joined[:, :width].reshape(total_rows, heads_here, E)
    key_rows = joined[:, width : 2 * width].reshape(total_rows, heads_here, E)
    value_rows = joined[:, 2 * width :].reshape(total_rows, heads_here, E)
    query_blocks = query_rows.reshape(blocks, block_rows, heads_here, E)

    def forward_block(packed):
        query_block, block_start = packed
        scores = scores_for(query_block, key_rows, segments, block_start, block_rows)
        row_top = jnp.max(scores, axis=-1, keepdims=True)
        weights_exp = jnp.exp(scores - row_top)
        totals = jnp.sum(weights_exp, axis=-1, keepdims=True)
        probability = (weights_exp / totals).astype(jnp.bfloat16)
        attended_block = jnp.einsum(
            "hqk,khe->qhe", probability, value_rows, preferred_element_type=jnp.float32
        )
        return (attended_block.astype(jnp.bfloat16), (row_top + jnp.log(totals))[..., 0])

    attended, log_sums = lax.map(forward_block, (query_blocks, starts))
    attended = attended.reshape(total_rows, width)
    w_out_full = gathered[3]
    own_attended = lax.all_to_all(attended, "tensor", split_axis=0, concat_axis=1, tiled=True)
    w_out_all = lax.all_gather(w_out_full, "tensor", axis=0, tiled=True)
    attn_branch = jnp.dot(own_attended, w_out_all, preferred_element_type=jnp.float32)
    middle = inputs_f + attn_branch
    normed_two = normed(middle, gain_second).astype(jnp.bfloat16)
    full_two = lax.all_gather(normed_two, "tensor", axis=0, tiled=True)
    hidden = jnp.dot(full_two, gathered[4], preferred_element_type=jnp.float32)
    active = gelu_local(hidden).astype(jnp.bfloat16)
    w_back_full = gathered[5]
    result = middle + lax.psum_scatter(
        jnp.dot(active, w_back_full, preferred_element_type=jnp.float32).astype(jnp.bfloat16),
        "tensor",
        scatter_dimension=0,
        tiled=True,
    ).astype(jnp.float32)
    gathered = (
        lax.all_gather(owned[0], "dp", axis=0, tiled=True),
        lax.all_gather(owned[1], "dp", axis=0, tiled=True),
        lax.all_gather(owned[2], "dp", axis=0, tiled=True),
        lax.all_gather(owned[3], "dp", axis=1, tiled=True),
        lax.all_gather(owned[4], "dp", axis=0, tiled=True),
        lax.all_gather(owned[5], "dp", axis=1, tiled=True),
        lax.all_gather(owned[6], "dp", axis=0, tiled=True),
        lax.all_gather(owned[7], "dp", axis=0, tiled=True),
    )
    w_joined = jnp.concatenate([gathered[0], gathered[1], gathered[2]], axis=1)
    grad_out = cotangent.astype(jnp.float32)
    full_grad = lax.all_gather(cotangent, "tensor", axis=0, tiled=True)
    grad_w_back = jnp.einsum("rf,rd->fd", active, full_grad, preferred_element_type=jnp.float32)
    grad_active = jnp.einsum(
        "rd,fd->rf", full_grad, gathered[5], preferred_element_type=jnp.float32
    )
    gelu_pull = jax.vjp(gelu_local, hidden)[1]
    grad_hidden_rows = gelu_pull(grad_active)[0].astype(jnp.bfloat16)
    grad_w_hidden = jnp.einsum(
        "rd,rf->df", full_two, grad_hidden_rows, preferred_element_type=jnp.float32
    )
    w_hidden_full = gathered[4]
    piece = grad_hidden_rows
    grad_normed_two = lax.psum_scatter(
        jnp.einsum("rf,df->rd", piece, w_hidden_full, preferred_element_type=jnp.float32).astype(
            jnp.bfloat16
        ),
        "tensor",
        scatter_dimension=0,
        tiled=True,
    ).astype(jnp.float32)
    second_pull = jax.vjp(normed, middle, gain_second)[1]
    grad_mid_norm, grad_second = second_pull(grad_normed_two)
    grad_middle = grad_out + grad_mid_norm
    full_middle = lax.all_gather(grad_middle.astype(jnp.bfloat16), "tensor", axis=0, tiled=True)
    grad_w_output = jnp.einsum(
        "rh,rd->hd", attended, full_middle, preferred_element_type=jnp.float32
    )
    grad_attended = jnp.einsum(
        "rd,hd->rh", full_middle, gathered[3], preferred_element_type=jnp.float32
    ).astype(jnp.bfloat16)

    def backward_block(carry, packed):
        grad_keys, grad_values = carry
        query_block, grad_block, log_block, block_start = packed
        scores = scores_for(query_block, key_rows, segments, block_start, block_rows)
        probability = jnp.exp(scores - log_block[..., None])
        grad_values = grad_values + jnp.einsum(
            "hqk,qhe->khe",
            probability.astype(jnp.bfloat16),
            grad_block,
            preferred_element_type=jnp.float32,
        )
        grad_probs = jnp.einsum(
            "qhe,khe->hqk", grad_block, value_rows, preferred_element_type=jnp.float32
        )
        delta_rows = jnp.sum(grad_probs * probability, axis=-1, keepdims=True)
        grad_scores = (probability * (grad_probs - delta_rows)).astype(jnp.bfloat16)
        grad_query_block = (
            jnp.einsum("hqk,khe->qhe", grad_scores, key_rows, preferred_element_type=jnp.float32)
            * scale
        )
        grad_keys = (
            grad_keys
            + jnp.einsum(
                "hqk,qhe->khe", grad_scores, query_block, preferred_element_type=jnp.float32
            )
            * scale
        )
        return ((grad_keys, grad_values), grad_query_block)

    zero_state = jnp.zeros((total_rows, heads_here, E), jnp.float32)
    grad_blocks = grad_attended.reshape(blocks, block_rows, heads_here, E)
    (grad_keys, grad_values), grad_queries = lax.scan(
        backward_block, (zero_state, zero_state), (query_blocks, grad_blocks, log_sums, starts)
    )
    grad_joined = jnp.concatenate(
        [
            grad_queries.reshape(total_rows, width),
            grad_keys.reshape(total_rows, width),
            grad_values.reshape(total_rows, width),
        ],
        axis=1,
    ).astype(jnp.bfloat16)
    grad_w_joined = jnp.einsum(
        "rd,rc->dc", full_one, grad_joined, preferred_element_type=jnp.float32
    )
    piece = grad_joined
    grad_normed_one = lax.psum_scatter(
        jnp.einsum("rc,dc->rd", piece, w_joined, preferred_element_type=jnp.float32).astype(
            jnp.bfloat16
        ),
        "tensor",
        scatter_dimension=0,
        tiled=True,
    ).astype(jnp.float32)
    first_pull = jax.vjp(normed, inputs_f, gain_first)[1]
    grad_in_norm, grad_first = first_pull(grad_normed_one)
    grad_inputs = grad_middle + grad_in_norm
    weight_sums = (
        lax.psum_scatter(grad_w_joined[:, :width], "dp", scatter_dimension=0, tiled=True),
        lax.psum_scatter(
            grad_w_joined[:, width : 2 * width], "dp", scatter_dimension=0, tiled=True
        ),
        lax.psum_scatter(grad_w_joined[:, 2 * width :], "dp", scatter_dimension=0, tiled=True),
        lax.psum_scatter(grad_w_output, "dp", scatter_dimension=1, tiled=True),
        lax.psum_scatter(grad_w_hidden, "dp", scatter_dimension=0, tiled=True),
        lax.psum_scatter(grad_w_back, "dp", scatter_dimension=1, tiled=True),
    )
    gain_sums = (
        lax.psum_scatter(grad_first, ("dp", "tensor"), scatter_dimension=0, tiled=True),
        lax.psum_scatter(grad_second, ("dp", "tensor"), scatter_dimension=0, tiled=True),
    )
    return (
        result.astype(jnp.bfloat16),
        grad_inputs.astype(jnp.bfloat16),
        weight_sums[0],
        weight_sums[1],
        weight_sums[2],
        weight_sums[3],
        weight_sums[4],
        weight_sums[5],
        gain_sums[0],
        gain_sums[1],
    )


def solution(mesh):
    rows, cols = P(("dp", "tensor"), None), P("dp", "tensor")
    turned, part = P("tensor", "dp"), P("dp")
    in_specs = (rows, part, cols, cols, cols, turned, cols, turned, part, part, rows)
    out_specs = (rows, rows, cols, cols, cols, turned, cols, turned, P(("dp", "tensor")), P(("dp", "tensor")))
    here = mesh.shape["dp"] == 2 * NZ and mesh.shape["tensor"] == 4
    body = block if here else shards
    return jax.shard_map(body, mesh=mesh, in_specs=in_specs, out_specs=out_specs, check_vma=False)
```

```python
import functools

import jax
import jax.numpy as jnp
from jax import lax
from jax.experimental import pallas as pl
from jax.experimental.pallas import tpu as pltpu
from jax.sharding import PartitionSpec as P

MESH = pl.DeviceIdType.MESH
f32, bf = jnp.float32, jnp.bfloat16
E = 64
WINDOW = 1536
B = 256
LOG2E = 1.4426950408889634
SCALE = E**-0.5
FILL = -1e30
NZ = 4
HB = 256
UNIT = 2 * HB


def nn(a, b):
    return lax.dot_general(a, b, (((1,), (0,)), ((), ())), preferred_element_type=f32)


def nt(a, b):
    return lax.dot_general(a, b, (((1,), (1,)), ((), ())), preferred_element_type=f32)


def tn(a, b):
    return lax.dot_general(a, b, (((0,), (0,)), ((), ())), preferred_element_type=f32)


class Place:
    def __init__(self):
        self.dp = lax.axis_index("dp")
        self.t = lax.axis_index("tensor")
        self.z, self.y = lax.div(self.dp, 2), lax.rem(self.dp, 2)
        self.x, self.c = lax.div(self.t, 2), lax.rem(self.t, 2)
        self.left, self.right = self.at(z=self.z - 1), self.at(z=self.z + 1)
        self.sides = [sides(self, rnd) for rnd in range(NZ)]

    def at(self, z=None, y=None, x=None, c=None):
        z = self.z if z is None else z
        y = self.y if y is None else y
        x = self.x if x is None else x
        c = self.c if c is None else c
        return (z * 2 + y, x * 2 + c)

    def greet(self, far_z):
        barrier = pltpu.get_barrier_semaphore()
        x, y, z, c = self.x, self.y, self.z, self.c
        near = [self.at(y=1 - y), self.at(x=1 - x), self.at(c=1 - c), self.at(x=1 - x, c=1 - c)]
        for there in near:
            pl.semaphore_signal(barrier, inc=1, device_id=there, device_id_type=MESH)
        for step in range(1, NZ):
            pl.semaphore_signal(
                barrier, inc=1, device_id=self.at(z=lax.rem(z + step, NZ)), device_id_type=MESH
            )
        pl.semaphore_wait(barrier, len(near) + NZ - 1)


class Lanes:
    def __init__(self, send, recv):
        self.send, self.recv, self.n, self.base, self.late = send, recv, 0, {}, []

    def block(self, name, count):
        self.base[name] = self.n
        self.n += count

    def copy(self, name, k, src, dst, there, land=None):
        i = self.base[name]
        return pltpu.make_async_remote_copy(
            src_ref=src,
            dst_ref=dst,
            send_sem=self.send.at[i + k],
            recv_sem=self.recv.at[i + (k if land is None else land)],
            device_id=there,
            device_id_type=MESH,
        )

    def start(self, name, k, ends, there, when=None):
        at = k if callable(k) else lambda: k
        self.copy(name, at(), *ends(), there).start()

        def finish():
            self.copy(name, at(), *ends(), there).wait_send()

        self.late.append((finish, when))

    def start_at(self, name, k, src, dst, there):
        self.copy(name, k, src, dst, there).start()

    def arrived(self, name, k, dst, there):
        self.copy(name, k, dst, dst, there).wait_recv()

    def finish(self):
        for act, when in self.late:
            if when is None:
                act()
            else:
                pl.when(when())(act)


def sides(me, rnd):
    z = me.z
    if rnd == 0:
        return [(z, None, None)]
    return [(z - rnd, True, lambda: z >= rnd), (z + rnd, False, lambda: z + rnd < NZ)]


def line_round(me, lanes, name, rnd, ref_of, arrive):
    z = me.z
    left, right = me.left, me.right

    def go(zi, to_right, when):
        def side():
            return z < NZ - 1 if to_right else z > 0

        def whole():
            return side() if when is None else jnp.logical_and(when(), side())

        lane, there = name + ("R" if to_right else "L"), right if to_right else left

        def copy():
            return lanes.copy(lane, zi, ref_of(zi), ref_of(zi), there)

        pl.when(side())(lambda: copy().start())
        lanes.late.append((lambda: copy().wait_send(), whole))

    for zi, from_left, ok in me.sides[rnd]:
        if rnd == 0:
            go(zi, True, None)
            go(zi, False, None)
            arrive(zi, None)
            continue

        @pl.when(ok())
        def _(zi=zi, from_left=from_left, ok=ok):
            lanes.arrived(name + ("R" if from_left else "L"), zi, ref_of(zi), left if from_left else right)
            go(zi, from_left, ok)
            arrive(zi, ok)


def masked(i, j, blocks):
    return j == i or j == 0 or i >= blocks - 2 or i - j >= WINDOW // B


def keep(i, j, low, value, fill):
    key_pos = lax.broadcasted_iota(jnp.int32, value.shape, 0) + j * B
    ok = key_pos >= low
    if i == j:
        ok = ok & (key_pos <= lax.broadcasted_iota(jnp.int32, value.shape, 1) + i * B)
    return jnp.where(ok, value, fill)


def spans(i):
    first = max(0, i - WINDOW // B)
    return first, list(range(first, i + 1))


def score_pass(i, h, slot, blocks, kn, qh, low_ref, S):
    j0, js = spans(i)
    cols = slice(i * B, (i + 1) * B)
    qT = qh[h, 0:E, cols]
    low = low_ref[0:1, cols]
    top = jnp.full((1, B), FILL, f32)
    for j in js:
        s = nn(kn[h, j * B : (j + 1) * B, :], qT)
        if masked(i, j, blocks):
            s = keep(i, j, low, s, FILL)
        S[slot, (j - j0) * B : (j - j0 + 1) * B, :] = s
        top = jnp.maximum(top, jnp.max(s, axis=0, keepdims=True))
    return top * (SCALE * LOG2E)


def value_pass(i, h, slot, top, qh, S, o_ref, L_ref):
    j0, js = spans(i)
    total = jnp.zeros((1, B), f32)
    out = jnp.zeros((E, B), f32)
    for j in js:
        p = jnp.exp2(S[slot, (j - j0) * B : (j - j0 + 1) * B, :] * (SCALE * LOG2E) - top)
        total = total + jnp.sum(p, axis=0, keepdims=True)
        out = out + nn(qh[h, 2 * E : 3 * E, j * B : (j + 1) * B], p.astype(bf))
    half = i % 2
    o_ref[i // 2, pl.ds(pl.multiple_of(h * E, E), E), half * B : (half + 1) * B] = (out / total).astype(bf)
    L_ref[h, :, i * B : (i + 1) * B] = jnp.broadcast_to(top + jnp.log2(total), (8, B))


def lows(seg, total):
    pos = lax.broadcasted_iota(jnp.int32, (1, total), 1)
    low = jnp.maximum(pos - (WINDOW - 1), 0)
    first = seg[0:1, 0:1]
    for d in range(1, 5):
        begin = jnp.sum((seg < first + d).astype(f32), axis=1, keepdims=True).astype(jnp.int32)
        low = jnp.where(seg >= first + d, jnp.maximum(low, begin), low)
    return low


def pack(v):
    n = v.shape[-2] // 2
    tail = v[..., 128:192]
    return jnp.concatenate([v[..., 0:128], jnp.concatenate([tail[..., 0:n, :], tail[..., n:, :]], axis=-1)], axis=-2)


def unpack(v):
    n = v.shape[-2] // 3
    low = v[..., 2 * n :, :]
    return jnp.concatenate([v[..., 0 : 2 * n, :], jnp.concatenate([low[..., 0:64], low[..., 64:]], axis=-2)], axis=-1)


def gelu_and_slope(u):
    root = 0.7978845608028654
    square = u * u
    th = jnp.tanh(u * (root + (root * 0.044715) * square))
    half = 0.5 + 0.5 * th
    slope = half + (0.5 * u) * (1.0 - th * th) * (root + (3.0 * root * 0.044715) * square)
    return u * half, slope


def norm_pull(value, gain, grad):
    inv = lax.rsqrt(jnp.mean(value * value, axis=-1, keepdims=True) + 1e-05)
    scaled = grad * gain
    return inv * scaled - value * (inv * inv * inv * jnp.mean(value * scaled, axis=-1, keepdims=True))


def kernel(xo, cot, seg, wq, wk, wv, wo, wh, wb, g1, g2,
           gin, result, g1s, g2s, gains,
           X4, n1, W1, W1T, W5, G5, WO, qh, o_ref, oin, L_ref, low_ref, cb, n2b, x1, rdn, rres, dsend, do_ref,
           gws, gwr, gwx, R1, R2, G1, RY, RZ, RA, RA2, RZ2, RC, RX, RYc, gs, gr, send, recv):
    me = Place()
    dp, t, x, y, z, c = me.dp, me.t, me.x, me.y, me.z, me.c
    rows, dm = xo.shape
    total = n1.shape[0]
    blocks = total // B
    heads = qh.shape[0]
    part, width = wq.shape
    ff = wh.shape[1]
    units = ff // HB
    routed = 2 * ff - HB
    X_, Y_, C_, XC_ = me.at(x=1 - x), me.at(y=1 - y), me.at(c=1 - c), me.at(x=1 - x, c=1 - c)
    far = [None] + [me.at(z=lax.rem(z + step, NZ)) for step in range(1, NZ)]
    near_t, cross_t, core_t = (1 - x) * 2 + c, (1 - x) * 2 + 1 - c, x * 2 + 1 - c
    lanes = Lanes(send, recv)
    for name, count in (
        ("aR", 4), ("aL", 4), ("ay", 4), ("x", 2), ("cx", 2), ("co", 1), ("cc", 1),
        ("wz", 3), ("wy", 1), ("wx", 1), ("wc", 2),
        ("bz", 3 * units), ("by", 3 * units), ("bo", 1), ("bx", units), ("bxy", units), ("o", 4),
        ("fy", 1), ("fx", 1), ("fz", 3), ("hz", 3), ("hx", 1), ("hy", 1),
        ("n2", 1), ("dn", 1), ("rs", 1), ("gw", 1), ("gx", 1), ("do", 4),
        ("ra", 2 * units), ("ra2", units), ("z2", 3 * units),
        ("d1", 2), ("d2", 1), ("y1", 4 * (heads + 1)), ("z1", 3 * (heads + 1)), ("g", 3),
    ):
        lanes.block(name, count)

    def unit(u):
        return pl.ds(u * UNIT, UNIT if u < units - 1 else HB)

    rest = pl.ds((units - 1) * UNIT + HB, HB)

    me.greet(True)
    half = rows // 2
    for k in range(2):
        lanes.start("x", k, lambda k=k: (xo.at[pl.ds(k * half, half)], X4.at[t, pl.ds(k * half, half)]), X_)
    zeros = jnp.zeros((part, 56), f32)
    both_gains = jnp.concatenate([g1[...].astype(f32), g2[...].astype(f32), jnp.zeros((6, part), f32)], axis=0)
    both_gains = jnp.concatenate([both_gains, jnp.zeros((8, 128 - part), f32)], axis=1).T[0:part]
    pieces = []
    for h in range(heads):
        for w in (wq, wk, wv):
            pieces.append(w[:, h * E : (h + 1) * E])
    pieces.append(jnp.concatenate([both_gains, zeros], axis=1).astype(bf))
    W1[dp] = jnp.concatenate(pieces, axis=1)

    def a_ref(zi):
        return W1.at[zi * 2 + y]

    def a_arrive(zi, when):
        lanes.start("ay", zi, lambda: (a_ref(zi), a_ref(zi)), Y_, when)

    line_round(me, lanes, "a", 0, a_ref, a_arrive)
    lanes.start("co", 0, lambda: (xo, X4.at[t]), C_)
    lanes.start("cc", 0, lambda: (cot, cb.at[pl.ds(rows, rows)]), C_)
    WO[t, z, y] = pack(wo[...].T)
    back_T = wb[...]
    for u in range(units):
        W5[x, z, y, :, u * UNIT : u * UNIT + HB] = wh[:, u * HB : (u + 1) * HB]
        W5[x, z, y, :, u * UNIT + HB : (u + 1) * UNIT] = back_T[:, u * HB : (u + 1) * HB]
    low_ref[...] = jnp.broadcast_to(lows(seg[...], total), low_ref.shape)
    X4[t] = xo[...]
    cb[0:rows, :] = cot[...]

    def w_z():
        for step in range(1, NZ):
            lanes.start("wz", step - 1, lambda: (WO.at[t, z, y],) * 2, far[step])

    zs = [None] + [lax.rem(z + NZ - step, NZ) for step in range(1, NZ)]

    def from_z(step):
        return lax.rem(z + NZ - step, NZ)

    def w_y():
        for step in range(1, NZ):
            lanes.arrived("wz", step - 1, WO.at[t, from_z(step), y], far[NZ - step])
        lanes.start("wy", 0, lambda: (WO.at[t, :, y],) * 2, Y_)

    def w_x():
        lanes.arrived("wy", 0, WO.at[t, :, 1 - y], Y_)
        lanes.start("wx", 0, lambda: (WO.at[t],) * 2, X_)
        lanes.start("wc", 0, lambda: (WO.at[t],) * 2, C_)

    def w_c():
        lanes.arrived("wx", 0, WO.at[near_t], X_)
        lanes.start("wc", 1, lambda: (WO.at[near_t],) * 2, C_)

    def w_end():
        lanes.arrived("wc", 0, WO.at[core_t], C_)
        lanes.arrived("wc", 1, WO.at[cross_t], C_)

    def b_z(u):
        for step in range(1, NZ):
            lanes.start("bz", u * 3 + step - 1, lambda: (W5.at[x, z, y, :, unit(u)],) * 2, far[step])

    def b_y(u):
        for step in range(1, NZ):
            lanes.arrived("bz", u * 3 + step - 1, W5.at[x, from_z(step), y, :, unit(u)], far[NZ - step])
        for step in range(1, NZ):
            zi = zs[step]
            lanes.start("by", u * 3 + step - 1, lambda zi=zi: (W5.at[x, zi, y, :, unit(u)],) * 2, Y_)

    def b_own():
        lanes.start("bo", 0, lambda: (W5.at[x, z, y, :, pl.ds(0, routed)],) * 2, Y_)

    def b_x(u):
        lanes.start("bx", u, lambda: (W5.at[x, :, y, :, unit(u)],) * 2, X_)

    def b_corner(u):
        lanes.arrived("bx", u, W5.at[1 - x, :, y, :, unit(u)], X_)
        lanes.start("bxy", u, lambda: (W5.at[1 - x, :, y, :, unit(u)],) * 2, Y_)

    def b_near(u):
        for step in range(1, NZ):
            lanes.arrived("by", u * 3 + step - 1, W5.at[x, zs[step], 1 - y, :, unit(u)], Y_)
        if u == 0:
            lanes.arrived("bo", 0, W5.at[x, z, 1 - y, :, pl.ds(0, routed)], Y_)

    def b_end(u):
        lanes.arrived("bxy", u, W5.at[1 - x, :, 1 - y, :, unit(u)], Y_)

    def f_y():
        lanes.start("fy", 0, lambda: (W5.at[x, z, y, :, rest],) * 2, Y_)

    def f_x():
        lanes.arrived("fy", 0, W5.at[x, z, 1 - y, :, rest], Y_)
        lanes.start("fx", 0, lambda: (W5.at[x, z, :, :, rest],) * 2, X_)

    def f_z():
        lanes.arrived("fx", 0, W5.at[1 - x, z, :, :, rest], X_)
        for step in range(1, NZ):
            lanes.start("fz", step - 1, lambda: (W5.at[:, z, :, :, rest],) * 2, far[step])

    def f_end():
        for step in range(1, NZ):
            lanes.arrived("fz", step - 1, W5.at[:, from_z(step), :, :, rest], far[NZ - step])

    def quarter(r, kn, S, events):
        def body(h, carry):
            tops = []
            for i in (2 * r, 2 * r + 1):
                tops.append(score_pass(i, h, i % 2, blocks, kn, qh, low_ref, S))
            for i in (2 * r, 2 * r + 1):
                value_pass(i, h, i % 2, tops[i % 2], qh, S, o_ref, L_ref)
            for k in range(heads):
                if k in events:
                    pl.when(h == k)(lambda: [act() for act in events[k]] and None)
            return carry

        lax.fori_loop(0, heads, body, 0)

        def out_copy():
            return lanes.copy("o", r, o_ref.at[r], oin.at[t], (dp, r), land=t)

        @pl.when(t == r)
        def _():
            oin[t] = o_ref[r]

        pl.when(t != r)(lambda: out_copy().start())
        lanes.late.append((lambda: out_copy().wait_send(), lambda: t != r))

    def forward(kn, S):
        line_round(me, lanes, "a", 1, a_ref, a_arrive)
        line_round(me, lanes, "a", 2, a_ref, a_arrive)
        w_z()
        line_round(me, lanes, "a", 3, a_ref, a_arrive)
        b_z(0)
        b_z(1)
        b_z(2)
        for zi in range(NZ):
            lanes.arrived("ay", zi, W1.at[zi * 2 + 1 - y], Y_)
        w_y()
        f_y()
        b_own()
        W1T[...] = W1[...].reshape(2 * NZ * part, W1.shape[2]).T

        def project(blk):
            base = pl.multiple_of(blk * rows, rows)
            gain = W1T[heads * 3 * E : heads * 3 * E + 16, :].astype(f32)[0:1]
            value = X4[blk].astype(f32)
            inv = lax.rsqrt(jnp.mean(value * value, axis=-1, keepdims=True) + 1e-05)
            normed = (value * inv * gain).astype(bf)
            n1[pl.ds(base, rows), :] = normed
            out = nt(W1T[0 : heads * 3 * E, :], normed).astype(bf)
            for h in range(heads):
                qh[h, :, pl.ds(base, rows)] = out[h * 3 * E : (h + 1) * 3 * E]
                kn[h, pl.ds(base, rows), :] = out[h * 3 * E + E : h * 3 * E + 2 * E].T

        project(t)
        lanes.arrived("co", 0, X4.at[core_t], C_)
        project(core_t)
        for k in range(2):
            got = X4.at[near_t, pl.ds(k * half, half)]
            lanes.arrived("x", k, got, X_)
            lanes.start_at("cx", k, got, got, C_)
        f_x()
        w_x()
        project(near_t)
        b_y(0)
        b_x(0)
        for k in range(2):
            lanes.arrived("cx", k, X4.at[cross_t, pl.ds(k * half, half)], C_)
        project(cross_t)
        f_z()
        quarter(0, kn, S, {})
        b_y(1)
        quarter(1, kn, S, {})
        w_c()
        b_x(1)
        b_y(2)
        quarter(2, kn, S, {})
        b_corner(0)
        quarter(3, kn, S, {})

    pl.run_scoped(forward, pltpu.VMEM((heads, total, E), bf), pltpu.VMEM((2, WINDOW + B, B), f32))

    r_unit = lanes.base["ra"]

    def sum_first(xs, u):
        lanes.start_at("ra", xs * units + u, G5.at[xs, :, 1 - y, :, unit(u)], RA.at[xs, :, :, unit(u)], Y_)

    def middle(wof, n2T, cT, res, dn2):
        w_end()
        for k in range(4):
            wof[k * width : (k + 1) * width, :] = unpack(WO[k].reshape(2 * NZ, 144, 128)).reshape(dm, width).T
        gain = W1T[heads * 3 * E : heads * 3 * E + 16, :].astype(f32)[1:2]
        lanes.arrived("cc", 0, cb.at[pl.ds(rows, rows)], C_)
        cT[...] = cb[...].T
        for there in (near_t, core_t, cross_t):
            lanes.arrived("o", there, oin.at[there], (dp, there))
        b_x(2)
        b_corner(1)
        mid = xo[...].astype(f32) + tn(oin[...].reshape(4 * width, rows), wof[...])
        x1[...] = mid
        inv = lax.rsqrt(jnp.mean(mid * mid, axis=-1, keepdims=True) + 1e-05)
        n2b[0:rows, :] = (mid * inv * gain).astype(bf)
        lanes.copy("n2", 0, n2b.at[pl.ds(0, rows)], n2b.at[pl.ds(rows, rows)], C_).start()
        n2T[:, 0:rows] = n2b[0:rows, :].T
        lanes.arrived("n2", 0, n2b.at[pl.ds(rows, rows)], C_)
        n2T[:, rows:] = n2b[rows:, :].T
        b_near(0)

        def weights(xs, u):
            col = u * UNIT
            return (W5[xs, :, :, :, col + k * HB : col + (k + 1) * HB].reshape(dm, HB) for k in range(2))

        def through(xs, u):
            w_h, w_b = weights(xs, u)
            hid = nn(n2b[...], w_h)
            act, slope = gelu_and_slope(hid)
            act = act.astype(bf)
            du = (nn(cb[...], w_b) * slope).astype(bf)
            return act, du, w_h, w_b

        def grads(xs, u, act, du):
            col = u * UNIT
            G5[xs, :, :, :, col : col + HB] = nn(n2T[...], du).astype(bf).reshape(NZ, 2, part, HB)
            G5[xs, :, :, :, col + HB : col + UNIT] = nn(cT[...], act).astype(bf).reshape(NZ, 2, part, HB)

        for u in range(units):
            if u > 0:
                b_near(u)
            if u == 1:
                b_corner(2)
            if u == units - 1:
                f_end()
            act, du, w_h, w_b = through(x, u)
            if u == 0:
                dn2[...] = nt(du, w_h)
                res[...] = nt(act, w_b)
            else:
                dn2[...] += nt(du, w_h)
                res[...] += nt(act, w_b)
            grads(x, u, act, du)
        for k in range(2):
            got = X4.at[near_t, pl.ds(k * half, half)]
            lanes.copy("cx", k, got, got, C_).wait_send()
        for u in range(units):
            b_end(u)
            if u == 0:
                sum_first(x, 0)
            cols = slice(u * HB, (u + 1) * HB)
            act, du, w_h, w_b = through(1 - x, u)
            dn2[...] += nt(du, w_h)
            if u < 1:
                grads(1 - x, u, act, du)
                sum_first(1 - x, u)
            for k in range(2):
                X4[k, :, cols] = act[k * rows : (k + 1) * rows]
                X4[2 + k, :, cols] = du[k * rows : (k + 1) * rows]

        def kept(k, u):
            return X4[2 * k : 2 * k + 2, :, u * HB : (u + 1) * HB].reshape(2 * rows, HB)

        lanes.copy("n2", 0, n2b.at[pl.ds(0, rows)], n2b.at[pl.ds(rows, rows)], C_).wait_send()
        n2b[0:rows, :] = dn2[rows:, :].astype(bf)
        lanes.start("dn", 0, lambda: (n2b.at[pl.ds(0, rows)], rdn), C_)
        for u in range(1):
            w_h, w_b = weights(1 - x, u)
            res[...] += nt(kept(0, u), w_b)
        lanes.arrived("dn", 0, rdn, C_)
        back = cot[...].astype(f32) + norm_pull(x1[...], gain, dn2[0:rows, :] + rdn[...].astype(f32))
        dn2[0:rows, :] = back
        back = back.astype(bf)
        out = nt(wof[...], back).astype(bf)
        for r in range(4):
            dsend[r] = out[r * width : (r + 1) * width]

            def to_owner(r=r):
                return lanes.copy("do", r, dsend.at[r], do_ref.at[t], (dp, r), land=t)

            @pl.when(t == r)
            def _():
                do_ref[t] = dsend[r]

            pl.when(t != r)(lambda: to_owner().start())
            lanes.late.append((lambda r=r, f=to_owner: f(r).wait_send(), lambda r=r: t != r))
        for u in range(units):
            if u >= 1:
                grads(1 - x, u, kept(0, u), kept(1, u))
                sum_first(1 - x, u)
        for step in range(1, NZ):
            zi = lax.rem(z + step, NZ)
            lanes.start_at("hz", step - 1, G5.at[:, zi, :, :, rest], RC.at[step - 1], far[step])
        for u in range(1, units):
            w_h, w_b = weights(1 - x, u)
            res[...] += nt(kept(0, u), w_b)
        n2b[rows:, :] = res[rows:, :].astype(bf)
        lanes.start("rs", 0, lambda: (n2b.at[pl.ds(rows, rows)], rres), C_)
        gw = nt(back.T, oin[...].reshape(4 * width, rows)).astype(bf)
        quarters = [pack(gw[:, k * width : (k + 1) * width].reshape(2 * NZ, part, width)) for k in range(4)]
        for xs in range(2):
            even, odd = quarters[2 * xs], quarters[2 * xs + 1]
            gws[xs] = jnp.where(c == 0, odd, even)
            gws[2 + xs] = jnp.where(c == 0, even, odd)
        lanes.start("gw", 0, lambda: (gws.at[pl.ds(0, 2)], gwr), C_)
        lanes.arrived("rs", 0, rres, C_)
        result[...] = (x1[...] + res[0:rows, :] + rres[...].astype(f32)).astype(bf)
        x1[...] = dn2[0:rows, :]

    pl.run_scoped(
        middle, pltpu.VMEM((dm, dm), bf), pltpu.VMEM((dm, 2 * rows), bf), pltpu.VMEM((dm, 2 * rows), bf),
        pltpu.VMEM((2 * rows, dm), f32), pltpu.VMEM((2 * rows, dm), f32),
    )

    def w_back_x():
        lanes.arrived("gw", 0, gwr, C_)
        gws[2 + 1 - x] = (gws[2 + 1 - x].astype(f32) + gwr[1 - x].astype(f32)).astype(bf)
        lanes.start("gx", 0, lambda: (gws.at[2 + 1 - x], gwx), X_)
        gws[2 + x] = (gws[2 + x].astype(f32) + gwr[x].astype(f32)).astype(bf)

    def w_back_y():
        lanes.arrived("gx", 0, gwx, X_)
        G1[heads] = (gws[2 + x].astype(f32) + gwx[...].astype(f32)).astype(bf)
        one_y(heads)

    def add(ref_at, *more):
        value = ref_at[...].astype(f32)
        for m in more:
            value = value + m.astype(f32)
        ref_at[...] = value.astype(bf)

    def second(u):
        lanes.arrived("ra", (1 - x) * units + u, RA.at[1 - x, :, :, unit(u)], Y_)
        add(G5.at[1 - x, :, y, :, unit(u)], RA[1 - x, :, :, unit(u)])
        lanes.start_at("ra2", u, G5.at[1 - x, :, y, :, unit(u)], RA2.at[:, :, unit(u)], X_)

    def rest_x():
        for step in range(1, NZ):
            lanes.arrived("hz", step - 1, RC.at[step - 1], far[NZ - step])
        add(G5.at[:, z, :, :, rest], RC[0], RC[1], RC[2])
        lanes.start_at("hx", 0, G5.at[1 - x, z, :, :, rest], RX, X_)

    def rest_y():
        lanes.arrived("hx", 0, RX, X_)
        add(G5.at[x, z, :, :, rest], RX[...])
        lanes.start_at("hy", 0, G5.at[x, z, 1 - y, :, rest], RYc, Y_)

    def third(u):
        lanes.arrived("ra", x * units + u, RA.at[x, :, :, unit(u)], Y_)
        lanes.arrived("ra2", u, RA2.at[:, :, unit(u)], X_)
        add(G5.at[x, :, y, :, unit(u)], RA[x, :, :, unit(u)], RA2[:, :, unit(u)])
        for step in range(1, NZ):
            zi = lax.rem(z + step, NZ)
            lanes.start_at("z2", u * 3 + step - 1, G5.at[x, zi, y, :, unit(u)], RZ2.at[step - 1, :, unit(u)], far[step])

    def last():
        value = G5[x, z, y, :, 0:routed].astype(f32)
        for step in range(1, NZ):
            for u in range(units):
                lanes.arrived("z2", u * 3 + step - 1, RZ2.at[step - 1, :, unit(u)], far[NZ - step])
            value = value + RZ2[step - 1].astype(f32)
        g2s[:, 0:routed] = value
        lanes.arrived("hy", 0, RYc, Y_)
        g2s[:, routed:] = G5[x, z, y, :, routed:].astype(f32) + RYc[...].astype(f32)

    def one_y(h):
        for zi in range(NZ):
            lanes.start_at("y1", h * 4 + zi, G1.at[h, zi * 2 + 1 - y], RY.at[h, zi], Y_)

    def one_z(h):
        for step in range(NZ):
            zi = lax.rem(z + step, NZ)
            lanes.arrived("y1", h * 4 + zi, RY.at[h, zi], Y_)
            G1[h, zi * 2 + y] = (G1[h, zi * 2 + y].astype(f32) + RY[h, zi].astype(f32)).astype(bf)
            if step:
                lanes.start_at("z1", h * 3 + step - 1, G1.at[h, zi * 2 + y], RZ.at[h, step - 1], far[step])

    def one_last(h):
        value = G1[h, dp].astype(f32)
        for step in range(1, NZ):
            lanes.arrived("z1", h * 3 + step - 1, RZ.at[h, step - 1], far[NZ - step])
            value = value + RZ[h, step - 1].astype(f32)
        value = unpack(value)
        g1s[:, h * 256 : h * 256 + 3 * E] = value
        return value

    def backward(kn, vn, dk, dv):
        def rows_first(r):
            xr, cr = r // 2, r % 2
            piece = qh[:, :, r * rows : (r + 1) * rows].reshape(heads * 3 * E, rows)
            X4[r] = tn(piece, W1T[0 : heads * 3 * E, :]).astype(bf)
            pl.when(c != cr)(lambda: lanes.start_at("d1", xr, X4.at[r], R1.at[xr], C_))

        def rows_second(r):
            xr, cr = r // 2, r % 2

            @pl.when(c == cr)
            def _():
                lanes.arrived("d1", xr, R1.at[xr], C_)
                X4[r] = (X4[r].astype(f32) + R1[xr].astype(f32)).astype(bf)
                pl.when(x != xr)(lambda: lanes.start_at("d2", 0, X4.at[r], R2, X_))

        events = {
            (0, 7): [lambda: second(0), lambda: sum_first(x, 1)],
            (0, 5): [lambda: second(1), lambda: sum_first(x, 2)],
            (0, 2): [lambda: second(2), rest_x],
            (1, 7): [lambda: third(0), w_back_x],
            (1, 4): [rest_y],
            (1, 2): [lambda: third(1)],
            (2, 7): [w_back_y],
            (2, 5): [lambda: third(2)],
            (2, 1): [lambda: one_z(heads)],
        }

        def head(h, carry):
            kn[...] = qh[h, E : 2 * E, :].T
            vn[...] = qh[h, 2 * E : 3 * E, :].T

            @pl.when(h == 0)
            def _():
                for there in (core_t, near_t, cross_t):
                    lanes.arrived("do", there, do_ref.at[there], (dp, there))

            for i in range(blocks)[::-1]:
                j0, js = spans(i)
                cols = slice(i * B, (i + 1) * B)
                half = slice((i % 2) * B, (i % 2 + 1) * B)
                hs = pl.ds(pl.multiple_of(h * E, E), E)
                qT, doT = qh[h, 0:E, cols], do_ref[i // 2, hs, half]
                low, L = low_ref[0:1, cols], L_ref[h, 0:1, cols]
                D = jnp.sum(doT.astype(f32) * o_ref[i // 2, hs, half].astype(f32), axis=0, keepdims=True)
                dq = jnp.zeros((E, B), f32)

                def front(j):
                    ks = slice(j * B, (j + 1) * B)
                    return nn(kn[ks, :], qT), nn(vn[ks, :], doT)

                queue = [front(j) for j in js[:2]]
                for n, j in enumerate(js):
                    ks = slice(j * B, (j + 1) * B)
                    if n + 2 < len(js):
                        queue.append(front(js[n + 2]))
                    s, dp_ = queue.pop(0)
                    p = jnp.exp2(s * (SCALE * LOG2E) - L)
                    if masked(i, j, blocks):
                        p = keep(i, j, low, p, 0.0)
                    ds = (p * (dp_ - D)).astype(bf)
                    dvj, dkj = nt(doT, p.astype(bf)), nt(qT, ds)
                    if i == min(blocks - 1, j + WINDOW // B):
                        dv[:, ks] = dvj
                        dk[:, ks] = dkj
                    else:
                        dv[:, ks] += dvj
                        dk[:, ks] += dkj
                    dq = dq + nn(qh[h, E : 2 * E, ks], ds)
                qh[h, 0:E, cols] = (dq * SCALE).astype(bf)
                qh[h, E : 2 * E, cols] = (dk[:, cols] * SCALE).astype(bf)
                qh[h, 2 * E : 3 * E, cols] = dv[:, cols].astype(bf)
                for k in range(heads):
                    for act in events.get((k, i), ()):
                        pl.when(h == k)(act)
                if i == 4:
                    pl.when(h > 0)(lambda: one_z(h - 1))
                if i % 2 == 0:

                    @pl.when(h == heads - 1)
                    def _():
                        rows_first(i // 2)
                        if i // 2 < 3:
                            rows_second(i // 2 + 1)

            G1[h] = pack(nn(qh[h], n1[...]).T.astype(bf).reshape(2 * NZ, part, 3 * E))
            one_y(h)
            return carry

        lax.fori_loop(0, heads, head, 0)
        rows_second(0)

    pl.run_scoped(
        backward, pltpu.VMEM((total, E), bf), pltpu.VMEM((total, E), bf), pltpu.VMEM((E, total), f32), pltpu.VMEM((E, total), f32)
    )
    one_z(heads - 1)
    last()
    w1v = W1[dp].astype(f32)
    sums = [one_last(h) for h in range(heads + 1)]
    gain1 = sum(
        jnp.sum(sums[h][:, 0 : 3 * E] * w1v[:, h * 3 * E : (h + 1) * 3 * E], axis=1, keepdims=True) for h in range(heads)
    ) / w1v[:, heads * 3 * E : heads * 3 * E + 1]
    gain2 = sum(
        jnp.sum(g2s[:, u * UNIT : u * UNIT + HB] * wh[:, u * HB : (u + 1) * HB].astype(f32), axis=1, keepdims=True)
        for u in range(units)
    ) / w1v[:, heads * 3 * E + 1 : heads * 3 * E + 2]
    both_ = jnp.concatenate([gain1, gain2, jnp.zeros((part, 126), f32)], axis=1)
    gs[...] = jnp.concatenate([both_, jnp.zeros((128 - part, 128), f32)], axis=0).T[0:8]
    for k, there in enumerate((X_, C_, XC_)):
        lanes.start("g", k, lambda k=k: (gs, gr.at[k]), there)
    gain = W1T[heads * 3 * E : heads * 3 * E + 16, :].astype(f32)[0:1]
    lanes.arrived("d2", 0, R2, X_)
    dn1 = X4[t].astype(f32) + R2[...].astype(f32)
    gin[...] = (x1[...] + norm_pull(xo[...].astype(f32), gain, dn1)).astype(bf)
    for k, there in enumerate((X_, C_, XC_)):
        lanes.arrived("g", k, gr.at[k], there)
    gains[...] = gs[...] + gr[0] + gr[1] + gr[2]
    for xs in range(2):
        for u in range(units):
            lanes.copy("ra", xs * units + u, G5.at[xs, :, 1 - y, :, unit(u)], RA.at[xs, :, :, unit(u)], Y_).wait_send()
    for step in range(1, NZ):
        zi = lax.rem(z + step, NZ)
        lanes.copy("hz", step - 1, G5.at[:, zi, :, :, rest], RC.at[step - 1], far[step]).wait_send()
    lanes.copy("hx", 0, G5.at[1 - x, z, :, :, rest], RX, X_).wait_send()
    lanes.copy("hy", 0, G5.at[x, z, 1 - y, :, rest], RYc, Y_).wait_send()
    for u in range(units):
        lanes.copy("ra2", u, G5.at[1 - x, :, y, :, unit(u)], RA2.at[:, :, unit(u)], X_).wait_send()
        for step in range(1, NZ):
            zi = lax.rem(z + step, NZ)
            lanes.copy("z2", u * 3 + step - 1, G5.at[x, zi, y, :, unit(u)], RZ2.at[step - 1, :, unit(u)], far[step]).wait_send()
    for h in range(heads + 1):
        for zi in range(NZ):
            lanes.copy("y1", h * 4 + zi, G1.at[h, zi * 2 + 1 - y], RY.at[h, zi], Y_).wait_send()
        for step in range(1, NZ):
            zi = lax.rem(z + step, NZ)
            lanes.copy("z1", h * 3 + step - 1, G1.at[h, zi * 2 + y], RZ.at[h, step - 1], far[step]).wait_send()
    for r in range(4):
        xr, cr = r // 2, r % 2
        pl.when(c != cr)(lambda: lanes.copy("d1", xr, X4.at[r], R1.at[xr], C_).wait_send())
        pl.when(jnp.logical_and(c == cr, x != xr))(lambda: lanes.copy("d2", 0, X4.at[r], R2, X_).wait_send())
    lanes.finish()


VM = pl.BlockSpec(memory_space=pltpu.VMEM)


def unpack_kernel(gin, result, g1s, g2s, gains, o_result, o_gin, gq, gk, gv, go, gh, gb, gg1, gg2):
    o_result[...] = result[...]
    o_gin[...] = gin[...]
    heads = gq.shape[1] // E
    for h in range(heads):
        base = h * 256
        for k, out in enumerate((gq, gk, gv)):
            out[:, h * E : (h + 1) * E] = g1s[:, base + k * E : base + (k + 1) * E]
    go[...] = g1s[:, heads * 256 : (heads + 1) * 256].T[0 : go.shape[0]]
    units = gh.shape[1] // HB
    for u in range(units):
        gh[:, u * HB : (u + 1) * HB] = g2s[:, u * UNIT : u * UNIT + HB]
        gb[:, u * HB : (u + 1) * HB] = g2s[:, u * UNIT + HB : (u + 1) * UNIT]
    n = gg1.shape[1]
    t = lax.axis_index("tensor")
    for k, out in enumerate((gg1, gg2)):
        value = gains[k : k + 1, 0:n]
        for at in range(1, 4):
            value = jnp.where(t == at, gains[k : k + 1, at * n : (at + 1) * n], value)
        out[...] = value


def block(inputs, segments, w_query, w_key, w_value, w_output, w_hidden, w_back, gain_one, gain_two, cotangent):
    rows, dm = inputs.shape
    total = segments.shape[0]
    part, width = w_query.shape
    heads = width // E
    ff = w_hidden.shape[1]
    units = ff // HB
    s, v = jax.ShapeDtypeStruct, pltpu.VMEM
    first = (units - 1) * UNIT + HB
    gin, result, g1s, g2s, gains = pl.pallas_call(
        kernel,
        out_shape=(
            s((rows, dm), bf), s((rows, dm), bf), s((part, (heads + 1) * 256), f32), s((part, 2 * ff), f32), s((8, 128), f32),
        ),
        in_specs=[VM] * 11,
        out_specs=(VM,) * 5,
        scratch_shapes=[
            v((4, rows, dm), bf), v((total, dm), bf), v((2 * NZ, part, 640), bf), v((640, dm), bf),
            v((2, NZ, 2, part, 2 * ff), bf), v((2, NZ, 2, part, 2 * ff), bf), v((4, NZ, 2, 144, 128), bf),
            v((heads, 3 * E, total), bf), v((4, width, rows), bf), v((4, width, rows), bf),
            v((heads, 8, total), f32), v((8, total), jnp.int32), v((2 * rows, dm), bf), v((2 * rows, dm), bf), v((rows, dm), f32),
            v((rows, dm), bf), v((rows, dm), bf), v((4, width, rows), bf), v((4, width, rows), bf),
            v((4, 2 * NZ, 144, 128), bf), v((2, 2 * NZ, 144, 128), bf), v((2 * NZ, 144, 128), bf), v((2, rows, dm), bf), v((rows, dm), bf),
            v((heads + 1, 2 * NZ, 144, 128), bf), v((heads + 1, NZ, 144, 128), bf), v((heads + 1, 3, 144, 128), bf),
            v((2, NZ, part, first), bf), v((NZ, part, first), bf), v((3, part, first), bf),
            v((3, 2, 2, part, HB), bf), v((2, part, HB), bf), v((part, HB), bf), v((8, 128), f32), v((3, 8, 128), f32),
            pltpu.SemaphoreType.DMA((144,)), pltpu.SemaphoreType.DMA((144,)),
        ],
        compiler_params=pltpu.CompilerParams(collective_id=1, has_side_effects=True, vmem_limit_bytes=63 * 2**20),
    )(
        inputs, cotangent, segments.reshape(1, total), w_query, w_key, w_value, w_output, w_hidden, w_back.T,
        gain_one.reshape(1, part), gain_two.reshape(1, part),
    )
    outs = pl.pallas_call(
        unpack_kernel,
        out_shape=(
            s((rows, dm), bf), s((rows, dm), bf), s((part, width), f32), s((part, width), f32), s((part, width), f32),
            s((width, part), f32), s((part, ff), f32), s((part, ff), f32), s((1, part // 4), f32), s((1, part // 4), f32),
        ),
        in_specs=[VM] * 5,
        out_specs=(VM,) * 10,
    )(gin, result, g1s, g2s, gains)
    return (*outs[:7], outs[7].T, *(g.reshape(part // 4) for g in outs[8:]))


def normed(value, gain):
    return value * lax.rsqrt(jnp.mean(value * value, axis=-1, keepdims=True) + 1e-05) * gain


def gelu_local(value):
    return jax.nn.gelu(value, approximate=True)


def scores_for(query_block, key_rows, segment_ids, block_start, block_rows):
    positions = jnp.arange(key_rows.shape[0], dtype=jnp.int32)
    query_pos = block_start + jnp.arange(block_rows, dtype=jnp.int32)
    query_seg = lax.dynamic_slice_in_dim(segment_ids, block_start, block_rows)
    scores = jnp.einsum(
        "qhe,khe->hqk", query_block, key_rows, preferred_element_type=jnp.float32
    ) * E ** (-0.5)
    distance = query_pos[:, None] - positions[None, :]
    allowed = (query_seg[:, None] == segment_ids[None, :]) & (distance >= 0) & (distance < WINDOW)
    return jnp.where(allowed[None], scores, -1e30)


def shards(
    inputs,
    segments,
    w_query,
    w_key,
    w_value,
    w_output,
    w_hidden,
    w_back,
    gain_one,
    gain_two,
    cotangent,
):
    owned = (w_query, w_key, w_value, w_output, w_hidden, w_back, gain_one, gain_two)
    gathered = (
        lax.all_gather(owned[0], "dp", axis=0, tiled=True),
        lax.all_gather(owned[1], "dp", axis=0, tiled=True),
        lax.all_gather(owned[2], "dp", axis=0, tiled=True),
        lax.all_gather(owned[3], "dp", axis=1, tiled=True),
        lax.all_gather(owned[4], "dp", axis=0, tiled=True),
        lax.all_gather(owned[5], "dp", axis=1, tiled=True),
        lax.all_gather(owned[6], "dp", axis=0, tiled=True),
        lax.all_gather(owned[7], "dp", axis=0, tiled=True),
    )
    total_rows = segments.shape[0]
    block_rows = min(512, total_rows)
    blocks = total_rows // block_rows
    width = gathered[0].shape[1]
    heads_here = width // E
    scale = E ** (-0.5)
    starts = jnp.arange(blocks, dtype=jnp.int32) * block_rows
    w_joined = jnp.concatenate([gathered[0], gathered[1], gathered[2]], axis=1)
    gain_first = gathered[6].astype(jnp.float32)
    gain_second = gathered[7].astype(jnp.float32)
    inputs_f = inputs.astype(jnp.float32)
    normed_one = normed(inputs_f, gain_first).astype(jnp.bfloat16)
    full_one = lax.all_gather(normed_one, "tensor", axis=0, tiled=True)
    joined = jnp.dot(full_one, w_joined, preferred_element_type=jnp.float32).astype(jnp.bfloat16)
    query_rows = joined[:, :width].reshape(total_rows, heads_here, E)
    key_rows = joined[:, width : 2 * width].reshape(total_rows, heads_here, E)
    value_rows = joined[:, 2 * width :].reshape(total_rows, heads_here, E)
    query_blocks = query_rows.reshape(blocks, block_rows, heads_here, E)

    def forward_block(packed):
        query_block, block_start = packed
        scores = scores_for(query_block, key_rows, segments, block_start, block_rows)
        row_top = jnp.max(scores, axis=-1, keepdims=True)
        weights_exp = jnp.exp(scores - row_top)
        totals = jnp.sum(weights_exp, axis=-1, keepdims=True)
        probability = (weights_exp / totals).astype(jnp.bfloat16)
        attended_block = jnp.einsum(
            "hqk,khe->qhe", probability, value_rows, preferred_element_type=jnp.float32
        )
        return (attended_block.astype(jnp.bfloat16), (row_top + jnp.log(totals))[..., 0])

    attended, log_sums = lax.map(forward_block, (query_blocks, starts))
    attended = attended.reshape(total_rows, width)
    w_out_full = gathered[3]
    own_attended = lax.all_to_all(attended, "tensor", split_axis=0, concat_axis=1, tiled=True)
    w_out_all = lax.all_gather(w_out_full, "tensor", axis=0, tiled=True)
    attn_branch = jnp.dot(own_attended, w_out_all, preferred_element_type=jnp.float32)
    middle = inputs_f + attn_branch
    normed_two = normed(middle, gain_second).astype(jnp.bfloat16)
    full_two = lax.all_gather(normed_two, "tensor", axis=0, tiled=True)
    hidden = jnp.dot(full_two, gathered[4], preferred_element_type=jnp.float32)
    active = gelu_local(hidden).astype(jnp.bfloat16)
    w_back_full = gathered[5]
    result = middle + lax.psum_scatter(
        jnp.dot(active, w_back_full, preferred_element_type=jnp.float32).astype(jnp.bfloat16),
        "tensor",
        scatter_dimension=0,
        tiled=True,
    ).astype(jnp.float32)
    gathered = (
        lax.all_gather(owned[0], "dp", axis=0, tiled=True),
        lax.all_gather(owned[1], "dp", axis=0, tiled=True),
        lax.all_gather(owned[2], "dp", axis=0, tiled=True),
        lax.all_gather(owned[3], "dp", axis=1, tiled=True),
        lax.all_gather(owned[4], "dp", axis=0, tiled=True),
        lax.all_gather(owned[5], "dp", axis=1, tiled=True),
        lax.all_gather(owned[6], "dp", axis=0, tiled=True),
        lax.all_gather(owned[7], "dp", axis=0, tiled=True),
    )
    w_joined = jnp.concatenate([gathered[0], gathered[1], gathered[2]], axis=1)
    grad_out = cotangent.astype(jnp.float32)
    full_grad = lax.all_gather(cotangent, "tensor", axis=0, tiled=True)
    grad_w_back = jnp.einsum("rf,rd->fd", active, full_grad, preferred_element_type=jnp.float32)
    grad_active = jnp.einsum(
        "rd,fd->rf", full_grad, gathered[5], preferred_element_type=jnp.float32
    )
    gelu_pull = jax.vjp(gelu_local, hidden)[1]
    grad_hidden_rows = gelu_pull(grad_active)[0].astype(jnp.bfloat16)
    grad_w_hidden = jnp.einsum(
        "rd,rf->df", full_two, grad_hidden_rows, preferred_element_type=jnp.float32
    )
    w_hidden_full = gathered[4]
    piece = grad_hidden_rows
    grad_normed_two = lax.psum_scatter(
        jnp.einsum("rf,df->rd", piece, w_hidden_full, preferred_element_type=jnp.float32).astype(
            jnp.bfloat16
        ),
        "tensor",
        scatter_dimension=0,
        tiled=True,
    ).astype(jnp.float32)
    second_pull = jax.vjp(normed, middle, gain_second)[1]
    grad_mid_norm, grad_second = second_pull(grad_normed_two)
    grad_middle = grad_out + grad_mid_norm
    full_middle = lax.all_gather(grad_middle.astype(jnp.bfloat16), "tensor", axis=0, tiled=True)
    grad_w_output = jnp.einsum(
        "rh,rd->hd", attended, full_middle, preferred_element_type=jnp.float32
    )
    grad_attended = jnp.einsum(
        "rd,hd->rh", full_middle, gathered[3], preferred_element_type=jnp.float32
    ).astype(jnp.bfloat16)

    def backward_block(carry, packed):
        grad_keys, grad_values = carry
        query_block, grad_block, log_block, block_start = packed
        scores = scores_for(query_block, key_rows, segments, block_start, block_rows)
        probability = jnp.exp(scores - log_block[..., None])
        grad_values = grad_values + jnp.einsum(
            "hqk,qhe->khe",
            probability.astype(jnp.bfloat16),
            grad_block,
            preferred_element_type=jnp.float32,
        )
        grad_probs = jnp.einsum(
            "qhe,khe->hqk", grad_block, value_rows, preferred_element_type=jnp.float32
        )
        delta_rows = jnp.sum(grad_probs * probability, axis=-1, keepdims=True)
        grad_scores = (probability * (grad_probs - delta_rows)).astype(jnp.bfloat16)
        grad_query_block = (
            jnp.einsum("hqk,khe->qhe", grad_scores, key_rows, preferred_element_type=jnp.float32)
            * scale
        )
        grad_keys = (
            grad_keys
            + jnp.einsum(
                "hqk,qhe->khe", grad_scores, query_block, preferred_element_type=jnp.float32
            )
            * scale
        )
        return ((grad_keys, grad_values), grad_query_block)

    zero_state = jnp.zeros((total_rows, heads_here, E), jnp.float32)
    grad_blocks = grad_attended.reshape(blocks, block_rows, heads_here, E)
    (grad_keys, grad_values), grad_queries = lax.scan(
        backward_block, (zero_state, zero_state), (query_blocks, grad_blocks, log_sums, starts)
    )
    grad_joined = jnp.concatenate(
        [
            grad_queries.reshape(total_rows, width),
            grad_keys.reshape(total_rows, width),
            grad_values.reshape(total_rows, width),
        ],
        axis=1,
    ).astype(jnp.bfloat16)
    grad_w_joined = jnp.einsum(
        "rd,rc->dc", full_one, grad_joined, preferred_element_type=jnp.float32
    )
    piece = grad_joined
    grad_normed_one = lax.psum_scatter(
        jnp.einsum("rc,dc->rd", piece, w_joined, preferred_element_type=jnp.float32).astype(
            jnp.bfloat16
        ),
        "tensor",
        scatter_dimension=0,
        tiled=True,
    ).astype(jnp.float32)
    first_pull = jax.vjp(normed, inputs_f, gain_first)[1]
    grad_in_norm, grad_first = first_pull(grad_normed_one)
    grad_inputs = grad_middle + grad_in_norm
    weight_sums = (
        lax.psum_scatter(grad_w_joined[:, :width], "dp", scatter_dimension=0, tiled=True),
        lax.psum_scatter(
            grad_w_joined[:, width : 2 * width], "dp", scatter_dimension=0, tiled=True
        ),
        lax.psum_scatter(grad_w_joined[:, 2 * width :], "dp", scatter_dimension=0, tiled=True),
        lax.psum_scatter(grad_w_output, "dp", scatter_dimension=1, tiled=True),
        lax.psum_scatter(grad_w_hidden, "dp", scatter_dimension=0, tiled=True),
        lax.psum_scatter(grad_w_back, "dp", scatter_dimension=1, tiled=True),
    )
    gain_sums = (
        lax.psum_scatter(grad_first, ("dp", "tensor"), scatter_dimension=0, tiled=True),
        lax.psum_scatter(grad_second, ("dp", "tensor"), scatter_dimension=0, tiled=True),
    )
    return (
        result.astype(jnp.bfloat16),
        grad_inputs.astype(jnp.bfloat16),
        weight_sums[0],
        weight_sums[1],
        weight_sums[2],
        weight_sums[3],
        weight_sums[4],
        weight_sums[5],
        gain_sums[0],
        gain_sums[1],
    )


def solution(mesh):
    rows, cols = P(("dp", "tensor"), None), P("dp", "tensor")
    turned, part = P("tensor", "dp"), P("dp")
    in_specs = (rows, part, cols, cols, cols, turned, cols, turned, part, part, rows)
    out_specs = (rows, rows, cols, cols, cols, turned, cols, turned, P(("dp", "tensor")), P(("dp", "tensor")))
    here = mesh.shape["dp"] == 2 * NZ and mesh.shape["tensor"] == 4
    body = block if here else shards
    return jax.shard_map(body, mesh=mesh, in_specs=in_specs, out_specs=out_specs, check_vma=False)
```
